32 devices in a mesh: dp: 4 (over y, x), vocab: 8 (over z, core).
Axes of the slice: x: 2, y: 2, z: 4, core: 2. Of those that a mesh axis runs over, the one named last changes fastest.
Arguments:
- token_ids: int32 [32, 128], P(('dp', 'vocab')), may hold values from 0 to 50256, as said below
- pick_rows: int32 [32, 64], P(('dp', 'vocab')), may hold values from 0 to 127, as said below
- target_ids: int32 [32, 64], P(('dp', 'vocab')), may hold values from 0 to 50256
- attn_in: float32 [768, 2304], P(('dp', 'vocab')), may hold values from -0.21875 to 0.21875
- attn_out: float32 [768, 768], P(('dp', 'vocab')), may hold values from -0.875 to 0.875
- mlp_in: float32 [768, 3072], P(('dp', 'vocab')), may hold values from -0.21875 to 0.21875
- mlp_out: float32 [3072, 768], P(('dp', 'vocab')), may hold values from -0.109375 to 0.109375
- positions: float32 [128, 768], P(('dp', 'vocab')), may hold values from -0.4375 to 0.4375
- vectors: float32 [14, 768], P(None, ('dp', 'vocab'))
- table: float32 [50304, 768], P('vocab'), may hold values from -0.4375 to 0.4375
- first_attn_in: float32 [768, 2304], P(('dp', 'vocab')), may hold values from -9.536743e-07 to 9.536743e-07
- first_attn_out: float32 [768, 768], P(('dp', 'vocab')), may hold values from -9.536743e-07 to 9.536743e-07
- first_mlp_in: float32 [768, 3072], P(('dp', 'vocab')), may hold values from -9.536743e-07 to 9.536743e-07
- first_mlp_out: float32 [3072, 768], P(('dp', 'vocab')), may hold values from -9.536743e-07 to 9.536743e-07
- first_positions: float32 [128, 768], P(('dp', 'vocab')), may hold values from -9.536743e-07 to 9.536743e-07
- first_vectors: float32 [14, 768], P(None, ('dp', 'vocab')), may hold values from -9.536743e-07 to 9.536743e-07
- first_table: float32 [50304, 768], P('vocab'), may hold values from -9.536743e-07 to 9.536743e-07
- second_attn_in: float32 [768, 2304], P(('dp', 'vocab')), may hold values from 2.1824333e-15 to 8.729733e-15
- second_attn_out: float32 [768, 768], P(('dp', 'vocab')), may hold values from 2.1824333e-15 to 8.729733e-15
- second_mlp_in: float32 [768, 3072], P(('dp', 'vocab')), may hold values from 2.1824333e-15 to 8.729733e-15
- second_mlp_out: float32 [3072, 768], P(('dp', 'vocab')), may hold values from 2.1824333e-15 to 8.729733e-15
- second_positions: float32 [128, 768], P(('dp', 'vocab')), may hold values from 2.1824333e-15 to 8.729733e-15
- second_vectors: float32 [14, 768], P(None, ('dp', 'vocab')), may hold values from 2.1824333e-15 to 8.729733e-15
- second_table: float32 [50304, 768], P('vocab'), may hold values from 2.1824333e-15 to 8.729733e-15
Outputs:
- loss: float32 [], replicated
- grad_norm: float32 [], replicated
- ratios: float32 [7], replicated
- new_attn_in: float32 [768, 2304], P(('dp', 'vocab'))
- new_attn_out: float32 [768, 768], P(('dp', 'vocab'))
- new_mlp_in: float32 [768, 3072], P(('dp', 'vocab'))
- new_mlp_out: float32 [3072, 768], P(('dp', 'vocab'))
- new_positions: float32 [128, 768], P(('dp', 'vocab'))
- new_vectors: float32 [14, 768], P(None, ('dp', 'vocab'))
- new_table: float32 [50304, 768], P('vocab')
- new_first_attn_in: float32 [768, 2304], P(('dp', 'vocab'))
- new_first_attn_out: float32 [768, 768], P(('dp', 'vocab'))
- new_first_mlp_in: float32 [768, 3072], P(('dp', 'vocab'))
- new_first_mlp_out: float32 [3072, 768], P(('dp', 'vocab'))
- new_first_positions: float32 [128, 768], P(('dp', 'vocab'))
- new_first_vectors: float32 [14, 768], P(None, ('dp', 'vocab'))
- new_first_table: float32 [50304, 768], P('vocab')
- new_second_attn_in: float32 [768, 2304], P(('dp', 'vocab'))
- new_second_attn_out: float32 [768, 768], P(('dp', 'vocab'))
- new_second_mlp_in: float32 [768, 3072], P(('dp', 'vocab'))
- new_second_mlp_out: float32 [3072, 768], P(('dp', 'vocab'))
- new_second_positions: float32 [128, 768], P(('dp', 'vocab'))
- new_second_vectors: float32 [14, 768], P(None, ('dp', 'vocab'))
- new_second_table: float32 [50304, 768], P('vocab')
The draws below stay inside these ranges and needn't reach their ends.
Inputs may be any that keep to these rules, and one draw needn't show every extreme that they name: `pick_rows`: each sequence's 64 positions are distinct and increasing. `token_ids`: the table's rows split into 8 aligned blocks of 6288 ids; of one sequence's tokens at most 64 have ids in one block, and every sequence has exactly 64 in some block.
All inputs are finite; a program needn't handle non-finite values.
Results may differ from the reference program's by a relative error of at most 0.008.
The reference program's roundings to bfloat16 on the way count: a program that leaves them out, or rounds other values in their place, can miss the bound.
Values may be sent and summed in bfloat16 or wider, within the bound.
No kernel may reach another device: no remote copies, remote signals or barrier semaphores. Data moves between devices by JAX's collectives and lax.ppermute only.
A program may use at most 448 MiB of HBM per device.

```python
import math
import jax
import jax.numpy as jnp
import numpy as np
from jax import lax

D = 768
HEADS = 12
HD = 64
FF = 3072
V_REAL = 50257
V = 50304
LEN = 128
PICK = 64
STEP = 5
SEQS = 32
CAP = 64
COUNT = 2048
NPARAM = 45820416
N_VOCAB = 8


def draw_pick_rows(key, part):
    keys_all = jax.random.split(key, SEQS)

    def one_row(row_key):
        order = jax.random.permutation(row_key, LEN)
        return jnp.sort(order[:PICK])
    return jax.vmap(one_row)(keys_all).astype(jnp.int32)


def draw_token_ids(key, part):
    keys_all = jax.random.split(jax.random.fold_in(key, 7), SEQS)
    shard = V // N_VOCAB

    def one_row(row_key):
        key_heavy, key_slots, key_order, key_bound, key_local = jax.random.split(row_key, 5)
        heavy = jax.random.randint(key_heavy, (), 0, N_VOCAB)
        others = jnp.arange((N_VOCAB - 1) * CAP, dtype=jnp.int32) // CAP
        others = others + (others >= heavy).astype(jnp.int32)
        chosen = jax.random.permutation(key_slots, others)[:LEN - CAP]
        owners = jnp.concatenate([jnp.full((CAP,), heavy, jnp.int32), chosen])
        owners = jax.random.permutation(key_order, owners)
        upper = jnp.minimum(shard, V_REAL - owners * shard)
        bound = jax.random.randint(key_bound, (LEN,), 1, upper + 1)
        local = jax.random.randint(key_local, (LEN,), 0, bound)
        return owners * shard + local
    return jax.vmap(one_row)(keys_all).astype(jnp.int32)


def draw_vectors(key, part):
    gains = 1.0 + 0.2 * jax.random.uniform(jax.random.fold_in(key, 1), (14, D), jnp.float32, -1.0, 1.0)
    shifts = 0.1 * jax.random.normal(jax.random.fold_in(key, 2), (14, D), jnp.float32)
    row_index = jnp.arange(14)[:, None]
    is_gain = (row_index == 0) | (row_index == 2) | (row_index == 4)
    return jnp.where(is_gain, gains, shifts).astype(jnp.float32)


def with_ends(result, stream_key, smallest, high):
    longest = result.shape.index(max(result.shape))
    spots = []
    for shift in (0, 1):
        where = [jax.random.randint(jax.random.fold_in(stream_key, axis), (), 0, length) for axis, length in enumerate(result.shape)]
        where[longest] = (where[longest] + shift) % result.shape[longest]
        spots.append(tuple(where))
    return result.at[spots[0]].set(smallest).at[spots[1]].set(high)


def shard_levels(stream_key, extent, shards, smallest, top_value):
    level = 1.0
    for position, parts in shards:
        steps = jax.random.uniform(jax.random.fold_in(jax.random.fold_in(stream_key, 6), position), (parts,), jnp.float32, smallest / len(shards), top_value / len(shards))
        level = level * jnp.repeat(jnp.exp(steps), extent[position] // parts).reshape((-1,) + (1,) * (len(extent) - 1 - position))
    return level


def rank_bounds(number_of, lean):
    portions = [(1 << 20) // math.isqrt(grade ** lean) + 1 for grade in range(1, number_of + 1)]
    scale = 1 + sum(portions) // (1 << 30)
    return np.cumsum(np.array([max(1, weight // scale) for weight in portions]))


def ranked(own_key, shape, number_of, skew):
    listing = rank_bounds(number_of, skew)
    lot = jax.random.randint(jax.random.fold_in(own_key, 1), shape, 0, int(listing[number_of - 1]))
    grade = jnp.searchsorted(jnp.asarray(listing, jnp.int32), lot, side="right")
    return jax.random.permutation(jax.random.fold_in(own_key, 2), number_of)[grade].astype(jnp.int32)


def normal_values(key, shape, scale, most, cuts=(), kind=jnp.bfloat16):
    result = scale * jax.random.normal(key, shape, jnp.float32)
    if cuts:
        result = result * shard_levels(key, shape, cuts, -0.22, 0.18)
    return jnp.clip(result, -most, most).astype(kind)


def setup_inputs(seed: int = 0) -> dict:
    splits = jax.random.split(jax.random.key(seed), 25)
    return {
        "token_ids": draw_token_ids(jax.random.fold_in(splits[24], 71), 0),
        "pick_rows": draw_pick_rows(jax.random.fold_in(splits[24], 71), 0),
        "target_ids": with_ends(ranked(splits[2], (SEQS, PICK), V_REAL, 2), jax.random.fold_in(splits[2], 3), 0, V_REAL - 1).astype(jnp.int32),
        "attn_in": normal_values(splits[3], (D, 3 * D), D ** -0.5, 0.21875, ((0, 32),), jnp.float32),
        "attn_out": normal_values(splits[4], (D, D), (D // 16) ** -0.5, 0.875, ((0, 32),), jnp.float32),
        "mlp_in": normal_values(splits[5], (D, FF), D ** -0.5, 0.21875, ((0, 32),), jnp.float32),
        "mlp_out": normal_values(splits[6], (FF, D), FF ** -0.5, 0.109375, ((0, 32),), jnp.float32),
        "positions": normal_values(splits[7], (LEN, D), 0.07, 0.4375, ((0, 32),), jnp.float32),
        "vectors": draw_vectors(jax.random.fold_in(splits[24], 71), 0),
        "table": normal_values(splits[9], (V, D), 0.07, 0.4375, ((0, 8),), jnp.float32),
        "first_attn_in": normal_values(splits[10], (D, 3 * D), (0.111 * 10 ** -2 * NPARAM ** -0.5), 9.5367431640625e-07, ((0, 32),), jnp.float32),
        "first_attn_out": normal_values(splits[11], (D, D), (0.111 * 10 ** -2 * NPARAM ** -0.5), 9.5367431640625e-07, ((0, 32),), jnp.float32),
        "first_mlp_in": normal_values(splits[12], (D, FF), (0.111 * 10 ** -2 * NPARAM ** -0.5), 9.5367431640625e-07, ((0, 32),), jnp.float32),
        "first_mlp_out": normal_values(splits[13], (FF, D), (0.111 * 10 ** -2 * NPARAM ** -0.5), 9.5367431640625e-07, ((0, 32),), jnp.float32),
        "first_positions": normal_values(splits[14], (LEN, D), (0.111 * 10 ** -2 * NPARAM ** -0.5), 9.5367431640625e-07, ((0, 32),), jnp.float32),
        "first_vectors": normal_values(splits[15], (14, D), (0.111 * 10 ** -2 * NPARAM ** -0.5), 9.5367431640625e-07, ((1, 32),), jnp.float32),
        "first_table": normal_values(splits[16], (V, D), (0.111 * 10 ** -2 * NPARAM ** -0.5), 9.5367431640625e-07, ((0, 8),), jnp.float32),
        "second_attn_in": jnp.clip(jnp.exp(math.log(8.729733312639633e-15) - 1.3862944 * jax.random.uniform(splits[17], (D, 3 * D), jnp.float32) ** shard_levels(splits[17], (D, 3 * D), ((0, 32),), -0.2, 0.2)), 2.1824333281599082e-15, 8.729733312639633e-15),
        "second_attn_out": jnp.clip(jnp.exp(math.log(8.729733312639633e-15) - 1.3862944 * jax.random.uniform(splits[18], (D, D), jnp.float32) ** shard_levels(splits[18], (D, D), ((0, 32),), -0.2, 0.2)), 2.1824333281599082e-15, 8.729733312639633e-15),
        "second_mlp_in": jnp.clip(jnp.exp(math.log(8.729733312639633e-15) - 1.3862944 * jax.random.uniform(splits[19], (D, FF), jnp.float32) ** shard_levels(splits[19], (D, FF), ((0, 32),), -0.2, 0.2)), 2.1824333281599082e-15, 8.729733312639633e-15),
        "second_mlp_out": jnp.clip(jnp.exp(math.log(8.729733312639633e-15) - 1.3862944 * jax.random.uniform(splits[20], (FF, D), jnp.float32) ** shard_levels(splits[20], (FF, D), ((0, 32),), -0.2, 0.2)), 2.1824333281599082e-15, 8.729733312639633e-15),
        "second_positions": jnp.clip(jnp.exp(math.log(8.729733312639633e-15) - 1.3862944 * jax.random.uniform(splits[21], (LEN, D), jnp.float32) ** shard_levels(splits[21], (LEN, D), ((0, 32),), -0.2, 0.2)), 2.1824333281599082e-15, 8.729733312639633e-15),
        "second_vectors": jnp.clip(jnp.exp(math.log(8.729733312639633e-15) - 1.3862944 * jax.random.uniform(splits[22], (14, D), jnp.float32) ** shard_levels(splits[22], (14, D), ((1, 32),), -0.2, 0.2)), 2.1824333281599082e-15, 8.729733312639633e-15),
        "second_table": jnp.clip(jnp.exp(math.log(8.729733312639633e-15) - 1.3862944 * jax.random.uniform(splits[23], (V, D), jnp.float32) ** shard_levels(splits[23], (V, D), ((0, 8),), -0.2, 0.2)), 2.1824333281599082e-15, 8.729733312639633e-15),
    }


@jax.custom_vjp
def low(v):
    return lax.optimization_barrier(v.astype(jnp.bfloat16)).astype(jnp.float32)

@jax.custom_vjp
def low_back(v):
    return v

def low_keep(v):
    return (low(v), None)

def low_pass(kept, grad):
    return (grad,)

def back_keep(v):
    return (v, None)

def back_low(kept, grad):
    return (low(grad),)
low.defvjp(low_keep, low_pass)
low_back.defvjp(back_keep, back_low)
LN_EPS = 1e-05
SMOOTHING = 0.1
BETA_ONE = 0.9
BETA_TWO = 0.999
ADAM_EPS = 1e-12
DECAY = 0.01
RATE = 0.3
CLIP_AT = 0.01
MASKED = -1e+30
HIGHEST = lax.Precision.HIGHEST

def layer_norm(inputs, gain, shift):
    centre = lax.optimization_barrier(jnp.mean(inputs, axis=-1, keepdims=True))
    centred = inputs - centre
    spread = lax.optimization_barrier(jnp.mean(centred * centred, axis=-1, keepdims=True))
    return centred * lax.rsqrt(spread + LN_EPS) * gain + shift

def gelu_tanh(inputs):
    return 0.5 * inputs * (1.0 + jnp.tanh(0.7978845608028654 * (inputs + 0.044715 * inputs * inputs * inputs)))

def matmul(left_op, right_op):
    return jnp.dot(left_op, right_op, precision=HIGHEST)

def sequence_loss(lowered, seq_ids, seq_picks, seq_targets):
    attn_in, attn_out, mlp_in, mlp_out, positions, vectors, table = lowered
    looked = low_back(jnp.take(table, seq_ids, axis=0))
    resid_in = looked + positions
    normed_one = low(layer_norm(resid_in, vectors[0], vectors[1]))
    qkv_bias = jnp.concatenate([vectors[6], jnp.zeros((D,), jnp.float32), vectors[7]])
    packed = low(low_back(matmul(normed_one, attn_in) + qkv_bias))
    queries = packed[:, :D].reshape(LEN, HEADS, HD)
    keys_all = packed[:, D:2 * D].reshape(LEN, HEADS, HD)
    values_all = packed[:, 2 * D:].reshape(LEN, HEADS, HD)
    scores = jnp.einsum('qhd,khd->hqk', queries, keys_all, precision=HIGHEST) * HD ** (-0.5)
    causal = jnp.arange(LEN)[None, :] <= jnp.arange(LEN)[:, None]
    scores = low_back(jnp.where(causal[None], scores, MASKED))
    row_top = lax.optimization_barrier(jnp.max(scores, axis=-1, keepdims=True))
    exp_scores = jnp.exp(scores - row_top)
    attn_probs = low(exp_scores / lax.optimization_barrier(jnp.sum(exp_scores, axis=-1, keepdims=True)))
    attended = jnp.einsum('hqk,khd->qhd', attn_probs, values_all, precision=HIGHEST).reshape(LEN, D)
    attended = low(low_back(attended))
    resid_mid = resid_in + low_back(matmul(attended, attn_out) + vectors[8])
    normed_two = low(layer_norm(resid_mid, vectors[2], vectors[3]))
    hidden_pre = low_back(matmul(normed_two, mlp_in) + vectors[10:14].reshape(FF))
    hidden_act = low(gelu_tanh(hidden_pre))
    resid_out = resid_mid + low_back(matmul(hidden_act, mlp_out) + vectors[9])
    final = low(layer_norm(resid_out, vectors[4], vectors[5]))
    logits = low_back(jnp.dot(final[seq_picks], table.T, precision=HIGHEST))
    is_real = jnp.arange(V) < V_REAL
    logits = jnp.where(is_real[None, :], logits, MASKED)
    logit_top = lax.optimization_barrier(jnp.max(logits, axis=1, keepdims=True))
    log_norm = logit_top[:, 0] + jnp.log(lax.optimization_barrier(jnp.sum(jnp.exp(logits - logit_top), axis=1)))
    target_logit = jnp.take_along_axis(logits, seq_targets[:, None], axis=1)[:, 0]
    logit_total = lax.optimization_barrier(jnp.sum(jnp.where(is_real[None, :], logits, 0.0), axis=1))
    row_loss = (1.0 - SMOOTHING) * (log_norm - target_logit) + SMOOTHING * (log_norm - logit_total / V_REAL)
    return jnp.sum(row_loss)

def total_loss(masters, token_ids, pick_rows, target_ids):
    lowered = tuple((low(weight) for weight in masters))
    step_loss = jax.checkpoint(sequence_loss)

    def add_one(carry, inputs):
        return (carry + step_loss(lowered, inputs[0], inputs[1], inputs[2]), None)
    summed, _ = lax.scan(add_one, jnp.float32(0.0), (token_ids, pick_rows, target_ids))
    return summed / COUNT

def reference(token_ids, pick_rows, target_ids, attn_in, attn_out, mlp_in, mlp_out, positions, vectors, table, first_attn_in, first_attn_out, first_mlp_in, first_mlp_out, first_positions, first_vectors, first_table, second_attn_in, second_attn_out, second_mlp_in, second_mlp_out, second_positions, second_vectors, second_table):
    masters = (attn_in, attn_out, mlp_in, mlp_out, positions, vectors, table)
    firsts = (first_attn_in, first_attn_out, first_mlp_in, first_mlp_out, first_positions, first_vectors, first_table)
    seconds = (second_attn_in, second_attn_out, second_mlp_in, second_mlp_out, second_positions, second_vectors, second_table)
    loss, pullback = jax.vjp(lambda *weights: total_loss(weights, token_ids, pick_rows, target_ids), *masters)
    gradients = pullback(jnp.float32(1.0))
    grad_norm = jnp.sqrt(sum((jnp.sum(gradient * gradient) for gradient in gradients)))
    factor = jnp.minimum(1.0, CLIP_AT / grad_norm)
    new_weights, new_firsts, new_seconds, ratio_list = ([], [], [], [])
    for weight, gradient, moment_one, moment_two in zip(masters, gradients, firsts, seconds):
        clipped = gradient * factor
        moment_one = BETA_ONE * moment_one + (1.0 - BETA_ONE) * clipped
        moment_two = BETA_TWO * moment_two + (1.0 - BETA_TWO) * clipped * clipped
        update = moment_one / (1.0 - BETA_ONE ** STEP) / (jnp.sqrt(moment_two / (1.0 - BETA_TWO ** STEP)) + ADAM_EPS) + DECAY * weight
        ratio = jnp.sqrt(jnp.sum(weight * weight)) / jnp.sqrt(jnp.sum(update * update))
        new_weights.append(weight - RATE * ratio * update)
        new_firsts.append(moment_one)
        new_seconds.append(moment_two)
        ratio_list.append(ratio)
    ratios = jnp.stack(ratio_list)
    return (loss, grad_norm, ratios, new_weights[0], new_weights[1], new_weights[2], new_weights[3], new_weights[4], new_weights[5], new_weights[6], new_firsts[0], new_firsts[1], new_firsts[2], new_firsts[3], new_firsts[4], new_firsts[5], new_firsts[6], new_seconds[0], new_seconds[1], new_seconds[2], new_seconds[3], new_seconds[4], new_seconds[5], new_seconds[6])
```

```python
import jax
import jax.numpy as jnp
from jax import lax
from jax.sharding import PartitionSpec as P

HD = 64
V_REAL = 50257
STEP = 5


LN_EPS = 1e-05
SMOOTHING = 0.1
BETA_ONE = 0.9
BETA_TWO = 0.999
ADAM_EPS = 1e-12
DECAY = 0.01
RATE = 0.3
CLIP_AT = 0.01
MASKED = -1e30


def layer_norm(inputs, gain, shift):
    centre = jnp.mean(inputs, axis=-1, keepdims=True)
    centred = inputs - centre
    spread = jnp.mean(centred * centred, axis=-1, keepdims=True)
    return centred * lax.rsqrt(spread + LN_EPS) * gain + shift


def gelu_tanh(inputs):
    return (
        0.5
        * inputs
        * (1.0 + jnp.tanh(0.7978845608028654 * (inputs + 0.044715 * inputs * inputs * inputs)))
    )


def dot_plain(left_op, right_op):
    return jnp.dot(left_op, right_op, preferred_element_type=jnp.float32)


def dot_first(left_op, right_op):
    return lax.dot_general(
        left_op, right_op, (((0,), (0,)), ((), ())), preferred_element_type=jnp.float32
    )


def dot_second(left_op, right_op):
    return lax.dot_general(
        left_op, right_op, (((1,), (1,)), ((), ())), preferred_element_type=jnp.float32
    )


def block_scores(query_blk, keys_all, offset):
    scores = jnp.einsum(
        "qhd,khd->hqk", query_blk, keys_all, preferred_element_type=jnp.float32
    ) * HD ** (-0.5)
    places = offset + jnp.arange(query_blk.shape[0])[:, None]
    causal = jnp.arange(keys_all.shape[0])[None, :] <= places
    return jnp.where(causal[None], scores, MASKED)


def split_blocks(queries):
    seq_len = queries.shape[0]
    block_rows = min(512, seq_len)
    count_blocks = seq_len // block_rows
    starts = jnp.arange(count_blocks, dtype=jnp.int32) * block_rows
    return (block_rows, count_blocks, starts)


def attention_forward(queries, keys_all, values_all):
    block_rows, count_blocks, starts = split_blocks(queries)
    stacked = queries.reshape(count_blocks, block_rows, queries.shape[1], queries.shape[2])

    def one_block(inputs):
        query_blk, offset = inputs
        scores = block_scores(query_blk, keys_all, offset)
        row_top = jnp.max(scores, axis=-1, keepdims=True)
        exp_scores = jnp.exp(scores - row_top)
        totals = jnp.sum(exp_scores, axis=-1, keepdims=True)
        attn_probs = (exp_scores / totals).astype(jnp.bfloat16)
        mixed_out = jnp.einsum(
            "hqk,khd->qhd", attn_probs, values_all, preferred_element_type=jnp.float32
        )
        return (mixed_out, (row_top + jnp.log(totals))[..., 0])

    mixed_out, log_total = lax.map(one_block, (stacked, starts))
    return (mixed_out.reshape(queries.shape), log_total)


def attention_backward(queries, keys_all, values_all, log_total, grad_mixed):
    block_rows, count_blocks, starts = split_blocks(queries)
    shape_blk = (count_blocks, block_rows, queries.shape[1], queries.shape[2])

    def one_block(carry, inputs):
        query_blk, grad_blk, lse_blk, offset = inputs
        scores = block_scores(query_blk, keys_all, offset)
        soft = jnp.exp(scores - lse_blk[..., None])
        grad_p = jnp.einsum(
            "qhd,khd->hqk", grad_blk, values_all, preferred_element_type=jnp.float32
        )
        centre = jnp.sum(soft * grad_p, axis=-1, keepdims=True)
        grad_s = (soft * (grad_p - centre)).astype(jnp.bfloat16)
        grad_q = jnp.einsum(
            "hqk,khd->qhd", grad_s, keys_all, preferred_element_type=jnp.float32
        ) * HD ** (-0.5)
        grad_k = carry[0] + jnp.einsum(
            "hqk,qhd->khd", grad_s, query_blk, preferred_element_type=jnp.float32
        ) * HD ** (-0.5)
        grad_v = carry[1] + jnp.einsum(
            "hqk,qhd->khd", soft.astype(jnp.bfloat16), grad_blk, preferred_element_type=jnp.float32
        )
        return ((grad_k, grad_v), grad_q)

    zeros_kv = jnp.zeros(keys_all.shape, jnp.float32)
    (grad_k, grad_v), grad_q = lax.scan(
        one_block,
        (zeros_kv, zeros_kv),
        (queries.reshape(shape_blk), grad_mixed.reshape(shape_blk), log_total, starts),
    )
    return (grad_q.reshape(queries.shape), grad_k, grad_v)


def layer_forward(resid_in, w_qkv, w_proj, w_up, w_down, vec_rows):
    seq_len, width = resid_in.shape
    head_count = width // HD
    normed_one = layer_norm(resid_in, vec_rows[0], vec_rows[1]).astype(jnp.bfloat16)
    qkv_bias = jnp.concatenate([vec_rows[6], jnp.zeros_like(vec_rows[6]), vec_rows[7]])
    packed = (dot_plain(normed_one, w_qkv) + qkv_bias).astype(jnp.bfloat16)
    queries = packed[:, :width].reshape(seq_len, head_count, HD)
    keys_all = packed[:, width : 2 * width].reshape(seq_len, head_count, HD)
    values_all = packed[:, 2 * width :].reshape(seq_len, head_count, HD)
    attended, log_total = attention_forward(queries, keys_all, values_all)
    attended = attended.reshape(seq_len, width).astype(jnp.bfloat16)
    resid_mid = resid_in + dot_plain(attended, w_proj) + vec_rows[8]
    normed_two = layer_norm(resid_mid, vec_rows[2], vec_rows[3]).astype(jnp.bfloat16)
    hidden_pre = dot_plain(normed_two, w_up) + vec_rows[10:14].reshape(-1)
    hidden_act = gelu_tanh(hidden_pre).astype(jnp.bfloat16)
    resid_out = resid_mid + dot_plain(hidden_act, w_down) + vec_rows[9]
    kept = (
        resid_in,
        resid_mid,
        normed_one,
        normed_two,
        queries,
        keys_all,
        values_all,
        log_total,
        attended,
        hidden_pre,
        hidden_act,
    )
    return (resid_out, kept)


def layer_backward(grad_out, kept, w_qkv, w_proj, w_up, w_down, vec_rows):
    (
        resid_in,
        resid_mid,
        normed_one,
        normed_two,
        queries,
        keys_all,
        values_all,
        log_total,
        attended,
        hidden_pre,
        hidden_act,
    ) = kept
    seq_len, width = resid_in.shape
    devices = lax.axis_size("dp") * lax.axis_size("vocab")
    grad_branch = grad_out.astype(jnp.bfloat16)
    grad_down = grad_shard(hidden_act, grad_branch, hidden_act.shape[1] // devices, halves(width))
    bias_down = jnp.sum(grad_branch.astype(jnp.float32), axis=0)
    grad_act = dot_second(grad_branch, w_down)
    grad_pre = jax.vjp(gelu_tanh, hidden_pre)[1](grad_act)[0].astype(jnp.bfloat16)
    grad_up = grad_shard(normed_two, grad_pre, width // devices, halves(grad_pre.shape[1]))
    bias_up = jnp.sum(grad_pre.astype(jnp.float32), axis=0)
    grad_two = dot_second(grad_pre, w_up)
    grad_mid, gain_two, shift_two = jax.vjp(layer_norm, resid_mid, vec_rows[2], vec_rows[3])[1](
        grad_two
    )
    grad_mid = grad_mid + grad_out
    grad_attn = grad_mid.astype(jnp.bfloat16)
    grad_proj = grad_shard(attended, grad_attn, width // devices, halves(width))
    bias_proj = jnp.sum(grad_attn.astype(jnp.float32), axis=0)
    grad_mixed = dot_second(grad_attn, w_proj).astype(jnp.bfloat16).reshape(queries.shape)
    grad_q, grad_k, grad_v = attention_backward(
        queries, keys_all, values_all, log_total, grad_mixed
    )
    grad_packed = jnp.concatenate(
        [
            grad_q.reshape(seq_len, width),
            grad_k.reshape(seq_len, width),
            grad_v.reshape(seq_len, width),
        ],
        axis=1,
    ).astype(jnp.bfloat16)
    grad_qkv = grad_shard(normed_one, grad_packed, width // devices, halves(3 * width))
    bias_qkv = jnp.sum(grad_packed.astype(jnp.float32), axis=0)
    grad_one = dot_second(grad_packed, w_qkv)
    grad_in, gain_one, shift_one = jax.vjp(layer_norm, resid_in, vec_rows[0], vec_rows[1])[1](
        grad_one
    )
    grad_in = grad_in + grad_mid
    vec_grads = (
        gain_one,
        shift_one,
        gain_two,
        shift_two,
        bias_qkv[:width],
        bias_qkv[2 * width :],
        bias_proj,
        bias_down,
        bias_up.reshape(4, width),
    )
    return (grad_in, (grad_qkv, grad_proj, grad_up, grad_down), vec_grads)


def bit_of(index, level):
    return (index >> level) & 1


def xor_order(parts, index):
    level = 0
    while (1 << level) < len(parts):
        odd = bit_of(index, level) == 1
        step = 1 << level
        placed = list(parts)
        for place in range(len(parts)):
            if not place & step:
                low, high = parts[place], parts[place | step]
                placed[place] = jnp.where(odd, high, low)
                placed[place | step] = jnp.where(odd, low, high)
        parts = placed
        level += 1
    return parts


def tree_sum(parts):
    while len(parts) > 1:
        parts = [parts[place] + parts[place + 1] for place in range(0, len(parts), 2)]
    return parts[0]


def swap_core(value):
    count = lax.axis_size("vocab")
    return lax.ppermute(value, "vocab", [(i, i ^ 1) for i in range(count)])


def swap_outer(value, step):
    count = lax.axis_size("vocab")
    return lax.ppermute(value, "vocab", [(i, i ^ (2 * step)) for i in range(count)])


def swap_dp(value, step):
    count = lax.axis_size("dp")
    return lax.ppermute(value, "dp", [(i, i ^ step) for i in range(count)])


def places():
    vocab_index = lax.axis_index("vocab")
    return (lax.axis_index("dp"), vocab_index // 2, vocab_index % 2)


def gather_vocab(value):
    _, outer, core = places()
    pair = jnp.stack(xor_order([value, swap_core(value)], core))
    count = lax.axis_size("vocab") // 2
    parts = [pair] + [swap_outer(pair, step) for step in range(1, count)]
    return jnp.concatenate(xor_order(parts, outer), axis=0)


def gather_dp(value):
    dp_index, _, _ = places()
    parts = [value] + [swap_dp(value, step) for step in range(1, lax.axis_size("dp"))]
    return jnp.stack(xor_order(parts, dp_index))


def sum_all(value):
    value = value + swap_core(value)
    value = tree_sum([value] + [swap_dp(value, step) for step in range(1, lax.axis_size("dp"))])
    count = lax.axis_size("vocab") // 2
    return tree_sum([value] + [swap_outer(value, step) for step in range(1, count)])


def gather_all(value, flip):
    dp_index, outer, core = places()
    count = lax.axis_size("vocab") // 2
    parts = [value] + [swap_outer(value, step) for step in range(1, count)]
    held = jnp.stack(xor_order(parts, outer))
    held = held[None, None]
    for bit in (0, 1) if flip else (1, 0):
        other = swap_dp(held, 1 << bit)
        held = jnp.concatenate(xor_order([held, other], bit_of(dp_index, bit)), axis=1 - bit)
    held = held.reshape((-1,) + value.shape)
    return jnp.stack(xor_order([held, swap_core(held)], core), axis=1).reshape(
        (-1,) + value.shape[1:]
    )


def pick_half(value, index, axis):
    return lax.dynamic_index_in_dim(value, index, axis, keepdims=False)


def scatter_sum(keep, sent, flip):
    dp_index, outer, _ = places()
    count = lax.axis_size("vocab") // 2
    held = keep + swap_core(sent.astype(jnp.bfloat16)).astype(jnp.float32)
    held = held.reshape((2, 2, count) + keep.shape[1:])
    first, second = (0, 1) if flip else (1, 0)
    own = bit_of(dp_index, first)
    axis = 1 - first
    out = pick_half(held, 1 - own, axis).astype(jnp.bfloat16)
    held = pick_half(held, own, axis) + swap_dp(out, 1 << first).astype(jnp.float32)
    own = bit_of(dp_index, second)
    out = pick_half(held, 1 - own, 0).astype(jnp.bfloat16)
    held = pick_half(held, own, 0) + swap_dp(out, 1 << second).astype(jnp.float32)
    terms = [pick_half(held, outer, 0)]
    for step in range(1, count):
        out = pick_half(held, outer ^ step, 0).astype(jnp.bfloat16)
        terms.append(swap_outer(out, step).astype(jnp.float32))
    return tree_sum(terms)


def core_split(value, rows):
    _, _, core = places()
    tokens = value.shape[0]
    grouped = value.reshape(tokens, -1, 2, rows)
    keep = pick_half(grouped, core, 2).reshape(tokens, -1)
    sent = pick_half(grouped, 1 - core, 2).reshape(tokens, -1)
    return (keep, sent)


def grad_shard(left, right, rows, cuts):
    keep_cols, sent_cols = core_split(left, rows)
    made = []
    for place, (start, stop) in enumerate(cuts):
        piece = right[:, start:stop]
        sent = dot_first(sent_cols, piece).astype(jnp.bfloat16)
        keep = dot_first(keep_cols, piece)
        shape = (-1, rows, stop - start)
        made.append(scatter_sum(keep.reshape(shape), sent.reshape(shape), place % 2 == 1))
    return jnp.concatenate(made, axis=1)


def halves(width):
    return ((0, width // 2), (width // 2, width))


def shards(
    token_ids,
    pick_rows,
    target_ids,
    attn_in,
    attn_out,
    mlp_in,
    mlp_out,
    positions,
    vectors,
    table,
    *moments,
):
    low = jnp.bfloat16
    dp_index, outer, core = places()
    dp_count = lax.axis_size("dp")
    shard_count = lax.axis_size("vocab")
    device_count = dp_count * shard_count
    outer_count = shard_count // 2
    vocab_rows, width = table.shape
    seq_len = token_ids.shape[1]
    pick_count = pick_rows.shape[1]
    vocab_start = lax.axis_index("vocab") * vocab_rows

    packed_ids = jnp.concatenate([token_ids, target_ids], axis=1)
    group_packed = gather_vocab(packed_ids).reshape(shard_count, -1)
    group_ids = group_packed[:, :seq_len]
    group_targets = group_packed[:, seq_len:]

    small_rows = positions.shape[0]
    vec_flat = vectors.astype(low).reshape(-1)
    vec_pad = -vec_flat.size % width
    small = jnp.concatenate(
        [positions.astype(low), jnp.pad(vec_flat, (0, vec_pad)).reshape(-1, width)], axis=0
    )
    small_all = gather_all(small, False).reshape((device_count,) + small.shape)
    pos_low = small_all[:, :small_rows].reshape(-1, width)
    vec_low = small_all[:, small_rows:].reshape(device_count, -1)[:, : vec_flat.size]
    vec_low = vec_low.reshape((device_count,) + vectors.shape)
    vec_rows = jnp.moveaxis(vec_low, 0, 1).reshape(vectors.shape[0], width).astype(jnp.float32)

    def gather_weight(weight):
        return jnp.concatenate(
            [
                gather_all(weight[:, start:stop].astype(low), place % 2 == 1)
                for place, (start, stop) in enumerate(halves(weight.shape[1]))
            ],
            axis=1,
        )

    w_qkv = gather_weight(attn_in)
    w_proj = gather_weight(attn_out)
    w_up = gather_weight(mlp_in)
    w_down = gather_weight(mlp_out)
    table_low = table.astype(low)

    group_local = group_ids - vocab_start
    mine = (group_local >= 0) & (group_local < vocab_rows)
    served = jnp.take(table, jnp.where(mine, group_local, 0).reshape(-1), axis=0)
    served = jnp.where(mine.reshape(-1)[:, None], served, 0.0).astype(low)
    served = served.reshape(outer_count, 2, seq_len, width)
    held = pick_half(served, core, 1) + swap_core(pick_half(served, 1 - core, 1))
    terms = [pick_half(held, outer, 0)]
    for step in range(1, outer_count):
        terms.append(swap_outer(pick_half(held, outer ^ step, 0), step))
    resid_in = tree_sum(terms).astype(jnp.float32) + pos_low.astype(jnp.float32)

    resid_out, kept = layer_forward(resid_in, w_qkv, w_proj, w_up, w_down, vec_rows)
    final_low = layer_norm(resid_out, vec_rows[4], vec_rows[5]).astype(low)
    own_picks = pick_rows.reshape(-1)
    pick_hot = own_picks[:, None] == jnp.arange(seq_len, dtype=jnp.int32)[None, :]
    picked = dot_plain(pick_hot.astype(low), final_low).astype(low)

    _parts = [picked] + [swap_outer(picked, step) for step in range(1, outer_count)]
    same_core = jnp.stack(xor_order(_parts, outer))
    head_in = jnp.stack(xor_order([same_core, swap_core(same_core)], core), axis=1)
    head_in = head_in.reshape(-1, width)
    columns = vocab_start + jnp.arange(vocab_rows, dtype=jnp.int32)
    is_real = columns < V_REAL
    flat_targets = group_targets.reshape(-1)
    logits = jnp.where(is_real[None, :], dot_second(head_in, table_low), MASKED)
    is_target = columns[None, :] == flat_targets[:, None]
    target_part = jnp.sum(jnp.where(is_target, logits, 0.0), axis=1)
    logit_part = jnp.sum(jnp.where(is_real[None, :], logits, 0.0), axis=1)
    top_part = jnp.max(logits, axis=1)
    exp_part = jnp.sum(jnp.exp(logits - top_part[:, None]), axis=1)
    stats = gather_vocab(jnp.stack([top_part, exp_part, target_part, logit_part]))
    stats = stats.reshape(shard_count, 4, -1)
    row_top = jnp.max(stats[:, 0], axis=0)
    exp_total = jnp.sum(stats[:, 1] * jnp.exp(stats[:, 0] - row_top[None]), axis=0)
    target_logit = jnp.sum(stats[:, 2], axis=0)
    logit_total = jnp.sum(stats[:, 3], axis=0)
    log_norm = row_top + jnp.log(exp_total)
    row_loss = (1.0 - SMOOTHING) * (log_norm - target_logit) + SMOOTHING * (
        log_norm - logit_total / V_REAL
    )
    token_count = device_count * pick_count

    def logit_grad(values, norms, targets):
        soft = jnp.exp(values - norms[:, None])
        hit = columns[None, :] == targets[:, None]
        return (
            (soft - (1.0 - SMOOTHING) * hit - SMOOTHING / V_REAL * is_real[None, :]) / token_count
        ).astype(low)

    partial = dot_plain(logit_grad(logits, log_norm, flat_targets), table_low)
    partial = partial.reshape(outer_count, 2, pick_count, width)
    held = pick_half(partial, core, 1) + swap_core(
        pick_half(partial, 1 - core, 1).astype(low)
    ).astype(jnp.float32)
    terms = [pick_half(held, outer, 0)]
    for step in range(1, outer_count):
        out = pick_half(held, outer ^ step, 0).astype(low)
        terms.append(swap_outer(out, step).astype(jnp.float32))
    picked_grad = tree_sum(terms)
    final_grad = lax.dot_general(
        pick_hot.astype(jnp.float32),
        picked_grad,
        (((0,), (0,)), ((), ())),
        precision=lax.Precision.HIGHEST,
        preferred_element_type=jnp.float32,
    )

    half = lax.dynamic_slice_in_dim(head_in, core * (width // 2), width // 2, axis=1)
    half_all = half[None]
    for bit in (0, 1):
        half_all = jnp.concatenate(
            xor_order([half_all, swap_dp(half_all, 1 << bit)], bit_of(dp_index, bit)), axis=0
        )
    head_all = jnp.concatenate(xor_order([half_all, swap_core(half_all)], core), axis=2)
    head_all = head_all.reshape(-1, width)
    norm_all = gather_dp(log_norm).reshape(-1)
    packed_all = gather_dp(group_packed).reshape(device_count, -1)
    ids_all = packed_all[:, :seq_len].reshape(-1)
    targets_all = packed_all[:, seq_len:].reshape(-1)

    grad_top, gain_final, shift_final = jax.vjp(layer_norm, resid_out, vec_rows[4], vec_rows[5])[1](
        final_grad
    )
    grad_in, matrix_grads, vec_grads = layer_backward(
        grad_top, kept, w_qkv, w_proj, w_up, w_down, vec_rows
    )
    grad_rows = grad_in.astype(low)
    rows_all = jnp.concatenate(
        [
            gather_all(grad_rows[:, start:stop], place % 2 == 1)
            for place, (start, stop) in enumerate(halves(width))
        ],
        axis=1,
    )

    all_logits = jnp.where(is_real[None, :], dot_second(head_all, table_low), MASKED)
    table_grad = dot_first(logit_grad(all_logits, norm_all, targets_all), head_all)
    local_all = ids_all - vocab_start
    inside = (local_all >= 0) & (local_all < vocab_rows)
    table_grad = table_grad.at[jnp.where(inside, local_all, vocab_rows)].add(
        rows_all.astype(jnp.float32), mode="drop"
    )
    loss = tree_sum(
        [jnp.sum(row_loss)[None]]
        + [swap_dp(jnp.sum(row_loss)[None], step) for step in range(1, dp_count)]
    )[0] / token_count
    (
        gain_one,
        shift_one,
        gain_two,
        shift_two,
        bias_query,
        bias_value,
        bias_proj,
        bias_down,
        bias_up,
    ) = vec_grads
    vec_grad = jnp.concatenate(
        [
            jnp.stack(
                [
                    gain_one,
                    shift_one,
                    gain_two,
                    shift_two,
                    gain_final,
                    shift_final,
                    bias_query,
                    bias_value,
                    bias_proj,
                    bias_down,
                ]
            ),
            bias_up,
        ],
        axis=0,
    )
    vec_total = sum_all(vec_grad)
    vec_width = vectors.shape[1]
    device_index = lax.axis_index(("dp", "vocab"))
    vec_own = lax.dynamic_slice_in_dim(vec_total, device_index * vec_width, vec_width, axis=1)
    grad_blocks = grad_in.reshape(-1, 2, small_rows, width)
    pos_own = scatter_sum(
        pick_half(grad_blocks, core, 1), pick_half(grad_blocks, 1 - core, 1), False
    )
    gradients = tuple(matrix_grads) + (pos_own, vec_own, table_grad)
    masters = (attn_in, attn_out, mlp_in, mlp_out, positions, vectors, table)
    firsts = moments[:7]
    seconds = moments[7:]
    shares = (1.0, 1.0, 1.0, 1.0, 1.0, 1.0, 1.0 / dp_count)
    clip_term = sum(
        (jnp.sum(gradient * gradient) * share for gradient, share in zip(gradients, shares))
    )
    weight_terms = [jnp.sum(weight * weight) * share for weight, share in zip(masters, shares)]
    sums = sum_all(jnp.stack([clip_term] + weight_terms))
    clip_total, weight_total = sums[0], sums[1:]
    grad_norm = jnp.sqrt(clip_total)
    factor = jnp.minimum(1.0, CLIP_AT / grad_norm)
    new_firsts, new_seconds, updates, update_terms = ([], [], [], [])
    for weight, gradient, moment_one, moment_two, share in zip(
        masters, gradients, firsts, seconds, shares
    ):
        clipped = gradient * factor
        moment_one = BETA_ONE * moment_one + (1.0 - BETA_ONE) * clipped
        moment_two = BETA_TWO * moment_two + (1.0 - BETA_TWO) * clipped * clipped
        update = (
            moment_one
            / (1.0 - BETA_ONE**STEP)
            / (jnp.sqrt(moment_two / (1.0 - BETA_TWO**STEP)) + ADAM_EPS)
            + DECAY * weight
        )
        new_firsts.append(moment_one)
        new_seconds.append(moment_two)
        updates.append(update)
        update_terms.append(jnp.sum(update * update) * share)
    update_total = sum_all(jnp.stack(update_terms))
    ratios = jnp.sqrt(weight_total) / jnp.sqrt(update_total)
    new_weights = [
        weight - RATE * ratios[index] * update
        for index, (weight, update) in enumerate(zip(masters, updates))
    ]
    return (loss, grad_norm, ratios, *new_weights, *new_firsts, *new_seconds)


def solution(mesh):
    rows = P(("dp", "vocab"), None)
    weights = (rows, rows, rows, rows, rows, P(None, ("dp", "vocab")), P("vocab", None))
    return jax.shard_map(
        shards,
        mesh=mesh,
        in_specs=(rows, rows, rows) + weights * 3,
        out_specs=(P(), P(), P()) + weights * 3,
        check_vma=False,
    )
```

```python
import functools
import math

import jax
import jax.numpy as jnp
from jax import lax
from jax.experimental import pallas as pl
from jax.experimental.pallas import tpu as pltpu
from jax.sharding import PartitionSpec as P

HD = 64
V_REAL = 50257
STEP = 5


LN_EPS = 1e-05
SMOOTHING = 0.1
BETA_ONE = 0.9
BETA_TWO = 0.999
ADAM_EPS = 1e-12
DECAY = 0.01
RATE = 0.3
CLIP_AT = 0.01
MASKED = -1e30
CHUNK = 1280
PIECE = 640
VMEM_BYTES = 58 * 2**20


def layer_norm(inputs, gain, shift):
    centre = jnp.mean(inputs, axis=-1, keepdims=True)
    centred = inputs - centre
    spread = jnp.mean(centred * centred, axis=-1, keepdims=True)
    return centred * lax.rsqrt(spread + LN_EPS) * gain + shift


def gelu_tanh(inputs):
    return (
        0.5
        * inputs
        * (1.0 + jnp.tanh(0.7978845608028654 * (inputs + 0.044715 * inputs * inputs * inputs)))
    )


def dot_plain(left_op, right_op):
    return jnp.dot(left_op, right_op, preferred_element_type=jnp.float32)


def dot_first(left_op, right_op):
    return lax.dot_general(
        left_op, right_op, (((0,), (0,)), ((), ())), preferred_element_type=jnp.float32
    )


def dot_second(left_op, right_op):
    return lax.dot_general(
        left_op, right_op, (((1,), (1,)), ((), ())), preferred_element_type=jnp.float32
    )


def params():
    return pltpu.CompilerParams(vmem_limit_bytes=VMEM_BYTES)


def cost(flops, bytes_accessed):
    return pl.CostEstimate(
        flops=int(flops), bytes_accessed=int(bytes_accessed), transcendentals=0
    )


def whole_block():
    return pl.BlockSpec(memory_space=pltpu.VMEM)


def shape_of(shape, dtype):
    return jax.ShapeDtypeStruct(tuple(shape), dtype)


def causal_scores(queries, keys, causal):
    return jnp.where(causal, dot_second(queries, keys) * HD ** (-0.5), MASKED)


def causal_mask(count):
    query = lax.broadcasted_iota(jnp.int32, (count, count), 0)
    key = lax.broadcasted_iota(jnp.int32, (count, count), 1)
    return key <= query


def head_span(head):
    return slice(head * HD, (head + 1) * HD)


def attention_forward(embedded, positions, vec_rows, w_qkv, w_proj):
    count, width = embedded.shape
    low = jnp.bfloat16

    def body(e_ref, p_ref, v_ref, qkv_ref, proj_ref, x0_ref, h1_ref, packed_ref, o_ref, x1_ref, h2_ref):
        x0 = e_ref[...] + p_ref[...].astype(jnp.float32)
        x0_ref[...] = x0
        h1 = layer_norm(x0, v_ref[0:1, :], v_ref[1:2, :]).astype(low)
        h1_ref[...] = h1
        parts = []
        for place, bias in enumerate((6, None, 7)):
            span = slice(place * width, (place + 1) * width)
            part = dot_plain(h1, qkv_ref[:, span])
            if bias is not None:
                part = part + v_ref[bias : bias + 1, :]
            parts.append(part.astype(low))
            packed_ref[:, span] = parts[-1]
        queries, keys, values = parts
        causal = causal_mask(count)
        for head in range(0, width // HD, 2):
            mixed = []
            for one in (head, head + 1):
                span = head_span(one)
                scores = causal_scores(queries[:, span], keys[:, span], causal)
                grown = jnp.exp(scores - jnp.max(scores, axis=-1, keepdims=True))
                probs = (grown / jnp.sum(grown, axis=-1, keepdims=True)).astype(low)
                mixed.append(dot_plain(probs, values[:, span]))
            o_ref[:, head * HD : (head + 2) * HD] = jnp.concatenate(mixed, axis=1).astype(low)
        x1 = x0 + dot_plain(o_ref[...], proj_ref[...]) + v_ref[8:9, :]
        x1_ref[...] = x1
        h2_ref[...] = layer_norm(x1, v_ref[2:3, :], v_ref[3:4, :]).astype(low)

    shape = (count, width)
    return pl.pallas_call(
        body,
        out_shape=[
            shape_of(shape, jnp.float32),
            shape_of(shape, low),
            shape_of((count, 3 * width), low),
            shape_of(shape, low),
            shape_of(shape, jnp.float32),
            shape_of(shape, low),
        ],
        in_specs=[whole_block()] * 5,
        out_specs=[whole_block()] * 6,
        compiler_params=params(),
        cost_estimate=cost(16 * count * width * width, 8 * width * width),
    )(embedded, positions, vec_rows, w_qkv, w_proj)


def hidden_forward(normed, vec_rows, w_up):
    count, width = normed.shape
    hidden = w_up.shape[1]

    def body(h_ref, v_ref, w_ref, pre_ref, act_ref):
        for place in range(hidden // width):
            span = slice(place * width, (place + 1) * width)
            pre = dot_plain(h_ref[...], w_ref[:, span]) + v_ref[10 + place : 11 + place, :]
            pre_ref[:, span] = pre
            act_ref[:, span] = gelu_tanh(pre).astype(jnp.bfloat16)

    return pl.pallas_call(
        body,
        out_shape=[
            shape_of((count, hidden), jnp.float32),
            shape_of((count, hidden), jnp.bfloat16),
        ],
        in_specs=[whole_block()] * 3,
        out_specs=[whole_block()] * 2,
        compiler_params=params(),
        cost_estimate=cost(2 * count * width * hidden, 2 * width * hidden),
    )(normed, vec_rows, w_up)


def output_forward(act, w_down, resid_mid, vec_rows, picks):
    count, width = resid_mid.shape
    number = picks.shape[0]

    def body(act_ref, w_ref, x1_ref, v_ref, pick_ref, x2_ref, out_ref):
        x2 = x1_ref[...] + dot_plain(act_ref[...], w_ref[...]) + v_ref[9:10, :]
        x2_ref[...] = x2
        final = layer_norm(x2, v_ref[4:5, :], v_ref[5:6, :]).astype(jnp.bfloat16)
        hot = pick_ref[...] == lax.broadcasted_iota(jnp.int32, (number, count), 1)
        hot = jnp.where(hot, 1.0, 0.0).astype(jnp.bfloat16)
        out_ref[...] = dot_plain(hot, final).astype(jnp.bfloat16)

    return pl.pallas_call(
        body,
        out_shape=[
            shape_of((count, width), jnp.float32),
            shape_of((number, width), jnp.bfloat16),
        ],
        in_specs=[whole_block()] * 5,
        out_specs=[whole_block()] * 2,
        compiler_params=params(),
        cost_estimate=cost(2 * act.size * width, 2 * w_down.size),
    )(act, w_down, resid_mid, vec_rows, picks)


def norm_backward(grad, inputs, gain):
    centred = inputs - jnp.mean(inputs, axis=-1, keepdims=True)
    scale = lax.rsqrt(jnp.mean(centred * centred, axis=-1, keepdims=True) + LN_EPS)
    normed = centred * scale
    scaled = grad * gain
    back = scale * (
        scaled
        - jnp.mean(scaled, axis=-1, keepdims=True)
        - normed * jnp.mean(scaled * normed, axis=-1, keepdims=True)
    )
    return (
        back,
        jnp.sum(grad * normed, axis=0, keepdims=True),
        jnp.sum(grad, axis=0, keepdims=True),
    )


def column_sum(value):
    return jnp.sum(value.astype(jnp.float32), axis=0, keepdims=True)


def select_columns(value, chooser):
    unit = chooser.shape[0]
    parts = [
        dot_plain(value[:, start : start + unit], chooser).astype(jnp.bfloat16)
        for start in range(0, value.shape[1], unit)
    ]
    return parts[0] if len(parts) == 1 else jnp.concatenate(parts, axis=1)


def choosers(width, rows, core):
    column = jnp.arange(width, dtype=jnp.int32)
    target = jnp.arange(width // 2, dtype=jnp.int32)
    made = []
    for side in (core, 1 - core):
        source = (target // rows * 2 + side) * rows + target % rows
        made.append((column[:, None] == source[None, :]).astype(jnp.bfloat16))
    return jnp.stack(made)


def output_backward(picked_grad, picks, resid_out, vec_rows, act, chooser):
    count, width = resid_out.shape
    number = picks.shape[0]
    half = act.shape[1] // 2
    low = jnp.bfloat16

    def body(g_ref, pick_ref, x_ref, v_ref, act_ref, c_ref, dx_ref, dy_ref, keep_ref, sent_ref, vec_ref):
        hot = pick_ref[...] == lax.broadcasted_iota(jnp.int32, (number, count), 1)
        final_grad = lax.dot_general(
            jnp.where(hot, 1.0, 0.0),
            g_ref[...],
            (((0,), (0,)), ((), ())),
            precision=lax.Precision.HIGHEST,
            preferred_element_type=jnp.float32,
        )
        back, gain, shift = norm_backward(final_grad, x_ref[...], v_ref[4:5, :])
        dx_ref[...] = back
        dy = back.astype(low)
        dy_ref[...] = dy
        vec_ref[0:1, :] = gain
        vec_ref[1:2, :] = shift
        vec_ref[2:3, :] = column_sum(dy)
        vec_ref[3:8, :] = jnp.zeros((5, width), jnp.float32)
        sent_ref[...] = dot_first(select_columns(act_ref[...], c_ref[1]), dy).astype(low)
        keep_ref[...] = dot_first(select_columns(act_ref[...], c_ref[0]), dy)

    return pl.pallas_call(
        body,
        out_shape=[
            shape_of((count, width), jnp.float32),
            shape_of((count, width), low),
            shape_of((half, width), jnp.float32),
            shape_of((half, width), low),
            shape_of((8, width), jnp.float32),
        ],
        in_specs=[whole_block()] * 6,
        out_specs=[whole_block()] * 5,
        compiler_params=params(),
        cost_estimate=cost(4 * act.size * width, 6 * half * width),
    )(picked_grad, picks, resid_out, vec_rows, act, chooser)


def hidden_backward(dy, w_down, pre, normed, chooser):
    count, width = dy.shape
    hidden = pre.shape[1]
    half = width // 2
    low = jnp.bfloat16

    def body(dy_ref, w_ref, pre_ref, h_ref, c_ref, dpre_ref, keep_ref, sent_ref, vec_ref):
        keep_cols = select_columns(h_ref[...], c_ref[0])
        sent_cols = select_columns(h_ref[...], c_ref[1])
        vec_ref[...] = jnp.zeros_like(vec_ref)
        for place in range(hidden // width):
            span = slice(place * width, (place + 1) * width)
            grad = dot_second(dy_ref[...], w_ref[span, :])
            u = pre_ref[:, span]
            bent = jnp.tanh(0.7978845608028654 * (u + 0.044715 * u * u * u))
            slope = 0.5 * (1.0 + bent) + 0.5 * u * (1.0 - bent * bent) * (
                0.7978845608028654 * (1.0 + 3.0 * 0.044715 * u * u)
            )
            dpre = (grad * slope).astype(low)
            dpre_ref[:, span] = dpre
            vec_ref[place : place + 1, :] = column_sum(dpre)
            sent_ref[:, span] = dot_first(sent_cols, dpre).astype(low)
            keep_ref[:, span] = dot_first(keep_cols, dpre)

    return pl.pallas_call(
        body,
        out_shape=[
            shape_of((count, hidden), low),
            shape_of((half, hidden), jnp.float32),
            shape_of((half, hidden), low),
            shape_of((8, width), jnp.float32),
        ],
        in_specs=[whole_block()] * 5,
        out_specs=[whole_block()] * 4,
        compiler_params=params(),
        cost_estimate=cost(6 * count * width * hidden, 8 * width * hidden),
    )(dy, w_down, pre, normed, chooser)


def middle_backward(dpre, w_up, dx2, x1, attended, w_proj, vec_rows, chooser):
    count, width = x1.shape
    half = width // 2
    low = jnp.bfloat16

    def body(dpre_ref, up_ref, dx2_ref, x1_ref, o_ref, proj_ref, v_ref, c_ref, dx1_ref, mixed_ref, keep_ref, sent_ref, vec_ref):
        dh2 = dot_second(dpre_ref[...], up_ref[...])
        back, gain, shift = norm_backward(dh2, x1_ref[...], v_ref[2:3, :])
        dx1 = back + dx2_ref[...]
        dx1_ref[...] = dx1
        da = dx1.astype(low)
        vec_ref[0:1, :] = gain
        vec_ref[1:2, :] = shift
        vec_ref[2:3, :] = column_sum(da)
        vec_ref[3:8, :] = jnp.zeros((5, width), jnp.float32)
        sent_ref[...] = dot_first(select_columns(o_ref[...], c_ref[1]), da).astype(low)
        keep_ref[...] = dot_first(select_columns(o_ref[...], c_ref[0]), da)
        mixed_ref[...] = dot_second(da, proj_ref[...]).astype(low)

    return pl.pallas_call(
        body,
        out_shape=[
            shape_of((count, width), jnp.float32),
            shape_of((count, width), low),
            shape_of((half, width), jnp.float32),
            shape_of((half, width), low),
            shape_of((8, width), jnp.float32),
        ],
        in_specs=[whole_block()] * 8,
        out_specs=[whole_block()] * 5,
        compiler_params=params(),
        cost_estimate=cost(12 * count * width * width, 12 * width * width),
    )(dpre, w_up, dx2, x1, attended, w_proj, vec_rows, chooser)


def attention_backward(mixed, dx1, packed, x0, normed, w_qkv, vec_rows, chooser, proj_keep, proj_sent, extra):
    count, width = x0.shape
    half = width // 2
    low = jnp.bfloat16

    def body(mixed_ref, dx1_ref, packed_ref, x0_ref, h1_ref, qkv_ref, v_ref, c_ref, pk_ref, ps_ref,
             dx0_ref, rows_ref, keep_ref, sent_ref, vec_ref, grad_ref):
        causal = causal_mask(count)
        for head in range(0, width // HD, 2):
            sides = ([], [], [])
            for one in (head, head + 1):
                queries = packed_ref[:, one * HD : (one + 1) * HD]
                keys = packed_ref[:, width + one * HD : width + (one + 1) * HD]
                values = packed_ref[:, 2 * width + one * HD : 2 * width + (one + 1) * HD]
                scores = causal_scores(queries, keys, causal)
                grown = jnp.exp(scores - jnp.max(scores, axis=-1, keepdims=True))
                probs = grown / jnp.sum(grown, axis=-1, keepdims=True)
                out_grad = mixed_ref[:, one * HD : (one + 1) * HD]
                grad_p = dot_second(out_grad, values)
                centre = jnp.sum(probs * grad_p, axis=-1, keepdims=True)
                grad_s = (probs * (grad_p - centre)).astype(low)
                sides[0].append(dot_plain(grad_s, keys) * HD ** (-0.5))
                sides[1].append(dot_first(grad_s, queries) * HD ** (-0.5))
                sides[2].append(dot_first(probs.astype(low), out_grad))
            for place, side in enumerate(sides):
                start = place * width + head * HD
                grad_ref[:, start : start + 2 * HD] = jnp.concatenate(side, axis=1).astype(low)
        dh1 = dot_second(grad_ref[...], qkv_ref[...])
        back, gain, shift = norm_backward(dh1, x0_ref[...], v_ref[0:1, :])
        vec_ref[0:1, :] = gain
        vec_ref[1:2, :] = shift
        vec_ref[2:3, :] = column_sum(grad_ref[:, :width])
        vec_ref[3:4, :] = column_sum(grad_ref[:, 2 * width :])
        vec_ref[4:8, :] = jnp.zeros((4, width), jnp.float32)
        dx0 = back + dx1_ref[...]
        dx0_ref[...] = dx0
        rows_ref[...] = dx0.astype(low)
        keep_cols = select_columns(h1_ref[...], c_ref[0])
        sent_cols = select_columns(h1_ref[...], c_ref[1])
        for place in range(3):
            span = slice(place * width, (place + 1) * width)
            sent_ref[:, span] = dot_first(sent_cols, grad_ref[:, span]).astype(low)
            keep_ref[:, span] = dot_first(keep_cols, grad_ref[:, span])
        sent_ref[:, 3 * width : 4 * width] = ps_ref[...]
        keep_ref[:, 3 * width : 4 * width] = pk_ref[...]

    return pl.pallas_call(
        body,
        out_shape=[
            shape_of((count, width), jnp.float32),
            shape_of((count, width), low),
            shape_of((half, 4 * width + extra), jnp.float32),
            shape_of((half, 4 * width + extra), low),
            shape_of((8, width), jnp.float32),
        ],
        in_specs=[whole_block()] * 10,
        out_specs=[whole_block()] * 5,
        scratch_shapes=[pltpu.VMEM((count, 3 * width), low)],
        compiler_params=params(),
        cost_estimate=cost(20 * count * width * width, 16 * width * width),
    )(mixed, dx1, packed, x0, normed, w_qkv, vec_rows, chooser, proj_keep, proj_sent)


def bit_of(index, level):
    return (index >> level) & 1


def xor_order(parts, index):
    level = 0
    while (1 << level) < len(parts):
        odd = bit_of(index, level) == 1
        step = 1 << level
        placed = list(parts)
        for place in range(len(parts)):
            if not place & step:
                low, high = parts[place], parts[place | step]
                placed[place] = jnp.where(odd, high, low)
                placed[place | step] = jnp.where(odd, low, high)
        parts = placed
        level += 1
    return parts


def tree_sum(parts):
    while len(parts) > 1:
        parts = [parts[place] + parts[place + 1] for place in range(0, len(parts), 2)]
    return parts[0]


def swap_core(value):
    count = lax.axis_size("vocab")
    return lax.ppermute(value, "vocab", [(i, i ^ 1) for i in range(count)])


def swap_outer(value, step):
    count = lax.axis_size("vocab")
    return lax.ppermute(value, "vocab", [(i, i ^ (2 * step)) for i in range(count)])


def swap_dp(value, step):
    count = lax.axis_size("dp")
    return lax.ppermute(value, "dp", [(i, i ^ step) for i in range(count)])


def places():
    vocab_index = lax.axis_index("vocab")
    return (lax.axis_index("dp"), vocab_index // 2, vocab_index % 2)


def gather_vocab(value):
    _, outer, core = places()
    pair = jnp.stack(xor_order([value, swap_core(value)], core))
    count = lax.axis_size("vocab") // 2
    parts = [pair] + [swap_outer(pair, step) for step in range(1, count)]
    return jnp.concatenate(xor_order(parts, outer), axis=0)


def gather_dp(value):
    dp_index, _, _ = places()
    parts = [value] + [swap_dp(value, step) for step in range(1, lax.axis_size("dp"))]
    return jnp.stack(xor_order(parts, dp_index))


def sum_all(value):
    value = value + swap_core(value)
    value = tree_sum([value] + [swap_dp(value, step) for step in range(1, lax.axis_size("dp"))])
    count = lax.axis_size("vocab") // 2
    return tree_sum([value] + [swap_outer(value, step) for step in range(1, count)])


def outer_parts(value):
    count = lax.axis_size("vocab") // 2
    return [value] + [swap_outer(value, step) for step in range(1, count)]


def behind(value, *others):
    return lax.optimization_barrier((value, others))[0]


class Slots:
    def __init__(self):
        self.last = None

    def open(self, value):
        return value if self.last is None else behind(value, self.last)

    def close(self, *results):
        self.last = results


class OuterGather:
    def __init__(self, value):
        self.held = value[None]

    def advance(self, slots):
        count = lax.axis_size("vocab") // 2
        step = count // (2 * self.held.shape[0])
        if step:
            shape = (-1,) + self.held.shape[1:]
            held = slots.open(self.held)
            self.held = jnp.stack([held, swap_outer(held, step)], axis=1).reshape(shape)

    def finish(self, slots):
        while self.held.shape[0] < lax.axis_size("vocab") // 2:
            self.advance(slots)
        return self.held


def ring_first(held, slots):
    held = slots.open(held)
    return (held, swap_dp(held, 1), swap_dp(held, 2))


def ring_second(parts, slots):
    held, from_one, from_two = parts
    half = held.shape[0] // 2
    low, high = slots.open((from_two[:half], from_one[half:]))
    return jnp.concatenate([held, from_one, from_two, swap_dp(low, 1), swap_dp(high, 2)], axis=0)


def place_blocks(held, other, cuts):
    dp_index, outer, core = places()
    count = held.shape[0]
    outer_count = lax.axis_size("vocab") // 2
    here = jnp.stack([dp_index, outer, core]).astype(jnp.int32)
    spans = []
    for width in cuts:
        spans.append((sum(w for _, w in spans), width))

    def body(here_ref, held_ref, other_ref, *refs):
        out_refs, sems = refs[: len(cuts)], refs[len(cuts)]

        def copies(block):
            dp_place = (block // outer_count) ^ here_ref[0]
            outer_place = (block % outer_count) ^ here_ref[1]
            target = (dp_place * outer_count + outer_place) * 2
            made = []
            for side, ref in enumerate((held_ref, other_ref)):
                place = target + (here_ref[2] ^ side)
                for index, (start, width) in enumerate(spans):
                    made.append(
                        pltpu.make_async_copy(
                            ref.at[block, :, pl.ds(start, width)],
                            out_refs[index].at[place],
                            sems.at[index, side, block],
                        )
                    )
            return made

        def start(block, carry):
            for copy in copies(block):
                copy.start()
            return carry

        def wait(block, carry):
            for copy in copies(block):
                copy.wait()
            return carry

        lax.fori_loop(0, count, start, 0)
        lax.fori_loop(0, count, wait, 0)

    any_space = pl.BlockSpec(memory_space=pl.ANY)
    return pl.pallas_call(
        body,
        out_shape=[
            jax.ShapeDtypeStruct((2 * count, held.shape[1], width), held.dtype) for width in cuts
        ],
        in_specs=[pl.BlockSpec(memory_space=pltpu.SMEM), any_space, any_space],
        out_specs=[pl.BlockSpec(memory_space=pltpu.VMEM) for _ in cuts],
        scratch_shapes=[pltpu.SemaphoreType.DMA((len(cuts), 2, count))],
        compiler_params=pltpu.CompilerParams(vmem_limit_bytes=VMEM_BYTES),
        cost_estimate=pl.CostEstimate(
            flops=0, bytes_accessed=4 * held.size * held.dtype.itemsize, transcendentals=0
        ),
    )(here, held, other)


def tile_of(values):
    row = lax.broadcasted_iota(jnp.int32, (8, 128), 0)
    lane = lax.broadcasted_iota(jnp.int32, (8, 128), 1)
    tile = jnp.zeros((8, 128), jnp.float32)
    for place, value in enumerate(values):
        if value is not None:
            tile = jnp.where((row == 0) & (lane == place), value, tile)
    return tile


def total_of(value):
    return jnp.sum(jnp.sum(value, axis=1, keepdims=True), axis=0, keepdims=True)


def fold_rows(value):
    return jnp.sum(value.reshape(-1, 8, value.shape[1]), axis=0)


def prepare_table(table, smalls, dp_count):
    rows, width = table.shape
    chunks = -(-rows // CHUNK)
    per = max(n for n in range(1, 9) if chunks % n == 0 and n * CHUNK <= rows)
    tile = per * CHUNK
    steps = chunks // per

    def body(table_ref, *refs):
        small_refs, (low_ref, sum_ref, acc_ref) = refs[: len(smalls)], refs[len(smalls) :]
        step = pl.program_id(0)
        row = lax.broadcasted_iota(jnp.int32, (tile, 1), 0) + step * tile
        value = jnp.where(row < rows, table_ref[...], 0.0)
        low_ref[...] = value.astype(jnp.bfloat16)
        part = fold_rows(value * value)

        @pl.when(step == 0)
        def _():
            acc_ref[...] = part

        @pl.when(step > 0)
        def _():
            acc_ref[...] += part

        @pl.when(step == steps - 1)
        def _():
            terms = [None] + [total_of(ref[...] * ref[...]) for ref in small_refs]
            terms.append(total_of(acc_ref[...]) / dp_count)
            sum_ref[...] = tile_of(terms)

    return pl.pallas_call(
        body,
        grid=(steps,),
        out_shape=[
            jax.ShapeDtypeStruct((chunks * CHUNK, width), jnp.bfloat16),
            jax.ShapeDtypeStruct((8, 128), jnp.float32),
        ],
        in_specs=[pl.BlockSpec((tile, width), lambda i: (i, 0))] + [whole_block() for _ in smalls],
        out_specs=[pl.BlockSpec((tile, width), lambda i: (i, 0)), whole_block()],
        scratch_shapes=[pltpu.VMEM((8, width), jnp.float32)],
        compiler_params=pltpu.CompilerParams(vmem_limit_bytes=VMEM_BYTES),
        cost_estimate=pl.CostEstimate(
            flops=4 * table.size, bytes_accessed=6 * table.size, transcendentals=0
        ),
    )(table, *smalls)


def head_stats(head_in, table_low, targets, first, rows):
    count = head_in.shape[0]
    chunks = table_low.shape[0] // CHUNK

    def body(first_ref, head_ref, table_ref, target_ref, out_ref):
        head = head_ref[...]
        target = target_ref[...]
        real = jnp.minimum(rows, V_REAL - first_ref[0])

        def step(index, carry, masked):
            top, total, hit, plain = carry
            begin = pl.multiple_of(index * CHUNK, CHUNK)
            values = dot_second(table_ref[pl.ds(begin, CHUNK), :], head)
            local = lax.broadcasted_iota(jnp.int32, (CHUNK, 1), 0) + begin
            columns = local + first_ref[0]
            if masked:
                columns = jnp.where(local < real, columns, -1)
                plain = plain + fold_rows(jnp.where(local < real, values, 0.0))
                values = jnp.where(local < real, values, MASKED)
            else:
                plain = plain + fold_rows(values)
            blocks = values.reshape(-1, 8, count)
            higher = jnp.maximum(top, jnp.max(blocks, axis=0))
            total = total * jnp.exp(top - higher) + jnp.sum(jnp.exp(blocks - higher[None]), axis=0)
            hit = hit + fold_rows(jnp.where(columns == target, values, 0.0))
            return (higher, total, hit, plain)

        zeros = jnp.zeros((8, count), jnp.float32)
        carry = (jnp.full((8, count), MASKED, jnp.float32), zeros, zeros, zeros)
        unmasked = jnp.maximum(real, 0) // CHUNK
        carry = lax.fori_loop(0, unmasked, functools.partial(step, masked=False), carry)
        carry = lax.fori_loop(unmasked, chunks, functools.partial(step, masked=True), carry)
        top, total, hit, plain = carry
        highest = jnp.max(top, axis=0, keepdims=True)
        out_ref[0:1, :] = highest
        out_ref[1:2, :] = jnp.sum(total * jnp.exp(top - highest), axis=0, keepdims=True)
        out_ref[2:3, :] = jnp.sum(hit, axis=0, keepdims=True)
        out_ref[3:4, :] = jnp.sum(plain, axis=0, keepdims=True)
        out_ref[4:8, :] = jnp.zeros((4, count), jnp.float32)

    return pl.pallas_call(
        body,
        out_shape=jax.ShapeDtypeStruct((8, count), jnp.float32),
        in_specs=[pl.BlockSpec(memory_space=pltpu.SMEM)] + [whole_block()] * 3,
        out_specs=whole_block(),
        compiler_params=pltpu.CompilerParams(vmem_limit_bytes=VMEM_BYTES),
        cost_estimate=pl.CostEstimate(
            flops=2 * table_low.size * count,
            bytes_accessed=2 * table_low.size,
            transcendentals=table_low.shape[0] * count,
        ),
    )(first, head_in, table_low, targets)


def logit_grad(values, columns, norms, targets, scale):
    drop = jnp.where(
        columns == targets,
        scale * (1.0 - SMOOTHING + SMOOTHING / V_REAL),
        scale * (SMOOTHING / V_REAL),
    )
    return jnp.exp(values - norms) - drop


def head_back(head_in, table_low, targets, norms, first, rows, scale):
    count, width = head_in.shape
    chunks = table_low.shape[0] // CHUNK

    def body(first_ref, head_ref, table_ref, target_ref, norm_ref, out_ref):
        head = head_ref[...]
        target = target_ref[...]
        norm = norm_ref[...]
        real = jnp.minimum(rows, V_REAL - first_ref[0])
        out_ref[...] = jnp.zeros_like(out_ref)

        def step(index, carry, masked):
            begin = pl.multiple_of(index * CHUNK, CHUNK)
            part = table_ref[pl.ds(begin, CHUNK), :]
            local = lax.broadcasted_iota(jnp.int32, (1, CHUNK), 1) + begin
            grad = logit_grad(
                dot_second(head, part), local + first_ref[0], norm, target, scale
            )
            if masked:
                grad = jnp.where(local < real, grad, 0.0)
            out_ref[...] += dot_plain(grad.astype(jnp.bfloat16), part)
            return carry

        unmasked = jnp.maximum(real, 0) // CHUNK
        lax.fori_loop(0, unmasked, functools.partial(step, masked=False), 0)
        lax.fori_loop(unmasked, chunks, functools.partial(step, masked=True), 0)

    return pl.pallas_call(
        body,
        out_shape=jax.ShapeDtypeStruct((count, width), jnp.float32),
        in_specs=[pl.BlockSpec(memory_space=pltpu.SMEM)] + [whole_block()] * 4,
        out_specs=whole_block(),
        compiler_params=pltpu.CompilerParams(vmem_limit_bytes=VMEM_BYTES),
        cost_estimate=pl.CostEstimate(
            flops=4 * table_low.size * count,
            bytes_accessed=2 * table_low.size,
            transcendentals=table_low.shape[0] * count,
        ),
    )(first, head_in, table_low, targets, norms)


def table_part(earlier, head_all, table_low, targets, norms, first, rows, scale, start, stop):
    count, width = head_all.shape
    block = min(512, count)

    def body(first_ref, head_ref, table_ref, target_ref, norm_ref, *refs):
        out_ref, done_ref = refs[-2:]
        done_ref[...] = jnp.zeros_like(done_ref)
        begin = (pl.program_id(0) + start) * PIECE
        real = jnp.minimum(rows, V_REAL - first_ref[0])
        part = table_ref[...]
        local = lax.broadcasted_iota(jnp.int32, (PIECE, 1), 0) + begin
        columns = local + first_ref[0]

        def total_of_blocks(masked):
            total = jnp.zeros((PIECE, width), jnp.float32)
            for place in range(0, count, block):
                span = slice(place, place + block)
                head = head_ref[span, :]
                grad = logit_grad(
                    dot_second(part, head), columns, norm_ref[:, span], target_ref[:, span], scale
                )
                if masked:
                    grad = jnp.where(local < real, grad, 0.0)
                total = total + dot_plain(grad.astype(jnp.bfloat16), head)
            return total

        @pl.when(begin + PIECE <= real)
        def _():
            out_ref[...] = total_of_blocks(False)

        @pl.when(begin + PIECE > real)
        def _():
            out_ref[...] = total_of_blocks(True)

    args = [first, head_all, table_low, targets, norms]
    specs = [
        pl.BlockSpec(memory_space=pltpu.SMEM),
        whole_block(),
        pl.BlockSpec((PIECE, width), lambda i: (i + start, 0)),
        whole_block(),
        whole_block(),
    ]
    aliases = {}
    if earlier is not None:
        aliases = {len(args): 0}
        args.append(earlier)
        specs.append(pl.BlockSpec(memory_space=pl.ANY))
    size = (stop - start) * PIECE
    return pl.pallas_call(
        body,
        grid=(stop - start,),
        out_shape=[
            jax.ShapeDtypeStruct(table_low.shape, jnp.float32),
            jax.ShapeDtypeStruct((8, 128), jnp.float32),
        ],
        in_specs=specs,
        out_specs=[pl.BlockSpec((PIECE, width), lambda i: (i + start, 0)), whole_block()],
        input_output_aliases=aliases,
        compiler_params=pltpu.CompilerParams(vmem_limit_bytes=VMEM_BYTES),
        cost_estimate=pl.CostEstimate(
            flops=4 * size * width * count,
            bytes_accessed=6 * size * width,
            transcendentals=size * count,
        ),
    )(*args)


def token_lists(ids, first, rows, cap):
    local = ids - first
    mine = (local >= 0) & (local < rows)
    tokens = jnp.arange(ids.shape[1], dtype=jnp.int32)
    before = (tokens[:, None] < tokens[None, :]).astype(jnp.float32)
    slot = dot_plain(mine.astype(jnp.float32), before).astype(jnp.int32)
    slots = jnp.arange(cap, dtype=jnp.int32)
    hot = (slot[:, None, :] == slots[None, :, None]) & mine[:, None, :]
    row = jnp.sum(jnp.where(hot, local[:, None, :], 0), axis=2)
    token = jnp.sum(jnp.where(hot, tokens[None, None, :], 0), axis=2)
    return (jnp.sum(mine.astype(jnp.int32), axis=1), row, token)


def add_rows(table_grad, held, other, counts, row_list, token_list, gradients, weight_sums, dp_count):
    padded, width = table_grad.shape
    dp_index, outer, core = places()
    here = jnp.stack([dp_index, outer, core]).astype(jnp.int32)
    outer_count = lax.axis_size("vocab") // 2
    sequences = counts.shape[0]
    cap = row_list.shape[1]
    chunks = padded // CHUNK

    def body(here_ref, count_ref, row_ref, token_ref, grad_in_ref, held_ref, other_ref, sums_ref, *refs):
        small_refs = refs[: len(gradients)]
        grad_out_ref, total_ref, grad_ref, rows_ref, in_sems, out_sems = refs[len(gradients) :]

        def in_copy(index):
            span = pl.ds(pl.multiple_of(index * CHUNK, CHUNK), CHUNK)
            return pltpu.make_async_copy(grad_in_ref.at[span], grad_ref.at[span], in_sems.at[index])

        def out_copy(index):
            span = pl.ds(pl.multiple_of(index * CHUNK, CHUNK), CHUNK)
            return pltpu.make_async_copy(grad_ref.at[span], grad_out_ref.at[span], out_sems.at[index])

        def start_in(index, carry):
            in_copy(index).start()
            return carry

        def wait_in(index, carry):
            in_copy(index).wait()
            return carry

        lax.fori_loop(0, chunks, start_in, 0)
        terms = [total_of(ref[...] * ref[...]) for ref in small_refs]
        lax.fori_loop(0, chunks, wait_in, 0)

        def sequence(index, carry):
            dp_place = (index // 2) // outer_count
            outer_place = (index // 2) % outer_count
            block = (dp_place ^ here_ref[0]) * outer_count + (outer_place ^ here_ref[1])

            @pl.when(index % 2 == here_ref[2])
            def _():
                rows_ref[...] = held_ref[block].astype(jnp.float32)

            @pl.when(index % 2 != here_ref[2])
            def _():
                rows_ref[...] = other_ref[block].astype(jnp.float32)

            def one(slot, carry):
                row = row_ref[index * cap + slot]
                token = token_ref[index * cap + slot]
                grad_ref[pl.ds(row, 1), :] += rows_ref[pl.ds(token, 1), :]
                return carry

            lax.fori_loop(0, count_ref[index], one, 0)
            return carry

        lax.fori_loop(0, sequences, sequence, 0)

        def square(index, acc):
            span = pl.ds(pl.multiple_of(index * CHUNK, CHUNK), CHUNK)
            out_copy(index).start()
            value = grad_ref[span, :]
            return acc + fold_rows(value * value)

        acc = lax.fori_loop(0, chunks, square, jnp.zeros((8, width), jnp.float32))
        clip = total_of(acc) / dp_count
        for term in terms:
            clip = clip + term
        total_ref[...] = sums_ref[...] + tile_of([clip])

        def wait_out(index, carry):
            out_copy(index).wait()
            return carry

        lax.fori_loop(0, chunks, wait_out, 0)

    smem = pl.BlockSpec(memory_space=pltpu.SMEM)
    any_space = pl.BlockSpec(memory_space=pl.ANY)
    return pl.pallas_call(
        body,
        out_shape=[
            jax.ShapeDtypeStruct(table_grad.shape, jnp.float32),
            jax.ShapeDtypeStruct((8, 128), jnp.float32),
        ],
        in_specs=[smem, smem, smem, smem, any_space, whole_block(), whole_block(), whole_block()]
        + [whole_block() for _ in gradients],
        out_specs=[any_space, whole_block()],
        scratch_shapes=[
            pltpu.VMEM((padded, width), jnp.float32),
            pltpu.VMEM(held.shape[1:], jnp.float32),
            pltpu.SemaphoreType.DMA((chunks,)),
            pltpu.SemaphoreType.DMA((chunks,)),
        ],
        input_output_aliases={4: 0},
        compiler_params=pltpu.CompilerParams(vmem_limit_bytes=VMEM_BYTES),
        cost_estimate=pl.CostEstimate(
            flops=2 * table_grad.size, bytes_accessed=8 * table_grad.size, transcendentals=0
        ),
    )(here, counts, row_list.reshape(-1), token_list.reshape(-1), table_grad, held, other, weight_sums, *gradients)


def moments_of(gradient, first, second, factor):
    clipped = gradient * factor
    first = BETA_ONE * first + (1.0 - BETA_ONE) * clipped
    second = BETA_TWO * second + (1.0 - BETA_TWO) * clipped * clipped
    return (first, second)


def update_of(weight, first, second):
    scaled = second * (1.0 / (1.0 - BETA_TWO**STEP))
    root = scaled * lax.rsqrt(scaled) + ADAM_EPS
    return first * (1.0 / (1.0 - BETA_ONE**STEP)) / root + DECAY * weight


def clip_factor(sums):
    return jnp.minimum(1.0, CLIP_AT / jnp.sqrt(sums[0:1, 0:1]))


def table_tile(rows, dp_count):
    return -(-rows // (3 * dp_count * 8)) * 8


def update_norms(sums, smalls, table_set, dp_count):
    weight, gradient, first, second = table_set
    rows, width = weight.shape
    tile = table_tile(rows, dp_count)
    here = lax.axis_index("dp").astype(jnp.int32).reshape(1)
    number = len(smalls)

    def body(here_ref, sums_ref, w_ref, g_ref, m_ref, s_ref, *refs):
        small_refs = refs[: 4 * number]
        out_refs = refs[4 * number : 7 * number]
        norm_ref, acc_ref, term_ref = refs[7 * number :]
        step = pl.program_id(0)
        factor = clip_factor(sums_ref[...])

        @pl.when(step == 0)
        def _():
            acc_ref[...] = jnp.zeros_like(acc_ref)
            terms = [None]
            for place in range(number):
                w, g, m, s = (ref[...] for ref in small_refs[4 * place : 4 * place + 4])
                m, s = moments_of(g, m, s, factor)
                u = update_of(w, m, s)
                out_refs[3 * place][...] = m
                out_refs[3 * place + 1][...] = s
                out_refs[3 * place + 2][...] = u
                terms.append(total_of(u * u))
            term_ref[...] = tile_of(terms)

        row = (here_ref[0] * 3 + step) * tile + lax.broadcasted_iota(jnp.int32, (tile, 1), 0)
        m, s = moments_of(g_ref[...], m_ref[...], s_ref[...], factor)
        u = jnp.where(row < rows, update_of(w_ref[...], m, s), 0.0)
        acc_ref[...] += fold_rows(u * u)

        @pl.when(step == 2)
        def _():
            norm_ref[...] = term_ref[...] + tile_of([None] * (number + 1) + [total_of(acc_ref[...])])

    block = pl.BlockSpec((tile, width), lambda i, here_ref: (here_ref[0] * 3 + i, 0))
    flat = [value for group in smalls for value in group]
    outs = [jax.ShapeDtypeStruct(group[0].shape, jnp.float32) for group in smalls for _ in range(3)]
    made = pl.pallas_call(
        body,
        grid_spec=pltpu.PrefetchScalarGridSpec(
            num_scalar_prefetch=1,
            grid=(3,),
            in_specs=[whole_block()] + [block] * 4 + [whole_block() for _ in flat],
            out_specs=[whole_block() for _ in outs] + [whole_block()],
            scratch_shapes=[pltpu.VMEM((8, width), jnp.float32), pltpu.VMEM((8, 128), jnp.float32)],
        ),
        out_shape=outs + [jax.ShapeDtypeStruct((8, 128), jnp.float32)],
        compiler_params=pltpu.CompilerParams(vmem_limit_bytes=VMEM_BYTES),
        cost_estimate=pl.CostEstimate(
            flops=20 * tile * 3 * width, bytes_accessed=16 * tile * 3 * width, transcendentals=2 * tile * 3 * width
        ),
    )(here, sums, weight, gradient, first, second, *flat)
    return ([made[3 * place : 3 * place + 3] for place in range(number)], made[-1])


def write_updates(sums, norms, smalls, table_set):
    weight, gradient, first, second = table_set
    rows, width = weight.shape
    tile = table_tile(rows, lax.axis_size("dp"))
    steps = -(-rows // tile)
    number = len(smalls)

    def body(sums_ref, norms_ref, w_ref, g_ref, m_ref, s_ref, *refs):
        small_refs = refs[: 2 * number]
        out_w, out_m, out_s = refs[2 * number : 2 * number + 3]
        small_outs = refs[2 * number + 3 :]
        sums = sums_ref[...]
        pace = RATE * jnp.sqrt(sums) / jnp.sqrt(norms_ref[...])

        @pl.when(pl.program_id(0) == 0)
        def _():
            for place in range(number):
                w, u = (ref[...] for ref in small_refs[2 * place : 2 * place + 2])
                small_outs[place][...] = w - pace[0:1, place + 1 : place + 2] * u

        m, s = moments_of(g_ref[...], m_ref[...], s_ref[...], clip_factor(sums))
        w = w_ref[...]
        out_m[...] = m
        out_s[...] = s
        out_w[...] = w - pace[0:1, number + 1 : number + 2] * update_of(w, m, s)

    block = pl.BlockSpec((tile, width), lambda i: (i, 0))
    flat = [value for group in smalls for value in group]
    outs = [jax.ShapeDtypeStruct(weight.shape, jnp.float32)] * 3
    outs += [jax.ShapeDtypeStruct(group[0].shape, jnp.float32) for group in smalls]
    return pl.pallas_call(
        body,
        grid=(steps,),
        out_shape=outs,
        in_specs=[whole_block(), whole_block()] + [block] * 4 + [whole_block() for _ in flat],
        out_specs=[block] * 3 + [whole_block() for _ in smalls],
        compiler_params=pltpu.CompilerParams(vmem_limit_bytes=VMEM_BYTES),
        cost_estimate=pl.CostEstimate(
            flops=20 * weight.size, bytes_accessed=28 * weight.size, transcendentals=2 * weight.size
        ),
    )(sums, norms, weight, gradient, first, second, *flat)


def pick_half(value, index, axis):
    return lax.dynamic_index_in_dim(value, index, axis, keepdims=False)


class OuterSum:
    def __init__(self, held):
        self.held = held
        self.step = 1

    def advance(self, slots):
        held = self.held
        if held.shape[0] > 1:
            _, outer, _ = places()
            pairs = held.reshape((-1, 2) + held.shape[1:])
            own = (outer // self.step) % 2
            out = slots.open(pick_half(pairs, 1 - own, 1).astype(jnp.bfloat16))
            self.held = pick_half(pairs, own, 1) + swap_outer(out, self.step).astype(jnp.float32)
            self.step *= 2

    def finish(self, slots):
        while self.held.shape[0] > 1:
            self.advance(slots)
        return self.held.reshape(self.held.shape[1:])


def scatter_core(keep, sent, slots):
    held = keep + swap_core(slots.open(sent)).astype(jnp.float32)
    return held.reshape((4, -1) + keep.shape[1:])


def scatter_first(held, slots):
    dp_index, _, _ = places()
    half = held.shape[1] // 2
    low = jnp.bfloat16
    own, one, two, three = [pick_half(held, dp_index ^ step, 0) for step in range(4)]
    three = slots.open(three.astype(low))
    into_two = swap_dp(three[:half], 1)
    into_one = swap_dp(three[half:], 2)
    one = jnp.concatenate(
        [one[:half].astype(low), (one[half:] + into_one.astype(jnp.float32)).astype(low)], axis=0
    )
    two = jnp.concatenate(
        [(two[:half] + into_two.astype(jnp.float32)).astype(low), two[half:].astype(low)], axis=0
    )
    return (own, one, two)


def scatter_second(parts, slots):
    own, one, two = parts
    one, two = slots.open((one, two))
    return own + (swap_dp(one, 1).astype(jnp.float32) + swap_dp(two, 2).astype(jnp.float32))


def shards(
    token_ids,
    pick_rows,
    target_ids,
    attn_in,
    attn_out,
    mlp_in,
    mlp_out,
    positions,
    vectors,
    table,
    *moments,
):
    low = jnp.bfloat16
    dp_index, outer, core = places()
    dp_count = lax.axis_size("dp")
    shard_count = lax.axis_size("vocab")
    device_count = dp_count * shard_count
    outer_count = shard_count // 2
    vocab_rows, width = table.shape
    seq_len = token_ids.shape[1]
    pick_count = pick_rows.shape[1]
    vocab_start = lax.axis_index("vocab") * vocab_rows

    slots = Slots()
    unit_rows = attn_in.shape[0]
    small_count = positions.size + vectors.size
    small_width = -(-small_count // (unit_rows * 128)) * 128
    small = jnp.concatenate([positions.astype(low).reshape(-1), vectors.astype(low).reshape(-1)])
    small = jnp.pad(small, (0, unit_rows * small_width - small_count))
    first = OuterGather(
        jnp.concatenate(
            [attn_in.astype(low), attn_out.astype(low), small.reshape(unit_rows, small_width)], axis=1
        )
    )
    up = OuterGather(mlp_in.astype(low))
    down = OuterGather(mlp_out.astype(low))
    small_masters = (attn_in, attn_out, mlp_in, mlp_out, positions, vectors)

    first.advance(slots)
    packed_ids = jnp.concatenate([token_ids, target_ids], axis=1)
    ids_pair = jnp.stack(xor_order([packed_ids, swap_core(packed_ids)], core))
    slots.close(first.held, ids_pair)

    first.finish(slots)
    ids_parts = outer_parts(slots.open(ids_pair))
    group_packed = jnp.concatenate(xor_order(ids_parts, outer), axis=0).reshape(shard_count, -1)
    group_ids = group_packed[:, :seq_len]
    group_targets = group_packed[:, seq_len:]
    slots.close(first.held, group_packed)

    first_ring = ring_first(first.held, slots)
    up.advance(slots)
    table_low, weight_sums = prepare_table(slots.open(table), small_masters, dp_count)
    slots.close(first_ring, up.held, table_low)

    first_held = ring_second(first_ring, slots)
    up.finish(slots)
    slots.close(first_held, up.held)

    up_ring = ring_first(up.held, slots)
    first_other = swap_core(slots.open(first_held))
    down.advance(slots)
    group_local = slots.open(group_ids) - vocab_start
    mine = (group_local >= 0) & (group_local < vocab_rows)
    served = jnp.take(table, jnp.where(mine, group_local, 0).reshape(-1), axis=0)
    served = jnp.where(mine.reshape(-1)[:, None], served, 0.0).astype(low)
    served = served.reshape(outer_count, 2, seq_len, width)
    slots.close(up_ring, first_other, down.held, served)

    up_held = ring_second(up_ring, slots)
    down.finish(slots)
    served = slots.open(served)
    embedded = pick_half(served, core, 1) + swap_core(pick_half(served, 1 - core, 1))
    embedded = OuterSum(embedded.astype(jnp.float32))
    w_qkv, w_proj, small_all = place_blocks(
        slots.open(first_held), first_other, (3 * width, width, small_width)
    )
    slots.close(up_held, down.held, embedded.held, w_qkv)

    down_ring = ring_first(down.held, slots)
    up_other = swap_core(slots.open(up_held))
    embedded = embedded.finish(slots)
    w_qkv = w_qkv.reshape(width, 3 * width)
    w_proj = w_proj.reshape(width, width)
    small_all = small_all.reshape(device_count, -1)
    pos_low = small_all[:, : positions.size].reshape(seq_len, width)
    vec_low = small_all[:, positions.size : small_count].reshape((device_count,) + vectors.shape)
    vec_rows = jnp.moveaxis(vec_low, 0, 1).reshape(vectors.shape[0], width).astype(jnp.float32)
    resid_in, normed_one, packed, attended, resid_mid, normed_two = attention_forward(
        embedded, pos_low, vec_rows, w_qkv, w_proj
    )
    slots.close(down_ring, up_other, embedded, vec_rows)

    down_held = ring_second(down_ring, slots)
    w_up = place_blocks(slots.open(up_held), up_other, (mlp_in.shape[1],))[0].reshape(width, -1)
    slots.close(down_held, w_up, normed_two)

    down_other = swap_core(slots.open(down_held))
    hidden_pre, hidden_act = hidden_forward(slots.open(normed_two), vec_rows, w_up)
    w_down = place_blocks(down_held, down_other, (width,))[0].reshape(-1, width)
    picks = pick_rows.reshape(-1, 1)
    resid_out, picked = output_forward(hidden_act, w_down, resid_mid, vec_rows, picks)

    same_core = jnp.stack(outer_parts(picked))
    ordered = jnp.stack(xor_order([same_core[step] for step in range(outer_count)], outer))
    head_in = jnp.stack(xor_order([ordered, swap_core(ordered)], core), axis=1)
    head_in = head_in.reshape(-1, width)
    first_column = vocab_start.astype(jnp.int32).reshape(1)
    flat_targets = group_targets.reshape(1, -1)
    stats = gather_vocab(head_stats(head_in, table_low, flat_targets, first_column, vocab_rows))
    stats = stats.reshape(shard_count, 8, -1)
    row_top = jnp.max(stats[:, 0], axis=0)
    exp_total = jnp.sum(stats[:, 1] * jnp.exp(stats[:, 0] - row_top[None]), axis=0)
    target_logit = jnp.sum(stats[:, 2], axis=0)
    logit_total = jnp.sum(stats[:, 3], axis=0)
    log_norm = row_top + jnp.log(exp_total)
    row_loss = (1.0 - SMOOTHING) * (log_norm - target_logit) + SMOOTHING * (
        log_norm - logit_total / V_REAL
    )
    token_count = device_count * pick_count

    partial = head_back(
        head_in,
        table_low,
        flat_targets.reshape(-1, 1),
        (log_norm + math.log(token_count)).reshape(-1, 1),
        first_column,
        vocab_rows,
        1.0 / token_count,
    )
    partial = partial.reshape(outer_count, 2, pick_count, width)
    held = pick_half(partial, core, 1) + swap_core(
        pick_half(partial, 1 - core, 1).astype(low)
    ).astype(jnp.float32)
    terms = [pick_half(held, outer, 0)]
    for step in range(1, outer_count):
        out = pick_half(held, outer ^ step, 0).astype(low)
        terms.append(swap_outer(out, step).astype(jnp.float32))
    picked_grad = tree_sum(terms)
    ring = ring_second(ring_first(same_core, Slots()), Slots())
    head_all = place_blocks(ring, swap_core(ring), (width,))[0].reshape(-1, width)
    rows_stats = gather_dp(jnp.stack([log_norm, row_loss]))
    norm_all = (rows_stats[:, 0] + math.log(token_count)).reshape(1, -1)
    loss = jnp.sum(rows_stats[:, 1]) / token_count
    packed_all = gather_dp(behind(group_packed, same_core)).reshape(device_count, -1)
    targets_all = packed_all[:, seq_len:].reshape(1, -1)
    counts, row_list, token_list = token_lists(
        packed_all[:, :seq_len], vocab_start, vocab_rows, 4 * seq_len // shard_count
    )

    slots = Slots()
    blocks = (-1, unit_rows)
    unit_choosers = choosers(width, unit_rows, core)
    grad_top, grad_branch, down_keep, down_sent, vec_down = output_backward(
        picked_grad, picks, resid_out, vec_rows, hidden_act, choosers(width, mlp_out.shape[0], core)
    )
    down_shape = (-1,) + mlp_out.shape
    down = scatter_core(down_keep.reshape(down_shape), down_sent.reshape(down_shape), slots)
    grad_pre, up_keep, up_sent, vec_up = hidden_backward(
        grad_branch, w_down, hidden_pre, normed_two, unit_choosers
    )
    slots.close(down, grad_pre)

    down = scatter_first(down, slots)
    up_shape = blocks + up_keep.shape[1:]
    up = scatter_core(up_keep.reshape(up_shape), up_sent.reshape(up_shape), slots)
    grad_mid, grad_mixed, proj_keep, proj_sent, vec_middle = middle_backward(
        slots.open(grad_pre),
        w_up,
        grad_top,
        resid_mid,
        attended,
        w_proj,
        vec_rows,
        unit_choosers,
    )
    slots.close(down, up, grad_mid)

    down = OuterSum(scatter_second(down, slots))
    grad_in, grad_rows, first_keep, first_sent, vec_first = attention_backward(
        grad_mixed,
        slots.open(grad_mid),
        packed,
        resid_in,
        normed_one,
        w_qkv,
        vec_rows,
        unit_choosers,
        proj_keep,
        proj_sent,
        small_width,
    )
    slots.close(down.held, grad_in)

    vec_grad = jnp.concatenate(
        [
            vec_first[0:2],
            vec_middle[0:2],
            vec_down[0:2],
            vec_first[2:4],
            vec_middle[2:3],
            vec_down[2:3],
            vec_up[0:4],
        ],
        axis=0,
    )
    vec_width = vectors.shape[1]
    vec_blocks = jnp.moveaxis(vec_grad.reshape(-1, device_count, vec_width), 1, 0)
    small_grad = jnp.concatenate(
        [grad_in.reshape(device_count, -1), vec_blocks.reshape(device_count, -1)], axis=1
    )
    small_grad = jnp.pad(small_grad, ((0, 0), (0, unit_rows * small_width - small_count)))
    small_grad = small_grad.reshape(-1, 2, unit_rows, small_width)
    first_keep = first_keep.reshape(blocks + first_keep.shape[1:])
    first_keep = first_keep.at[:, :, 4 * width :].set(pick_half(small_grad, core, 1))
    first_sent = first_sent.reshape(blocks + first_sent.shape[1:])
    first_sent = first_sent.at[:, :, 4 * width :].set(pick_half(small_grad, 1 - core, 1).astype(low))

    pieces = table_low.shape[0] // PIECE
    parts = 5 if pieces % 5 == 0 else 1

    def head_part(earlier, part, mark):
        if part >= parts:
            return (earlier, mark)
        return table_part(
            earlier,
            head_all,
            table_low,
            targets_all,
            behind(norm_all, mark),
            first_column,
            vocab_rows,
            1.0 / token_count,
            part * pieces // parts,
            (part + 1) * pieces // parts,
        )

    up = scatter_first(up, slots)
    down.advance(slots)
    rows = OuterGather(slots.open(grad_rows))
    slots.close(up, down.held, first_sent)

    up = OuterSum(scatter_second(up, slots))
    first = scatter_core(first_keep, first_sent, slots)
    rows.advance(slots)
    down_own = down.finish(slots)
    table_grad, mark = head_part(None, 0, slots.last)
    slots.close(up.held, first, rows.held, down_own, mark)

    first = scatter_first(first, slots)
    rows_outer = rows.finish(slots)
    up.advance(slots)
    table_grad, mark = head_part(table_grad, 1, slots.last)
    slots.close(first, rows_outer, up.held, mark)

    first = OuterSum(scatter_second(first, slots))
    up_own = up.finish(slots)
    table_grad, mark = head_part(table_grad, 2, slots.last)
    slots.close(first.held, up_own, mark)

    rows_ring = ring_first(rows_outer, slots)
    first.advance(slots)
    table_grad, mark = head_part(table_grad, 3, slots.last)
    slots.close(rows_ring, first.held, mark)

    rows_held = ring_second(rows_ring, slots)
    first_own = first.finish(slots)
    table_grad, mark = head_part(table_grad, 4, slots.last)
    slots.close(rows_held, first_own, mark)

    rows_other = swap_core(slots.open(rows_held))
    small_own = first_own[:, 4 * width :].reshape(-1)
    gradients = (
        first_own[:, : 3 * width],
        first_own[:, 3 * width : 4 * width],
        up_own,
        down_own,
        small_own[: positions.size].reshape(positions.shape),
        small_own[positions.size : small_count].reshape(vectors.shape),
    )
    table_grad, sums = add_rows(
        table_grad, rows_held, rows_other, counts, row_list, token_list, gradients, weight_sums, dp_count
    )
    sums = sum_all(sums)
    grad_norm = jnp.sqrt(sums[0, 0])
    firsts, seconds = moments[:7], moments[7:]
    smalls = list(zip(small_masters, gradients, firsts, seconds))
    table_set = (table, table_grad, firsts[6], seconds[6])
    made, norms = update_norms(sums, smalls, table_set, dp_count)
    norms = sum_all(norms)
    ratios = jnp.sqrt(sums[0, 1:8]) / jnp.sqrt(norms[0, 1:8])
    written = write_updates(
        sums, norms, [(weight, group[2]) for weight, group in zip(small_masters, made)], table_set
    )
    new_weights = list(written[3:]) + [written[0]]
    new_firsts = [group[0] for group in made] + [written[1]]
    new_seconds = [group[1] for group in made] + [written[2]]
    return (loss, grad_norm, ratios, *new_weights, *new_firsts, *new_seconds)


def solution(mesh):
    rows = P(("dp", "vocab"), None)
    weights = (rows, rows, rows, rows, rows, P(None, ("dp", "vocab")), P("vocab", None))
    return jax.shard_map(
        shards,
        mesh=mesh,
        in_specs=(rows, rows, rows) + weights * 3,
        out_specs=(P(), P(), P()) + weights * 3,
        check_vma=False,
    )
```

```python
import functools
import math

import jax
import jax.numpy as jnp
from jax import lax
from jax.experimental import pallas as pl
from jax.experimental.pallas import tpu as pltpu
from jax.sharding import PartitionSpec as P

HD = 64
V_REAL = 50257
STEP = 5


LN_EPS = 1e-05
SMOOTHING = 0.1
BETA_ONE = 0.9
BETA_TWO = 0.999
ADAM_EPS = 1e-12
DECAY = 0.01
RATE = 0.3
CLIP_AT = 0.01
MASKED = -1e30
CHUNK = 1280
PIECE = 640
VMEM_BYTES = 58 * 2**20


def layer_norm(inputs, gain, shift):
    centre = jnp.mean(inputs, axis=-1, keepdims=True)
    centred = inputs - centre
    spread = jnp.mean(centred * centred, axis=-1, keepdims=True)
    return centred * lax.rsqrt(spread + LN_EPS) * gain + shift


def gelu_tanh(inputs):
    return (
        0.5
        * inputs
        * (1.0 + jnp.tanh(0.7978845608028654 * (inputs + 0.044715 * inputs * inputs * inputs)))
    )


def dot_plain(left_op, right_op):
    return jnp.dot(left_op, right_op, preferred_element_type=jnp.float32)


def dot_first(left_op, right_op):
    return lax.dot_general(
        left_op, right_op, (((0,), (0,)), ((), ())), preferred_element_type=jnp.float32
    )


def dot_second(left_op, right_op):
    return lax.dot_general(
        left_op, right_op, (((1,), (1,)), ((), ())), preferred_element_type=jnp.float32
    )


def params():
    return pltpu.CompilerParams(vmem_limit_bytes=VMEM_BYTES)


def cost(flops, bytes_accessed):
    return pl.CostEstimate(
        flops=int(flops), bytes_accessed=int(bytes_accessed), transcendentals=0
    )


def whole_block():
    return pl.BlockSpec(memory_space=pltpu.VMEM)


def shape_of(shape, dtype):
    return jax.ShapeDtypeStruct(tuple(shape), dtype)


def causal_scores(queries, keys, causal):
    return jnp.where(causal, dot_second(queries, keys) * HD ** (-0.5), MASKED)


def causal_mask(count):
    query = lax.broadcasted_iota(jnp.int32, (count, count), 0)
    key = lax.broadcasted_iota(jnp.int32, (count, count), 1)
    return key <= query


def head_span(head):
    return slice(head * HD, (head + 1) * HD)


def attention_forward(embedded, positions, vec_rows, w_qkv, w_proj, chooser):
    count, width = embedded.shape
    low = jnp.bfloat16

    half = width // 2

    def body(
        e_ref, p_ref, v_ref, qkv_ref, proj_ref, c_ref, x0_ref, packed_ref, x1_ref, h2_ref, own_ref, other_ref, o_ref
    ):
        x0 = e_ref[...] + p_ref[...].astype(jnp.float32)
        x0_ref[...] = x0
        h1 = layer_norm(x0, v_ref[0:1, :], v_ref[1:2, :]).astype(low)
        parts = []
        for place, bias in enumerate((6, None, 7)):
            span = slice(place * width, (place + 1) * width)
            part = dot_plain(h1, qkv_ref[:, span])
            if bias is not None:
                part = part + v_ref[bias : bias + 1, :]
            parts.append(part.astype(low))
            packed_ref[:, span] = parts[-1]
        queries, keys, values = parts
        causal = causal_mask(count)
        for head in range(0, width // HD, 2):
            mixed = []
            for one in (head, head + 1):
                span = head_span(one)
                scores = causal_scores(queries[:, span], keys[:, span], causal)
                grown = jnp.exp(scores - jnp.max(scores, axis=-1, keepdims=True))
                probs = (grown / jnp.sum(grown, axis=-1, keepdims=True)).astype(low)
                mixed.append(dot_plain(probs, values[:, span]))
            o_ref[:, head * HD : (head + 2) * HD] = jnp.concatenate(mixed, axis=1).astype(low)
        x1 = x0 + dot_plain(o_ref[...], proj_ref[...]) + v_ref[8:9, :]
        x1_ref[...] = x1
        h2 = layer_norm(x1, v_ref[2:3, :], v_ref[3:4, :]).astype(low)
        h2_ref[...] = h2
        for place, value in enumerate((h1, o_ref[...], h2)):
            span = slice(place * half, (place + 1) * half)
            own_ref[:, span] = dot_plain(value, c_ref[0]).astype(low)
            other_ref[:, span] = dot_plain(value, c_ref[1]).astype(low)

    shape = (count, width)
    return pl.pallas_call(
        body,
        out_shape=[
            shape_of(shape, jnp.float32),
            shape_of((count, 3 * width), low),
            shape_of(shape, jnp.float32),
            shape_of(shape, low),
            shape_of((count, 3 * half), low),
            shape_of((count, 3 * half), low),
        ],
        in_specs=[whole_block()] * 6,
        out_specs=[whole_block()] * 6,
        scratch_shapes=[pltpu.VMEM(shape, low)],
        compiler_params=params(),
        cost_estimate=cost(20 * count * width * width, 8 * width * width),
    )(embedded, positions, vec_rows, w_qkv, w_proj, chooser)


def hidden_forward(normed, vec_rows, w_up, chooser, dp_index):
    count, width = normed.shape
    blocks = len(w_up)
    hidden = blocks * width
    half = width // 2
    low = jnp.bfloat16

    def body(dp_ref, h_ref, v_ref, c_ref, *refs):
        w_refs = refs[:blocks]
        pre_ref, act_ref, own_ref, other_ref = refs[blocks:]
        for place in range(blocks):
            span = slice(place * width, (place + 1) * width)
            pre = dot_plain(h_ref[...], w_refs[place][...]) + v_ref[10 + place : 11 + place, :]
            pre_ref[:, span] = pre
            act_ref[:, span] = gelu_tanh(pre).astype(low)
        for place in range(blocks):
            source = pl.multiple_of((dp_ref[0] ^ place) * width, width)
            part = act_ref[:, pl.ds(source, width)]
            span = slice(place * half, (place + 1) * half)
            own_ref[:, span] = dot_plain(part, c_ref[0]).astype(low)
            other_ref[:, span] = dot_plain(part, c_ref[1]).astype(low)

    return pl.pallas_call(
        body,
        out_shape=[
            shape_of((count, hidden), jnp.float32),
            shape_of((count, hidden), low),
            shape_of((count, hidden // 2), low),
            shape_of((count, hidden // 2), low),
        ],
        in_specs=[pl.BlockSpec(memory_space=pltpu.SMEM)] + [whole_block()] * (3 + blocks),
        out_specs=[whole_block()] * 4,
        compiler_params=params(),
        cost_estimate=cost(3 * count * width * hidden, 2 * width * hidden),
    )(dp_index, normed, vec_rows, chooser, *w_up)


def output_forward(act, w_down, resid_mid, vec_rows, picks):
    count, width = resid_mid.shape
    number = picks.shape[0]

    def body(act_ref, w_ref, x1_ref, v_ref, pick_ref, x2_ref, out_ref):
        x2 = x1_ref[...] + dot_plain(act_ref[...], w_ref[...]) + v_ref[9:10, :]
        x2_ref[...] = x2
        final = layer_norm(x2, v_ref[4:5, :], v_ref[5:6, :]).astype(jnp.bfloat16)
        hot = pick_ref[...] == lax.broadcasted_iota(jnp.int32, (number, count), 1)
        hot = jnp.where(hot, 1.0, 0.0).astype(jnp.bfloat16)
        out_ref[...] = dot_plain(hot, final).astype(jnp.bfloat16)

    return pl.pallas_call(
        body,
        out_shape=[
            shape_of((count, width), jnp.float32),
            shape_of((number, width), jnp.bfloat16),
        ],
        in_specs=[whole_block()] * 5,
        out_specs=[whole_block()] * 2,
        compiler_params=params(),
        cost_estimate=cost(2 * act.size * width, 2 * w_down.size),
    )(act, w_down, resid_mid, vec_rows, picks)


def norm_backward(grad, inputs, gain):
    centred = inputs - jnp.mean(inputs, axis=-1, keepdims=True)
    scale = lax.rsqrt(jnp.mean(centred * centred, axis=-1, keepdims=True) + LN_EPS)
    normed = centred * scale
    scaled = grad * gain
    back = scale * (
        scaled
        - jnp.mean(scaled, axis=-1, keepdims=True)
        - normed * jnp.mean(scaled * normed, axis=-1, keepdims=True)
    )
    return (
        back,
        jnp.sum(grad * normed, axis=0, keepdims=True),
        jnp.sum(grad, axis=0, keepdims=True),
    )


def column_sum(value):
    return jnp.sum(value.astype(jnp.float32), axis=0, keepdims=True)


def choosers(width, rows, core, dp_index=None):
    column = jnp.arange(width, dtype=jnp.int32)
    target = jnp.arange(width // 2, dtype=jnp.int32)
    block = target // rows
    if dp_index is not None:
        per = width // (8 * rows)
        block = ((block // per) ^ dp_index) * per + block % per
    made = []
    for side in (core, 1 - core):
        source = (block * 2 + side) * rows + target % rows
        made.append((column[:, None] == source[None, :]).astype(jnp.bfloat16))
    return jnp.stack(made)


def gradient_blocks(lefts, spans, rights, smalls, name_rows):
    widths = [right[0].shape[1] for right in rights]
    total = sum(widths) + (smalls.shape[2] if smalls is not None else 0)
    arrays = [value for pair in zip(lefts, rights) for group in pair for value in group]
    if smalls is not None:
        arrays.append(smalls)
    number = len(lefts)
    rows = (spans[0][1] - spans[0][0]) // 4
    half = rows // 2
    low = jnp.bfloat16

    def body(*refs):
        in_refs, out_refs = refs[: len(arrays)], refs[len(arrays) :]

        def put(made, span):
            own, one, two, three = [made(place) for place in range(4)]
            out_refs[0][:, span] = own
            out_refs[1][:, span] = one.astype(low)
            out_refs[2][:, span] = two.astype(low)
            out_refs[3][:, span] = one[half:]
            out_refs[4][:, span] = two[:half]
            out_refs[5][:, span] = three[:half].astype(low)
            out_refs[6][:, span] = three[half:].astype(low)

        start = 0
        for index in range(number):
            left_a, left_b, right_a, right_b = in_refs[4 * index : 4 * index + 4]
            columns = slice(*spans[index])
            left = jnp.concatenate([left_a[:, columns], left_b[:, columns]], axis=0)
            for begin in range(0, widths[index], 768):
                stop = min(begin + 768, widths[index])
                right = jnp.concatenate([right_a[:, begin:stop], right_b[:, begin:stop]], axis=0)
                result = dot_first(left, right)
                put(
                    lambda place, result=result: result[place * rows : (place + 1) * rows],
                    slice(start + begin, start + stop),
                )
            start += widths[index]
        if smalls is not None:
            put(lambda place: in_refs[-1][place], slice(start, total))

    out = [shape_of((rows, total), jnp.float32)] + [shape_of((rows, total), low)] * 2
    out += [shape_of((half, total), jnp.float32)] * 2 + [shape_of((half, total), low)] * 2
    flops = sum(4 * left[0].shape[0] * 4 * rows * right[0].shape[1] for left, right in zip(lefts, rights))
    made = pl.pallas_call(
        body,
        out_shape=out,
        in_specs=[whole_block()] * len(arrays),
        out_specs=[whole_block()] * 7,
        compiler_params=params(),
        cost_estimate=cost(flops, 14 * rows * total),
    )(*arrays)
    return [value.reshape(-1, name_rows, total) for value in made]


def split_three(value):
    low = jnp.bfloat16
    first = value.astype(low)
    rest = value - first.astype(jnp.float32)
    second = rest.astype(low)
    return (first, second, (rest - second.astype(jnp.float32)).astype(low))


def pack_stats(top, total):
    lane = lax.broadcasted_iota(jnp.int32, (top.shape[0], 128), 1)
    tile = jnp.zeros((top.shape[0], 128), jnp.float32)
    for place, part in enumerate(split_three(top) + split_three(total)):
        tile = jnp.where(lane == place, part.astype(jnp.float32), tile)
    return tile.astype(jnp.bfloat16)


def unpack_stats(tile):
    wide = tile.astype(jnp.float32)
    return (
        wide[:, 0:1] + (wide[:, 1:2] + wide[:, 2:3]),
        wide[:, 3:4] + (wide[:, 4:5] + wide[:, 5:6]),
    )


def join(one, two):
    top = jnp.maximum(one[1], two[1])
    scale_one, scale_two = jnp.exp(one[1] - top), jnp.exp(two[1] - top)
    return (
        one[0] * scale_one + two[0] * scale_two,
        top,
        one[2] * scale_one + two[2] * scale_two,
    )


def unpack_rows(packed, width):
    top, total = unpack_stats(packed[:, width:])
    return (packed[:, :width].astype(jnp.float32), top, total)


def head_pass(head_in, table_low, here, rows, pick_count):
    count, width = head_in.shape
    chunks = table_low.shape[0] // CHUNK
    groups = count // (2 * pick_count)
    half = count // 2

    def body(here_ref, head_ref, table_ref, own_ref, stat_ref, sent_ref, acc_ref, tops_ref):
        head = head_ref[...]
        real = jnp.minimum(rows, V_REAL - here_ref[0])
        acc_ref[...] = jnp.zeros_like(acc_ref)

        def step(index, carry, masked):
            top, total = carry
            begin = pl.multiple_of(index * CHUNK, CHUNK)
            part = table_ref[pl.ds(begin, CHUNK), :]
            values = dot_second(head, part)
            if masked:
                local = lax.broadcasted_iota(jnp.int32, (1, CHUNK), 1) + begin
                values = jnp.where(local < real, values, MASKED)
            higher = jnp.maximum(top, jnp.max(values, axis=1, keepdims=True))
            grown = jnp.exp(values - higher)
            scale = jnp.exp(top - higher)
            acc_ref[...] = acc_ref[...] * scale + dot_plain(grown.astype(jnp.bfloat16), part)
            return (higher, total * scale + jnp.sum(grown, axis=1, keepdims=True))

        carry = (jnp.full((count, 1), MASKED, jnp.float32), jnp.zeros((count, 1), jnp.float32))
        unmasked = jnp.maximum(real, 0) // CHUNK
        carry = lax.fori_loop(0, unmasked, functools.partial(step, masked=False), carry)
        top, total = lax.fori_loop(unmasked, chunks, functools.partial(step, masked=True), carry)
        lane = lax.broadcasted_iota(jnp.int32, (count, 128), 1)
        tops_ref[...] = jnp.where(lane == 0, top, jnp.where(lane == 1, total, 0.0))
        for group in range(groups):
            own = pl.multiple_of((2 * group + here_ref[1]) * pick_count, pick_count)
            other = pl.multiple_of((2 * group + 1 - here_ref[1]) * pick_count, pick_count)
            span = slice(group * pick_count, (group + 1) * pick_count)
            own_ref[span, :] = acc_ref[pl.ds(own, pick_count), :]
            stat_ref[span, :] = tops_ref[pl.ds(own, pick_count), :]
            sent_ref[span, :width] = acc_ref[pl.ds(other, pick_count), :].astype(jnp.bfloat16)
            stats = tops_ref[pl.ds(other, pick_count), :]
            sent_ref[span, width:] = pack_stats(stats[:, 0:1], stats[:, 1:2])

    return pl.pallas_call(
        body,
        out_shape=[
            shape_of((half, width), jnp.float32),
            shape_of((half, 128), jnp.float32),
            shape_of((half, width + 128), jnp.bfloat16),
        ],
        in_specs=[pl.BlockSpec(memory_space=pltpu.SMEM)] + [whole_block()] * 2,
        out_specs=[whole_block()] * 3,
        scratch_shapes=[pltpu.VMEM((count, width), jnp.float32), pltpu.VMEM((count, 128), jnp.float32)],
        compiler_params=params(),
        cost_estimate=cost(4 * table_low.size * count, 2 * table_low.size),
    )(here, head_in, table_low)


def join_cores(own, stats, received, outer, pick_count):
    half, width = own.shape
    groups = half // pick_count

    def body(outer_ref, own_ref, stat_ref, received_ref, rows_ref, out_stat_ref, *sent_refs):
        for step in range(groups):
            start = pl.multiple_of((outer_ref[0] ^ step) * pick_count, pick_count)
            span = pl.ds(start, pick_count)
            stat = stat_ref[span, :]
            one = (own_ref[span, :], stat[:, 0:1], stat[:, 1:2])
            value, top, total = join(one, unpack_rows(received_ref[span, :], width))
            if step:
                sent_refs[step - 1][:, :width] = value.astype(jnp.bfloat16)
                sent_refs[step - 1][:, width:] = pack_stats(top, total)
            else:
                lane = lax.broadcasted_iota(jnp.int32, (pick_count, 128), 1)
                rows_ref[...] = value
                out_stat_ref[...] = jnp.where(lane == 0, top, jnp.where(lane == 1, total, 0.0))

    return pl.pallas_call(
        body,
        out_shape=[
            shape_of((pick_count, width), jnp.float32),
            shape_of((pick_count, 128), jnp.float32),
        ]
        + [shape_of((pick_count, width + 128), jnp.bfloat16)] * (groups - 1),
        in_specs=[pl.BlockSpec(memory_space=pltpu.SMEM)] + [whole_block()] * 3,
        out_specs=[whole_block()] * (groups + 1),
        compiler_params=params(),
        cost_estimate=cost(4 * own.size, 8 * own.size),
    )(outer, own, stats, received)


def output_backward(rows, stats, received, picked, target_rows, row_sum, picks, resid_out, vec_rows, token_count):
    count, width = resid_out.shape
    number = picks.shape[0]
    low = jnp.bfloat16
    others = len(received)

    def body(rows_ref, stat_ref, *refs):
        received_refs = refs[:others]
        f_ref, t_ref, sum_ref, pick_ref, x_ref, v_ref, dx_ref, dy_ref, vec_ref, norm_ref = refs[others:]
        stat = stat_ref[...]
        value = (rows_ref[...], stat[:, 0:1], stat[:, 1:2])
        for ref in received_refs:
            value = join(value, unpack_rows(ref[...], width))
        mean, top, total = value
        target = t_ref[...]
        final = f_ref[...].astype(jnp.float32)
        norm = top + jnp.log(total)
        hit = jnp.sum(final * target, axis=1, keepdims=True)
        plain = jnp.sum(final * sum_ref[...], axis=1, keepdims=True)
        loss = (1.0 - SMOOTHING) * (norm - hit) + SMOOTHING * (norm - plain / V_REAL)
        lane = lax.broadcasted_iota(jnp.int32, (number, 128), 1)
        norm_ref[...] = jnp.where(lane == 0, norm, jnp.where(lane == 1, loss, 0.0))
        soft = jnp.exp(hit - norm)
        whole = ((soft - (1.0 - SMOOTHING) - SMOOTHING / V_REAL) / token_count).astype(low)
        factor = whole.astype(jnp.float32) - (soft - SMOOTHING / V_REAL) / token_count
        picked_grad = (
            mean * (1.0 / token_count) / total
            - sum_ref[...] * (SMOOTHING / V_REAL / token_count)
            + target * factor
        )
        hot = pick_ref[...] == lax.broadcasted_iota(jnp.int32, (number, count), 1)
        final_grad = lax.dot_general(
            jnp.where(hot, 1.0, 0.0),
            picked_grad,
            (((0,), (0,)), ((), ())),
            precision=lax.Precision.HIGHEST,
            preferred_element_type=jnp.float32,
        )
        back, gain, shift = norm_backward(final_grad, x_ref[...], v_ref[4:5, :])
        dx_ref[...] = back
        dy = back.astype(low)
        dy_ref[...] = dy
        vec_ref[0:1, :] = gain
        vec_ref[1:2, :] = shift
        vec_ref[2:3, :] = column_sum(dy)
        vec_ref[3:8, :] = jnp.zeros((5, width), jnp.float32)

    return pl.pallas_call(
        body,
        out_shape=[
            shape_of((count, width), jnp.float32),
            shape_of((count, width), low),
            shape_of((8, width), jnp.float32),
            shape_of((number, 128), jnp.float32),
        ],
        in_specs=[whole_block()] * (8 + others),
        out_specs=[whole_block()] * 4,
        compiler_params=params(),
        cost_estimate=cost(20 * count * width, 20 * count * width),
    )(rows, stats, *received, picked, target_rows, row_sum, picks, resid_out, vec_rows)


def hidden_backward(dy, w_down, pre):
    count, width = dy.shape
    hidden = pre.shape[1]
    low = jnp.bfloat16

    def body(dy_ref, w_ref, pre_ref, dpre_ref, vec_ref):
        vec_ref[...] = jnp.zeros_like(vec_ref)
        for place in range(hidden // width):
            span = slice(place * width, (place + 1) * width)
            grad = dot_second(dy_ref[...], w_ref[span, :])
            u = pre_ref[:, span]
            bent = jnp.tanh(0.7978845608028654 * (u + 0.044715 * u * u * u))
            slope = 0.5 * (1.0 + bent) + 0.5 * u * (1.0 - bent * bent) * (
                0.7978845608028654 * (1.0 + 3.0 * 0.044715 * u * u)
            )
            dpre = (grad * slope).astype(low)
            dpre_ref[:, span] = dpre
            vec_ref[place : place + 1, :] = column_sum(dpre)

    return pl.pallas_call(
        body,
        out_shape=[shape_of((count, hidden), low), shape_of((8, width), jnp.float32)],
        in_specs=[whole_block()] * 3,
        out_specs=[whole_block()] * 2,
        compiler_params=params(),
        cost_estimate=cost(2 * count * width * hidden, 2 * width * hidden),
    )(dy, w_down, pre)


def middle_backward(dpre, w_up, dx2, x1, w_proj, vec_rows):
    count, width = x1.shape
    low = jnp.bfloat16

    blocks = len(w_up)

    def body(dpre_ref, dx2_ref, x1_ref, proj_ref, v_ref, *refs):
        up_refs = refs[:blocks]
        dx1_ref, da_ref, mixed_ref, vec_ref = refs[blocks:]
        dh2 = jnp.zeros((count, width), jnp.float32)
        for place in range(blocks):
            span = slice(place * width, (place + 1) * width)
            dh2 = dh2 + dot_second(dpre_ref[:, span], up_refs[place][...])
        back, gain, shift = norm_backward(dh2, x1_ref[...], v_ref[2:3, :])
        dx1 = back + dx2_ref[...]
        dx1_ref[...] = dx1
        da = dx1.astype(low)
        da_ref[...] = da
        vec_ref[0:1, :] = gain
        vec_ref[1:2, :] = shift
        vec_ref[2:3, :] = column_sum(da)
        vec_ref[3:8, :] = jnp.zeros((5, width), jnp.float32)
        mixed_ref[...] = dot_second(da, proj_ref[...]).astype(low)

    return pl.pallas_call(
        body,
        out_shape=[
            shape_of((count, width), jnp.float32),
            shape_of((count, width), low),
            shape_of((count, width), low),
            shape_of((8, width), jnp.float32),
        ],
        in_specs=[whole_block()] * (5 + blocks),
        out_specs=[whole_block()] * 4,
        compiler_params=params(),
        cost_estimate=cost(10 * count * width * width, 10 * width * width),
    )(dpre, dx2, x1, w_proj, vec_rows, *w_up)


def attention_backward(mixed, dx1, packed, x0, w_qkv, vec_rows):
    count, width = x0.shape
    low = jnp.bfloat16

    def body(mixed_ref, dx1_ref, packed_ref, x0_ref, qkv_ref, v_ref, dx0_ref, rows_ref, grad_ref, vec_ref):
        causal = causal_mask(count)
        for head in range(0, width // HD, 2):
            sides = ([], [], [])
            for one in (head, head + 1):
                queries = packed_ref[:, one * HD : (one + 1) * HD]
                keys = packed_ref[:, width + one * HD : width + (one + 1) * HD]
                values = packed_ref[:, 2 * width + one * HD : 2 * width + (one + 1) * HD]
                scores = causal_scores(queries, keys, causal)
                grown = jnp.exp(scores - jnp.max(scores, axis=-1, keepdims=True))
                probs = grown / jnp.sum(grown, axis=-1, keepdims=True)
                out_grad = mixed_ref[:, one * HD : (one + 1) * HD]
                grad_p = dot_second(out_grad, values)
                centre = jnp.sum(probs * grad_p, axis=-1, keepdims=True)
                grad_s = (probs * (grad_p - centre)).astype(low)
                sides[0].append(dot_plain(grad_s, keys) * HD ** (-0.5))
                sides[1].append(dot_first(grad_s, queries) * HD ** (-0.5))
                sides[2].append(dot_first(probs.astype(low), out_grad))
            for place, side in enumerate(sides):
                start = place * width + head * HD
                grad_ref[:, start : start + 2 * HD] = jnp.concatenate(side, axis=1).astype(low)
        dh1 = dot_second(grad_ref[...], qkv_ref[...])
        back, gain, shift = norm_backward(dh1, x0_ref[...], v_ref[0:1, :])
        vec_ref[0:1, :] = gain
        vec_ref[1:2, :] = shift
        vec_ref[2:3, :] = column_sum(grad_ref[:, :width])
        vec_ref[3:4, :] = column_sum(grad_ref[:, 2 * width :])
        vec_ref[4:8, :] = jnp.zeros((4, width), jnp.float32)
        dx0 = back + dx1_ref[...]
        dx0_ref[...] = dx0
        rows_ref[...] = dx0.astype(low)

    return pl.pallas_call(
        body,
        out_shape=[
            shape_of((count, width), jnp.float32),
            shape_of((count, width), low),
            shape_of((count, 3 * width), low),
            shape_of((8, width), jnp.float32),
        ],
        in_specs=[whole_block()] * 6,
        out_specs=[whole_block()] * 4,
        compiler_params=params(),
        cost_estimate=cost(16 * count * width * width, 10 * width * width),
    )(mixed, dx1, packed, x0, w_qkv, vec_rows)


def bit_of(index, level):
    return (index >> level) & 1


def xor_order(parts, index):
    level = 0
    while (1 << level) < len(parts):
        odd = bit_of(index, level) == 1
        step = 1 << level
        placed = list(parts)
        for place in range(len(parts)):
            if not place & step:
                low, high = parts[place], parts[place | step]
                placed[place] = jnp.where(odd, high, low)
                placed[place | step] = jnp.where(odd, low, high)
        parts = placed
        level += 1
    return parts


def tree_sum(parts):
    while len(parts) > 1:
        parts = [parts[place] + parts[place + 1] for place in range(0, len(parts), 2)]
    return parts[0]


def swap_core(value):
    count = lax.axis_size("vocab")
    return lax.ppermute(value, "vocab", [(i, i ^ 1) for i in range(count)])


def swap_outer(value, step):
    count = lax.axis_size("vocab")
    return lax.ppermute(value, "vocab", [(i, i ^ (2 * step)) for i in range(count)])


def swap_dp(value, step):
    count = lax.axis_size("dp")
    return lax.ppermute(value, "dp", [(i, i ^ step) for i in range(count)])


def places():
    vocab_index = lax.axis_index("vocab")
    return (lax.axis_index("dp"), vocab_index // 2, vocab_index % 2)


def gather_vocab(value):
    _, outer, core = places()
    pair = jnp.stack(xor_order([value, swap_core(value)], core))
    count = lax.axis_size("vocab") // 2
    parts = [pair] + [swap_outer(pair, step) for step in range(1, count)]
    return jnp.concatenate(xor_order(parts, outer), axis=0)


def gather_dp(value):
    dp_index, _, _ = places()
    parts = [value] + [swap_dp(value, step) for step in range(1, lax.axis_size("dp"))]
    return jnp.stack(xor_order(parts, dp_index))


def sum_all(value):
    value = value + swap_core(value)
    value = tree_sum([value] + [swap_dp(value, step) for step in range(1, lax.axis_size("dp"))])
    return tree_sum(outer_parts(value))


def outer_parts(value):
    count = lax.axis_size("vocab") // 2
    return [value] + [swap_outer(value, step) for step in range(1, count)]


def behind(value, *others):
    return lax.optimization_barrier((value, others))[0]


class Slots:
    def __init__(self):
        self.last = None

    def open(self, value):
        return value if self.last is None else behind(value, self.last)

    def close(self, *results):
        self.last = results


class OuterGather:
    def __init__(self, value):
        self.held = value[None]

    def advance(self, slots):
        count = lax.axis_size("vocab") // 2
        step = count // (2 * self.held.shape[0])
        if step:
            shape = (-1,) + self.held.shape[1:]
            held = slots.open(self.held)
            self.held = jnp.stack([held, swap_outer(held, step)], axis=1).reshape(shape)

    def finish(self, slots):
        while self.held.shape[0] < lax.axis_size("vocab") // 2:
            self.advance(slots)
        return self.held


def ring_first(held, slots):
    held = slots.open(held)
    return (held, swap_dp(held, 1), swap_dp(held, 2))


def ring_second(parts, slots):
    held, from_one, from_two = parts
    half = held.shape[0] // 2
    low, high = slots.open((from_two[:half], from_one[half:]))
    return jnp.concatenate([held, from_one, from_two, swap_dp(low, 1), swap_dp(high, 2)], axis=0)


def place_blocks(held, other, cuts):
    dp_index, outer, core = places()
    count = held.shape[0]
    outer_count = lax.axis_size("vocab") // 2
    here = jnp.stack([dp_index, outer, core]).astype(jnp.int32)
    if held.ndim == 3:
        spans, shapes = [], []
        for width in cuts:
            spans.append((sum(w for _, w in spans), width))
            shapes.append((held.shape[1], width))

        def take(ref, block, index):
            return ref.at[block, :, pl.ds(*spans[index])]

    else:
        shapes = [
            held.shape[2:] if isinstance(one, int) else (one[1] - one[0],) + held.shape[2:]
            for one in cuts
        ]

        def take(ref, block, index):
            one = cuts[index]
            if isinstance(one, int):
                return ref.at[block, one]
            return ref.at[block, pl.ds(one[0], one[1] - one[0])]


    def body(here_ref, held_ref, other_ref, *refs):
        out_refs, sems = refs[: len(cuts)], refs[len(cuts)]

        def copies(block):
            dp_place = (block // outer_count) ^ here_ref[0]
            outer_place = (block % outer_count) ^ here_ref[1]
            target = (dp_place * outer_count + outer_place) * 2
            made = []
            for side, ref in enumerate((held_ref, other_ref)):
                place = target + (here_ref[2] ^ side)
                for index in range(len(cuts)):
                    made.append(
                        pltpu.make_async_copy(
                            take(ref, block, index),
                            out_refs[index].at[place],
                            sems.at[index, side, block],
                        )
                    )
            return made

        def start(block, carry):
            for copy in copies(block):
                copy.start()
            return carry

        def wait(block, carry):
            for copy in copies(block):
                copy.wait()
            return carry

        lax.fori_loop(0, count, start, 0)
        lax.fori_loop(0, count, wait, 0)

    any_space = pl.BlockSpec(memory_space=pl.ANY)
    return pl.pallas_call(
        body,
        out_shape=[
            jax.ShapeDtypeStruct((2 * count,) + tuple(shape), held.dtype) for shape in shapes
        ],
        in_specs=[pl.BlockSpec(memory_space=pltpu.SMEM), any_space, any_space],
        out_specs=[pl.BlockSpec(memory_space=pltpu.VMEM) for _ in cuts],
        scratch_shapes=[pltpu.SemaphoreType.DMA((len(cuts), 2, count))],
        compiler_params=pltpu.CompilerParams(vmem_limit_bytes=VMEM_BYTES),
        cost_estimate=pl.CostEstimate(
            flops=0, bytes_accessed=4 * held.size * held.dtype.itemsize, transcendentals=0
        ),
    )(here, held, other)


def tile_of(values):
    row = lax.broadcasted_iota(jnp.int32, (8, 128), 0)
    lane = lax.broadcasted_iota(jnp.int32, (8, 128), 1)
    tile = jnp.zeros((8, 128), jnp.float32)
    for place, value in enumerate(values):
        if value is not None:
            tile = jnp.where((row == 0) & (lane == place), value, tile)
    return tile


def total_of(value):
    return jnp.sum(jnp.sum(value, axis=1, keepdims=True), axis=0, keepdims=True)


def fold_rows(value):
    return jnp.sum(value.reshape(-1, 8, value.shape[1]), axis=0)


def prepare_table(table, smalls, dp_count, first):
    rows, width = table.shape
    chunks = -(-rows // CHUNK)
    per = max(n for n in range(1, 9) if chunks % n == 0 and n * CHUNK <= rows)
    tile = per * CHUNK
    steps = chunks // per

    def body(first_ref, table_ref, *refs):
        small_refs, (low_ref, sum_ref, row_ref, acc_ref) = refs[: len(smalls)], refs[len(smalls) :]
        step = pl.program_id(0)
        row = lax.broadcasted_iota(jnp.int32, (tile, 1), 0) + step * tile
        value = jnp.where(row < rows, table_ref[...], 0.0)
        rounded = value.astype(jnp.bfloat16)
        low_ref[...] = rounded
        part = fold_rows(value * value)
        whole = jnp.where(row + first_ref[0] < V_REAL, rounded.astype(jnp.float32), 0.0)
        whole = jnp.sum(fold_rows(whole), axis=0, keepdims=True)

        @pl.when(step == 0)
        def _():
            acc_ref[...] = part
            row_ref[...] = whole

        @pl.when(step > 0)
        def _():
            acc_ref[...] += part
            row_ref[...] += whole

        @pl.when(step == steps - 1)
        def _():
            terms = [None] + [total_of(ref[...] * ref[...]) for ref in small_refs]
            terms.append(total_of(acc_ref[...]) / dp_count)
            sum_ref[...] = tile_of(terms)

    return pl.pallas_call(
        body,
        grid=(steps,),
        out_shape=[
            jax.ShapeDtypeStruct((chunks * CHUNK, width), jnp.bfloat16),
            jax.ShapeDtypeStruct((8, 128), jnp.float32),
            jax.ShapeDtypeStruct((1, width), jnp.float32),
        ],
        in_specs=[pl.BlockSpec(memory_space=pltpu.SMEM), pl.BlockSpec((tile, width), lambda i: (i, 0))]
        + [whole_block() for _ in smalls],
        out_specs=[pl.BlockSpec((tile, width), lambda i: (i, 0)), whole_block(), whole_block()],
        scratch_shapes=[pltpu.VMEM((8, width), jnp.float32)],
        compiler_params=pltpu.CompilerParams(vmem_limit_bytes=VMEM_BYTES),
        cost_estimate=pl.CostEstimate(
            flops=4 * table.size, bytes_accessed=6 * table.size, transcendentals=0
        ),
    )(first, table, *smalls)


def logit_grad(values, columns, norms, targets, scale):
    drop = jnp.where(
        columns == targets,
        scale * (1.0 - SMOOTHING + SMOOTHING / V_REAL),
        scale * (SMOOTHING / V_REAL),
    )
    return jnp.exp(values - norms) - drop


def table_part(earlier, head_all, table_low, targets, norms, first, rows, scale, start, stop):
    count, width = head_all.shape
    block = min(512, count)

    def body(first_ref, head_ref, table_ref, target_ref, norm_ref, *refs):
        out_ref, done_ref = refs[-2:]
        done_ref[...] = jnp.zeros_like(done_ref)
        begin = (pl.program_id(0) + start) * PIECE
        real = jnp.minimum(rows, V_REAL - first_ref[0])
        part = table_ref[...]
        local = lax.broadcasted_iota(jnp.int32, (PIECE, 1), 0) + begin
        columns = local + first_ref[0]

        def total_of_blocks(masked):
            total = jnp.zeros((PIECE, width), jnp.float32)
            for place in range(0, count, block):
                span = slice(place, place + block)
                head = head_ref[span, :]
                grad = logit_grad(
                    dot_second(part, head), columns, norm_ref[:, span], target_ref[:, span], scale
                )
                if masked:
                    grad = jnp.where(local < real, grad, 0.0)
                total = total + dot_plain(grad.astype(jnp.bfloat16), head)
            return total

        @pl.when(begin + PIECE <= real)
        def _():
            out_ref[...] = total_of_blocks(False)

        @pl.when(begin + PIECE > real)
        def _():
            out_ref[...] = total_of_blocks(True)

    args = [first, head_all, table_low, targets, norms]
    specs = [
        pl.BlockSpec(memory_space=pltpu.SMEM),
        whole_block(),
        pl.BlockSpec((PIECE, width), lambda i: (i + start, 0)),
        whole_block(),
        whole_block(),
    ]
    aliases = {}
    if earlier is not None:
        aliases = {len(args): 0}
        args.append(earlier)
        specs.append(pl.BlockSpec(memory_space=pl.ANY))
    size = (stop - start) * PIECE
    return pl.pallas_call(
        body,
        grid=(stop - start,),
        out_shape=[
            jax.ShapeDtypeStruct(table_low.shape, jnp.float32),
            jax.ShapeDtypeStruct((8, 128), jnp.float32),
        ],
        in_specs=specs,
        out_specs=[pl.BlockSpec((PIECE, width), lambda i: (i + start, 0)), whole_block()],
        input_output_aliases=aliases,
        compiler_params=pltpu.CompilerParams(vmem_limit_bytes=VMEM_BYTES),
        cost_estimate=pl.CostEstimate(
            flops=4 * size * width * count,
            bytes_accessed=6 * size * width,
            transcendentals=size * count,
        ),
    )(*args)


def token_lists(ids, first, rows, cap, bands):
    local = ids - first
    mine = (local >= 0) & (local < rows)
    tokens = jnp.arange(ids.shape[1], dtype=jnp.int32)
    band = local // CHUNK
    key = jnp.where(mine, band * ids.shape[1] + tokens[None, :], bands * ids.shape[1])
    slot = jnp.sum((key[:, None, :] < key[:, :, None]).astype(jnp.int32), axis=2)
    slots = jnp.arange(cap, dtype=jnp.int32)
    hot = (slot[:, None, :] == slots[None, :, None]) & mine[:, None, :]
    row = jnp.sum(jnp.where(hot, local[:, None, :], 0), axis=2)
    token = jnp.sum(jnp.where(hot, tokens[None, None, :], 0), axis=2)
    upto = jnp.arange(bands, dtype=jnp.int32)
    ends = (band[:, None, :] <= upto[None, :, None]) & mine[:, None, :]
    return (jnp.sum(ends.astype(jnp.int32), axis=2), row, token)


def add_rows(table_grad, held, other, ends, row_list, token_list, gradients, weight_sums, dp_count):
    padded, width = table_grad.shape
    dp_index, outer, core = places()
    here = jnp.stack([dp_index, outer, core]).astype(jnp.int32)
    outer_count = lax.axis_size("vocab") // 2
    sequences, bands = ends.shape
    tokens = held.shape[1]
    cap = row_list.shape[1]
    fine = 256
    per = CHUNK // fine
    kept = sequences if sequences * tokens * width * 4 <= 2**24 else 1

    def body(here_ref, end_ref, row_ref, token_ref, grad_in_ref, held_ref, other_ref, sums_ref, *refs):
        small_refs = refs[: len(gradients)]
        grad_out_ref, total_ref, grad_ref, rows_ref, in_sems, out_sems = refs[len(gradients) :]

        def in_copy(index):
            span = pl.ds(pl.multiple_of(index * CHUNK, CHUNK), CHUNK)
            return pltpu.make_async_copy(grad_in_ref.at[span], grad_ref.at[span], in_sems.at[index])

        def out_copy(index):
            span = pl.ds(pl.multiple_of(index * CHUNK, CHUNK), CHUNK)
            return pltpu.make_async_copy(grad_ref.at[span], grad_out_ref.at[span], out_sems.at[index])

        for index in range(bands):
            in_copy(index).start()
        clip = jnp.zeros((1, 1), jnp.float32)
        for ref in small_refs:
            clip = clip + total_of(ref[...] * ref[...])

        def widen(index, carry):
            dp_place = (index // 2) // outer_count
            outer_place = (index // 2) % outer_count
            block = (dp_place ^ here_ref[0]) * outer_count + (outer_place ^ here_ref[1])
            span = pl.ds(pl.multiple_of(index % kept * tokens, tokens), tokens)

            @pl.when(index % 2 == here_ref[2])
            def _():
                rows_ref[span, :] = held_ref[block].astype(jnp.float32)

            @pl.when(index % 2 != here_ref[2])
            def _():
                rows_ref[span, :] = other_ref[block].astype(jnp.float32)

            return carry

        if kept > 1:
            lax.fori_loop(0, sequences, widen, 0)
        acc = jnp.zeros((8, width), jnp.float32)
        for band in range(bands):
            in_copy(band).wait()

            def sequence(index, carry, band=band):
                if kept == 1:
                    widen(index, 0)

                def one(slot, carry):
                    row = row_ref[index * cap + slot]
                    token = index % kept * tokens + token_ref[index * cap + slot]
                    grad_ref[pl.ds(row, 1), :] += rows_ref[pl.ds(token, 1), :]
                    return carry

                begin = end_ref[index * bands + band - 1] if band else 0
                lax.fori_loop(begin, end_ref[index * bands + band], one, 0)
                return carry

            lax.fori_loop(0, sequences, sequence, 0)
            out_copy(band).start()

            def square(index, acc, band=band):
                span = pl.ds(pl.multiple_of(band * CHUNK + index * fine, fine), fine)
                value = grad_ref[span, :]
                return acc + fold_rows(value * value)

            acc = lax.fori_loop(0, per, square, acc)
        total_ref[...] = sums_ref[...] + tile_of([clip + total_of(acc) / dp_count])
        for band in range(bands):
            out_copy(band).wait()

    smem = pl.BlockSpec(memory_space=pltpu.SMEM)
    any_space = pl.BlockSpec(memory_space=pl.ANY)
    return pl.pallas_call(
        body,
        out_shape=[
            jax.ShapeDtypeStruct(table_grad.shape, jnp.float32),
            jax.ShapeDtypeStruct((8, 128), jnp.float32),
        ],
        in_specs=[smem, smem, smem, smem, any_space, whole_block(), whole_block(), whole_block()]
        + [whole_block() for _ in gradients],
        out_specs=[any_space, whole_block()],
        scratch_shapes=[
            pltpu.VMEM((padded, width), jnp.float32),
            pltpu.VMEM((kept * tokens, width), jnp.float32),
            pltpu.SemaphoreType.DMA((bands,)),
            pltpu.SemaphoreType.DMA((bands,)),
        ],
        input_output_aliases={4: 0},
        compiler_params=pltpu.CompilerParams(vmem_limit_bytes=VMEM_BYTES),
        cost_estimate=pl.CostEstimate(
            flops=2 * table_grad.size, bytes_accessed=8 * table_grad.size, transcendentals=0
        ),
    )(
        here,
        ends.reshape(-1),
        row_list.reshape(-1),
        token_list.reshape(-1),
        table_grad,
        held,
        other,
        weight_sums,
        *gradients,
    )


def moments_of(gradient, first, second, factor):
    clipped = gradient * factor
    first = BETA_ONE * first + (1.0 - BETA_ONE) * clipped
    second = BETA_TWO * second + (1.0 - BETA_TWO) * clipped * clipped
    return (first, second)


def update_of(weight, first, second):
    scaled = second * (1.0 / (1.0 - BETA_TWO**STEP))
    root = scaled * lax.rsqrt(scaled) + ADAM_EPS
    return first * (1.0 / (1.0 - BETA_ONE**STEP)) / root + DECAY * weight


def clip_factor(sums):
    return jnp.minimum(1.0, CLIP_AT / jnp.sqrt(sums[0:1, 0:1]))


def table_tile(rows, dp_count):
    return -(-rows // (3 * dp_count * 8)) * 8


def update_norms(sums, smalls, table_set, dp_count):
    weight, gradient, first, second = table_set
    rows, width = weight.shape
    tile = -(-rows // (6 * dp_count * 8)) * 8
    last = -(-rows // tile) - 1
    here = lax.axis_index("dp").astype(jnp.int32).reshape(1)
    number = len(smalls)

    def body(here_ref, sums_ref, w_ref, g_ref, m_ref, s_ref, *refs):
        small_refs = refs[: 4 * number]
        out_refs = refs[4 * number : 7 * number]
        norm_ref, acc_ref, term_ref = refs[7 * number :]
        step = pl.program_id(0)
        factor = clip_factor(sums_ref[...])

        @pl.when(step == 0)
        def _():
            acc_ref[...] = jnp.zeros_like(acc_ref)
            terms = [None]
            for place in range(number):
                w, g, m, s = (ref[...] for ref in small_refs[4 * place : 4 * place + 4])
                m, s = moments_of(g, m, s, factor)
                u = update_of(w, m, s)
                out_refs[3 * place][...] = m
                out_refs[3 * place + 1][...] = s
                out_refs[3 * place + 2][...] = u
                terms.append(total_of(u * u))
            term_ref[...] = tile_of(terms)

        row = (here_ref[0] * 6 + step) * tile + lax.broadcasted_iota(jnp.int32, (tile, 1), 0)
        m, s = moments_of(g_ref[...], m_ref[...], s_ref[...], factor)
        u = jnp.where(row < rows, update_of(w_ref[...], m, s), 0.0)
        acc_ref[...] += fold_rows(u * u)

        @pl.when(step == 5)
        def _():
            norm_ref[...] = term_ref[...] + tile_of([None] * (number + 1) + [total_of(acc_ref[...])])

    block = pl.BlockSpec(
        (tile, width), lambda i, here_ref: (jnp.minimum(here_ref[0] * 6 + i, last), 0)
    )
    flat = [value for group in smalls for value in group]
    outs = [jax.ShapeDtypeStruct(group[0].shape, jnp.float32) for group in smalls for _ in range(3)]
    made = pl.pallas_call(
        body,
        grid_spec=pltpu.PrefetchScalarGridSpec(
            num_scalar_prefetch=1,
            grid=(6,),
            in_specs=[whole_block()] + [block] * 4 + [whole_block() for _ in flat],
            out_specs=[whole_block() for _ in outs] + [whole_block()],
            scratch_shapes=[pltpu.VMEM((8, width), jnp.float32), pltpu.VMEM((8, 128), jnp.float32)],
        ),
        out_shape=outs + [jax.ShapeDtypeStruct((8, 128), jnp.float32)],
        compiler_params=pltpu.CompilerParams(vmem_limit_bytes=VMEM_BYTES),
        cost_estimate=pl.CostEstimate(
            flops=20 * tile * 6 * width, bytes_accessed=16 * tile * 6 * width, transcendentals=2 * tile * 6 * width
        ),
    )(here, sums, weight, gradient, first, second, *flat)
    return ([made[3 * place : 3 * place + 3] for place in range(number)], made[-1])


def write_updates(sums, norms, smalls, table_set):
    weight, gradient, first, second = table_set
    rows, width = weight.shape
    tile = table_tile(rows, lax.axis_size("dp"))
    steps = -(-rows // tile)
    number = len(smalls)

    def body(sums_ref, norms_ref, w_ref, g_ref, m_ref, s_ref, *refs):
        small_refs = refs[: 2 * number]
        out_w, out_m, out_s = refs[2 * number : 2 * number + 3]
        small_outs = refs[2 * number + 3 :]
        sums = sums_ref[...]
        pace = RATE * jnp.sqrt(sums) / jnp.sqrt(norms_ref[...])

        @pl.when(pl.program_id(0) == 0)
        def _():
            for place in range(number):
                w, u = (ref[...] for ref in small_refs[2 * place : 2 * place + 2])
                small_outs[place][...] = w - pace[0:1, place + 1 : place + 2] * u

        m, s = moments_of(g_ref[...], m_ref[...], s_ref[...], clip_factor(sums))
        w = w_ref[...]
        out_m[...] = m
        out_s[...] = s
        out_w[...] = w - pace[0:1, number + 1 : number + 2] * update_of(w, m, s)

    block = pl.BlockSpec((tile, width), lambda i: (i, 0))
    flat = [value for group in smalls for value in group]
    outs = [jax.ShapeDtypeStruct(weight.shape, jnp.float32)] * 3
    outs += [jax.ShapeDtypeStruct(group[0].shape, jnp.float32) for group in smalls]
    return pl.pallas_call(
        body,
        grid=(steps,),
        out_shape=outs,
        in_specs=[whole_block(), whole_block()] + [block] * 4 + [whole_block() for _ in flat],
        out_specs=[block] * 3 + [whole_block() for _ in smalls],
        compiler_params=pltpu.CompilerParams(vmem_limit_bytes=VMEM_BYTES),
        cost_estimate=pl.CostEstimate(
            flops=20 * weight.size, bytes_accessed=28 * weight.size, transcendentals=2 * weight.size
        ),
    )(sums, norms, weight, gradient, first, second, *flat)


def pick_half(value, index, axis):
    return lax.dynamic_index_in_dim(value, index, axis, keepdims=False)


class OuterSum:
    def __init__(self, held):
        self.held = held
        self.step = 1

    def advance(self, slots):
        held = self.held
        if held.shape[0] > 1:
            _, outer, _ = places()
            pairs = held.reshape((-1, 2) + held.shape[1:])
            own = (outer // self.step) % 2
            out = slots.open(pick_half(pairs, 1 - own, 1).astype(jnp.bfloat16))
            self.held = pick_half(pairs, own, 1) + swap_outer(out, self.step).astype(jnp.float32)
            self.step *= 2

    def finish(self, slots):
        while self.held.shape[0] > 1:
            self.advance(slots)
        return self.held.reshape(self.held.shape[1:])


def scatter_first(parts, slots):
    own, one, two, one_upper, two_lower, first, second = parts
    half = first.shape[0]
    low = jnp.bfloat16
    first, second = slots.open((first, second))
    into_two = swap_dp(first, 1).astype(jnp.float32)
    into_one = swap_dp(second, 2).astype(jnp.float32)
    return (
        own,
        one.at[half:].set((one_upper + into_one).astype(low)),
        two.at[:half].set((two_lower + into_two).astype(low)),
    )


def scatter_second(parts, slots):
    own, one, two = parts
    one, two = slots.open((one, two))
    return own + (swap_dp(one, 1).astype(jnp.float32) + swap_dp(two, 2).astype(jnp.float32))


def shards(
    token_ids,
    pick_rows,
    target_ids,
    attn_in,
    attn_out,
    mlp_in,
    mlp_out,
    positions,
    vectors,
    table,
    *moments,
):
    low = jnp.bfloat16
    dp_index, outer, core = places()
    dp_count = lax.axis_size("dp")
    shard_count = lax.axis_size("vocab")
    device_count = dp_count * shard_count
    outer_count = shard_count // 2
    vocab_rows, width = table.shape
    seq_len = token_ids.shape[1]
    pick_count = pick_rows.shape[1]
    vocab_start = lax.axis_index("vocab") * vocab_rows

    slots = Slots()
    unit_rows = attn_in.shape[0]
    small_count = positions.size + vectors.size
    small_width = -(-small_count // (unit_rows * 128)) * 128
    small = jnp.concatenate([positions.astype(low).reshape(-1), vectors.astype(low).reshape(-1)])
    small = jnp.pad(small, (0, unit_rows * small_width - small_count))
    first = OuterGather(
        jnp.concatenate(
            [attn_in.astype(low), attn_out.astype(low), small.reshape(unit_rows, small_width)], axis=1
        )
    )
    up_parts = mlp_in.shape[1] // width
    both = OuterGather(
        jnp.concatenate(
            [
                jnp.swapaxes(mlp_in.astype(low).reshape(unit_rows, up_parts, width), 0, 1),
                mlp_out.astype(low).reshape(-1, unit_rows, width),
            ],
            axis=0,
        )
    )
    small_masters = (attn_in, attn_out, mlp_in, mlp_out, positions, vectors)

    first.advance(slots)
    packed_ids = jnp.concatenate([token_ids, target_ids], axis=1)
    ids_pair = jnp.stack(xor_order([packed_ids, swap_core(packed_ids)], core))
    slots.close(first.held, ids_pair)

    first.finish(slots)
    ids_parts = outer_parts(slots.open(ids_pair))
    group_packed = jnp.concatenate(xor_order(ids_parts, outer), axis=0).reshape(shard_count, -1)
    group_targets = group_packed[:, seq_len:]
    slots.close(first.held, group_packed)

    first_ring = ring_first(first.held, slots)
    both.advance(slots)
    group_local = slots.open(group_packed) - vocab_start
    mine = (group_local >= 0) & (group_local < vocab_rows)
    served = jnp.take(table, jnp.where(mine, group_local, 0).reshape(-1), axis=0)
    served = jnp.where(mine.reshape(-1)[:, None], served, 0.0).astype(low)
    served = served.reshape(outer_count, 2, -1, width)
    slots.close(first_ring, both.held, served)

    first_held = ring_second(first_ring, slots)
    served = slots.open(served)
    served = pick_half(served, core, 1) + swap_core(pick_half(served, 1 - core, 1))
    slots.close(first_held, served)

    both.finish(slots)
    first_other = swap_core(slots.open(first_held))
    embedded = OuterSum(slots.open(served)[:, :seq_len].astype(jnp.float32))
    embedded.advance(slots)
    first_column = vocab_start.astype(jnp.int32).reshape(1)
    table_low, weight_sums, row_part = prepare_table(
        slots.open(table), small_masters, dp_count, first_column
    )
    slots.close(first_other, both.held, embedded.held, table_low)

    both_ring = ring_first(both.held, slots)
    embedded = embedded.finish(slots)
    w_qkv, w_proj, small_all = place_blocks(
        slots.open(first_held), first_other, (3 * width, width, small_width)
    )
    slots.close(embedded, w_qkv)

    w_qkv = w_qkv.reshape(width, 3 * width)
    w_proj = w_proj.reshape(width, width)
    small_all = slots.open(small_all).reshape(device_count, -1)
    pos_low = small_all[:, : positions.size].reshape(seq_len, width)
    vec_low = small_all[:, positions.size : small_count].reshape((device_count,) + vectors.shape)
    vec_rows = jnp.moveaxis(vec_low, 0, 1).reshape(vectors.shape[0], width).astype(jnp.float32)
    unit_chooser = choosers(width, unit_rows, core, dp_index)
    slots.close(both_ring, embedded, vec_rows, pos_low, unit_chooser)

    both_held = ring_second(both_ring, slots)
    resid_in, packed, resid_mid, normed_two, lefts_own, lefts_sent = attention_forward(
        slots.open(embedded), pos_low, vec_rows, w_qkv, w_proj, unit_chooser
    )
    target_rows = served[:, seq_len:].astype(jnp.float32)
    target_rows = OuterSum(target_rows)
    target_rows.advance(slots)
    slots.close(both_held, normed_two, target_rows.held)

    both_other = swap_core(slots.open(both_held))
    lefts_got = swap_core(slots.open(lefts_sent))
    target_rows = target_rows.finish(slots)
    packed_all = gather_dp(slots.open(group_packed)).reshape(device_count, -1)
    made = place_blocks(
        both_held, both_other, tuple(range(up_parts)) + ((up_parts, both_held.shape[1]),)
    )
    w_up = [value.reshape(width, width) for value in made[:up_parts]]
    w_down = made[up_parts].reshape(-1, width)
    hidden_pre, hidden_act, act_own, act_sent = hidden_forward(
        normed_two,
        vec_rows,
        w_up,
        choosers(width, mlp_out.shape[0], core),
        dp_index.astype(jnp.int32).reshape(1),
    )
    picks = pick_rows.reshape(-1, 1)
    resid_out, picked = output_forward(hidden_act, w_down, resid_mid, vec_rows, picks)
    slots.close(picked, packed_all, lefts_got, target_rows)

    tail_rows = jnp.concatenate(split_three(row_part), axis=0)
    sent = jnp.concatenate([picked, jnp.pad(tail_rows, ((0, 13), (0, 0)))], axis=0)
    same_core = jnp.stack(outer_parts(slots.open(sent)))
    act_got = swap_core(slots.open(act_sent))
    slots.close(same_core, act_got)

    ordered = jnp.stack(xor_order([same_core[step] for step in range(outer_count)], outer))
    head_in = jnp.stack(xor_order([ordered, swap_core(slots.open(ordered))], core), axis=1)
    row_sum = head_in[:, :, pick_count : pick_count + 3].astype(jnp.float32).reshape(-1, width)
    row_sum = jnp.sum(row_sum, axis=0, keepdims=True)
    head_in = head_in[:, :, :pick_count]
    head_in = head_in.reshape(-1, width)
    slots.close(head_in)
    ring = ring_first(same_core[:, :pick_count], slots)
    here = jnp.stack([vocab_start, core]).astype(jnp.int32)
    head_own, head_stat, head_sent = head_pass(slots.open(head_in), table_low, here, vocab_rows, pick_count)
    slots.close(head_sent, ring)

    head_got = swap_core(slots.open(head_sent))
    joined = join_cores(
        head_own, head_stat, head_got, outer.astype(jnp.int32).reshape(1), pick_count
    )
    slots.close(joined[0])

    received = [
        swap_outer(value, step + 1) for step, value in enumerate(slots.open(tuple(joined[2:])))
    ]
    token_count = device_count * pick_count
    grad_top, grad_branch, vec_down, row_stats = output_backward(
        joined[0],
        joined[1],
        received,
        picked,
        target_rows,
        row_sum,
        picks,
        resid_out,
        vec_rows,
        float(token_count),
    )
    slots.close(grad_branch)

    dy_got = swap_core(slots.open(grad_branch))
    stats_pair = slots.open(row_stats[:, :2].T)
    stats_pair = jnp.stack(xor_order([stats_pair, swap_core(stats_pair)], core))
    ring = ring_second(ring, slots)
    grad_pre, vec_up = hidden_backward(slots.open(grad_branch), w_down, hidden_pre)
    slots.close(dy_got, stats_pair, grad_pre, ring)

    pre_got = swap_core(slots.open(grad_pre))
    stats_parts = outer_parts(slots.open(stats_pair))
    stats_group = jnp.concatenate(xor_order(stats_parts, outer), axis=0)
    down = gradient_blocks(
        [(act_own, act_got)],
        [(0, act_own.shape[1])],
        [(slots.open(grad_branch), dy_got)],
        None,
        mlp_out.shape[0],
    )
    slots.close(pre_got, stats_group, down[5])

    lefts = (lefts_own, lefts_got)
    left_spans = [(place * width // 2, (place + 1) * width // 2) for place in range(3)]
    down = scatter_first(down, slots)
    stats_all = gather_dp(slots.open(stats_group))
    up = gradient_blocks(
        [lefts], left_spans[2:], [(slots.open(grad_pre), pre_got)], None, unit_rows
    )
    grad_mid, grad_attn, grad_mixed, vec_middle = middle_backward(
        behind(grad_pre, up[5]), w_up, grad_top, resid_mid, w_proj, vec_rows
    )
    slots.close(down, up, grad_mid, stats_all)

    down = OuterSum(scatter_second(down, slots))
    attn_got = swap_core(slots.open(grad_attn))
    ring_other = swap_core(slots.open(ring))
    grad_in, grad_rows, grad_packed, vec_first = attention_backward(
        grad_mixed, slots.open(grad_mid), packed, resid_in, w_qkv, vec_rows
    )
    slots.close(down.held, grad_rows, attn_got, ring_other)
    grad_in, vec_first = slots.open((grad_in, vec_first))

    norm_all = (stats_all[:, :, 0].reshape(1, -1) + math.log(token_count)).astype(jnp.float32)
    loss = jnp.sum(stats_all[:, :, 1]) / token_count
    targets_all = packed_all[:, seq_len:].reshape(1, -1)
    counts, row_list, token_list = token_lists(
        packed_all[:, :seq_len],
        vocab_start,
        vocab_rows,
        4 * seq_len // shard_count,
        table_low.shape[0] // CHUNK,
    )

    vec_grad = jnp.concatenate(
        [
            vec_first[0:2],
            vec_middle[0:2],
            vec_down[0:2],
            vec_first[2:4],
            vec_middle[2:3],
            vec_down[2:3],
            vec_up[0:4],
        ],
        axis=0,
    )
    vec_width = vectors.shape[1]
    vec_blocks = jnp.moveaxis(vec_grad.reshape(-1, device_count, vec_width), 1, 0)
    small_grad = jnp.concatenate(
        [grad_in.reshape(device_count, -1), vec_blocks.reshape(device_count, -1)], axis=1
    )
    small_grad = jnp.pad(small_grad, ((0, 0), (0, unit_rows * small_width - small_count)))
    small_grad = small_grad.reshape(-1, 2, unit_rows, small_width)
    small_sent = pick_half(small_grad, 1 - core, 1).astype(low)

    pieces = table_low.shape[0] // PIECE
    bounds = [0] + [round(pieces * share) for share in (0.3, 0.7, 0.9)] + [pieces]

    def head_part(earlier, part, mark):
        if bounds[part] == bounds[part + 1]:
            return (earlier, mark)
        return table_part(
            earlier,
            head_all,
            table_low,
            targets_all,
            behind(norm_all, mark),
            first_column,
            vocab_rows,
            1.0 / token_count,
            bounds[part],
            bounds[part + 1],
        )

    up = scatter_first(up, slots)
    packed_got = swap_core(slots.open(grad_packed))
    small_got = swap_core(slots.open(small_sent))
    small_sum = pick_half(small_grad, core, 1) + small_got.astype(jnp.float32)
    small_sum = small_sum.reshape(4, outer_count * unit_rows, small_width)
    small_sum = jnp.stack([pick_half(small_sum, dp_index ^ step, 0) for step in range(4)])
    head_all = place_blocks(slots.open(ring), ring_other, (width,))[0].reshape(-1, width)
    rows = OuterGather(slots.open(grad_rows))
    rows.advance(slots)
    slots.close(up[1:], packed_got, small_sum, rows.held, head_all)

    up = OuterSum(scatter_second(up, slots))
    rows_outer = rows.finish(slots)
    down.advance(slots)
    first = gradient_blocks(
        [lefts, lefts],
        left_spans[:2],
        [(grad_packed, slots.open(packed_got)), (grad_attn, attn_got)],
        small_sum,
        unit_rows,
    )
    table_grad, mark = head_part(None, 0, first[5])
    slots.close(up.held, first[5], rows_outer, down.held, mark)

    first = scatter_first(first, slots)
    rows_ring = ring_first(rows_outer, slots)
    up.advance(slots)
    table_grad, mark = head_part(table_grad, 1, slots.last)
    slots.close(first[1:], rows_ring, up.held, mark)

    first = scatter_second(first, slots)
    rows_held = ring_second(rows_ring, slots)
    up_own = up.finish(slots)
    table_grad, mark = head_part(table_grad, 2, slots.last)
    slots.close(first, up_own, rows_held, mark)

    first_terms = [pick_half(first, outer, 0)]
    for step in range(1, outer_count):
        sent = slots.open(pick_half(first, outer ^ step, 0).astype(low))
        first_terms.append(swap_outer(sent, step).astype(jnp.float32))
    first_own = tree_sum(first_terms)
    rows_other = swap_core(slots.open(rows_held))
    down_own = down.finish(slots)
    table_grad, mark = head_part(table_grad, 3, slots.last)
    small_own = first_own[:, 4 * width :].reshape(-1)
    gradients = (
        first_own[:, : 3 * width],
        first_own[:, 3 * width : 4 * width],
        up_own,
        down_own,
        small_own[: positions.size].reshape(positions.shape),
        small_own[positions.size : small_count].reshape(vectors.shape),
    )
    table_grad, sums = add_rows(
        table_grad, rows_held, rows_other, counts, row_list, token_list, gradients, weight_sums, dp_count
    )
    sums = sum_all(sums)
    grad_norm = jnp.sqrt(sums[0, 0])
    firsts, seconds = moments[:7], moments[7:]
    smalls = list(zip(small_masters, gradients, firsts, seconds))
    table_set = (table, table_grad, firsts[6], seconds[6])
    made, norms = update_norms(sums, smalls, table_set, dp_count)
    norms = sum_all(norms)
    ratios = jnp.sqrt(sums[0, 1:8]) / jnp.sqrt(norms[0, 1:8])
    written = write_updates(
        sums, norms, [(weight, group[2]) for weight, group in zip(small_masters, made)], table_set
    )
    new_weights = list(written[3:]) + [written[0]]
    new_firsts = [group[0] for group in made] + [written[1]]
    new_seconds = [group[1] for group in made] + [written[2]]
    return (loss, grad_norm, ratios, *new_weights, *new_firsts, *new_seconds)


def solution(mesh):
    rows = P(("dp", "vocab"), None)
    weights = (rows, rows, rows, rows, rows, P(None, ("dp", "vocab")), P("vocab", None))
    return jax.shard_map(
        shards,
        mesh=mesh,
        in_specs=(rows, rows, rows) + weights * 3,
        out_specs=(P(), P(), P()) + weights * 3,
        check_vma=False,
    )
```

```python
import functools
import math

import jax
import jax.numpy as jnp
from jax import lax
from jax.experimental import pallas as pl
from jax.experimental.pallas import tpu as pltpu
from jax.sharding import PartitionSpec as P

HD = 64
V_REAL = 50257
STEP = 5


LN_EPS = 1e-05
SMOOTHING = 0.1
BETA_ONE = 0.9
BETA_TWO = 0.999
ADAM_EPS = 1e-12
DECAY = 0.01
RATE = 0.3
CLIP_AT = 0.01
MASKED = -1e30
CHUNK = 1280
PIECE = 640
VMEM_BYTES = 58 * 2**20


def layer_norm(inputs, gain, shift):
    centre = jnp.mean(inputs, axis=-1, keepdims=True)
    centred = inputs - centre
    spread = jnp.mean(centred * centred, axis=-1, keepdims=True)
    return centred * lax.rsqrt(spread + LN_EPS) * gain + shift


def gelu_tanh(inputs):
    return (
        0.5
        * inputs
        * (1.0 + jnp.tanh(0.7978845608028654 * (inputs + 0.044715 * inputs * inputs * inputs)))
    )


def dot_plain(left_op, right_op):
    return jnp.dot(left_op, right_op, preferred_element_type=jnp.float32)


def dot_first(left_op, right_op):
    return lax.dot_general(
        left_op, right_op, (((0,), (0,)), ((), ())), preferred_element_type=jnp.float32
    )


def dot_second(left_op, right_op):
    return lax.dot_general(
        left_op, right_op, (((1,), (1,)), ((), ())), preferred_element_type=jnp.float32
    )


def params():
    return pltpu.CompilerParams(vmem_limit_bytes=VMEM_BYTES)


def cost(flops, bytes_accessed):
    return pl.CostEstimate(
        flops=int(flops), bytes_accessed=int(bytes_accessed), transcendentals=0
    )


def whole_block():
    return pl.BlockSpec(memory_space=pltpu.VMEM)


def shape_of(shape, dtype):
    return jax.ShapeDtypeStruct(tuple(shape), dtype)


def causal_scores(queries, keys, causal):
    return jnp.where(causal, dot_second(queries, keys) * HD ** (-0.5), MASKED)


def causal_mask(count):
    query = lax.broadcasted_iota(jnp.int32, (count, count), 0)
    key = lax.broadcasted_iota(jnp.int32, (count, count), 1)
    return key <= query


def head_span(head):
    return slice(head * HD, (head + 1) * HD)


def attention_forward(embedded, positions, vec_rows, w_qkv, w_proj, chooser):
    count, width = embedded.shape
    low = jnp.bfloat16

    half = width // 2

    def body(
        e_ref, p_ref, v_ref, qkv_ref, proj_ref, c_ref, x0_ref, packed_ref, x1_ref, h2_ref, own_ref, other_ref, o_ref
    ):
        x0 = e_ref[...] + p_ref[...].astype(jnp.float32)
        x0_ref[...] = x0
        h1 = layer_norm(x0, v_ref[0:1, :], v_ref[1:2, :]).astype(low)
        parts = []
        for place, bias in enumerate((6, None, 7)):
            span = slice(place * width, (place + 1) * width)
            part = dot_plain(h1, qkv_ref[:, span])
            if bias is not None:
                part = part + v_ref[bias : bias + 1, :]
            parts.append(part.astype(low))
            packed_ref[:, span] = parts[-1]
        queries, keys, values = parts
        causal = causal_mask(count)
        for head in range(0, width // HD, 2):
            mixed = []
            for one in (head, head + 1):
                span = head_span(one)
                scores = causal_scores(queries[:, span], keys[:, span], causal)
                grown = jnp.exp(scores - jnp.max(scores, axis=-1, keepdims=True))
                probs = (grown / jnp.sum(grown, axis=-1, keepdims=True)).astype(low)
                mixed.append(dot_plain(probs, values[:, span]))
            o_ref[:, head * HD : (head + 2) * HD] = jnp.concatenate(mixed, axis=1).astype(low)
        x1 = x0 + dot_plain(o_ref[...], proj_ref[...]) + v_ref[8:9, :]
        x1_ref[...] = x1
        h2 = layer_norm(x1, v_ref[2:3, :], v_ref[3:4, :]).astype(low)
        h2_ref[...] = h2
        for place, value in enumerate((h1, o_ref[...], h2)):
            span = slice(place * half, (place + 1) * half)
            own_ref[:, span] = dot_plain(value, c_ref[0]).astype(low)
            other_ref[:, span] = dot_plain(value, c_ref[1]).astype(low)

    shape = (count, width)
    return pl.pallas_call(
        body,
        out_shape=[
            shape_of(shape, jnp.float32),
            shape_of((count, 3 * width), low),
            shape_of(shape, jnp.float32),
            shape_of(shape, low),
            shape_of((count, 3 * half), low),
            shape_of((count, 3 * half), low),
        ],
        in_specs=[whole_block()] * 6,
        out_specs=[whole_block()] * 6,
        scratch_shapes=[pltpu.VMEM(shape, low)],
        compiler_params=params(),
        cost_estimate=cost(20 * count * width * width, 8 * width * width),
    )(embedded, positions, vec_rows, w_qkv, w_proj, chooser)


def hidden_forward(normed, vec_rows, w_up, chooser, dp_index):
    count, width = normed.shape
    blocks = len(w_up)
    hidden = blocks * width
    half = width // 2
    low = jnp.bfloat16

    def body(dp_ref, h_ref, v_ref, c_ref, *refs):
        w_refs = refs[:blocks]
        pre_ref, act_ref, own_ref, other_ref = refs[blocks:]
        for place in range(blocks):
            span = slice(place * width, (place + 1) * width)
            pre = dot_plain(h_ref[...], w_refs[place][...]) + v_ref[10 + place : 11 + place, :]
            pre_ref[:, span] = pre
            act_ref[:, span] = gelu_tanh(pre).astype(low)
        for place in range(blocks):
            source = pl.multiple_of((dp_ref[0] ^ place) * width, width)
            part = act_ref[:, pl.ds(source, width)]
            span = slice(place * half, (place + 1) * half)
            own_ref[:, span] = dot_plain(part, c_ref[0]).astype(low)
            other_ref[:, span] = dot_plain(part, c_ref[1]).astype(low)

    return pl.pallas_call(
        body,
        out_shape=[
            shape_of((count, hidden), jnp.float32),
            shape_of((count, hidden), low),
            shape_of((count, hidden // 2), low),
            shape_of((count, hidden // 2), low),
        ],
        in_specs=[pl.BlockSpec(memory_space=pltpu.SMEM)] + [whole_block()] * (3 + blocks),
        out_specs=[whole_block()] * 4,
        compiler_params=params(),
        cost_estimate=cost(3 * count * width * hidden, 2 * width * hidden),
    )(dp_index, normed, vec_rows, chooser, *w_up)


def output_forward(act, w_down, resid_mid, vec_rows, picks):
    count, width = resid_mid.shape
    number = picks.shape[0]

    def body(act_ref, w_ref, x1_ref, v_ref, pick_ref, x2_ref, out_ref):
        x2 = x1_ref[...] + dot_plain(act_ref[...], w_ref[...]) + v_ref[9:10, :]
        x2_ref[...] = x2
        final = layer_norm(x2, v_ref[4:5, :], v_ref[5:6, :]).astype(jnp.bfloat16)
        hot = pick_ref[...] == lax.broadcasted_iota(jnp.int32, (number, count), 1)
        hot = jnp.where(hot, 1.0, 0.0).astype(jnp.bfloat16)
        out_ref[...] = dot_plain(hot, final).astype(jnp.bfloat16)

    return pl.pallas_call(
        body,
        out_shape=[
            shape_of((count, width), jnp.float32),
            shape_of((number, width), jnp.bfloat16),
        ],
        in_specs=[whole_block()] * 5,
        out_specs=[whole_block()] * 2,
        compiler_params=params(),
        cost_estimate=cost(2 * act.size * width, 2 * w_down.size),
    )(act, w_down, resid_mid, vec_rows, picks)


def norm_backward(grad, inputs, gain):
    centred = inputs - jnp.mean(inputs, axis=-1, keepdims=True)
    scale = lax.rsqrt(jnp.mean(centred * centred, axis=-1, keepdims=True) + LN_EPS)
    normed = centred * scale
    scaled = grad * gain
    back = scale * (
        scaled
        - jnp.mean(scaled, axis=-1, keepdims=True)
        - normed * jnp.mean(scaled * normed, axis=-1, keepdims=True)
    )
    return (
        back,
        jnp.sum(grad * normed, axis=0, keepdims=True),
        jnp.sum(grad, axis=0, keepdims=True),
    )


def column_sum(value):
    return jnp.sum(value.astype(jnp.float32), axis=0, keepdims=True)


def choosers(width, rows, core, dp_index=None):
    column = jnp.arange(width, dtype=jnp.int32)
    target = jnp.arange(width // 2, dtype=jnp.int32)
    block = target // rows
    if dp_index is not None:
        per = width // (8 * rows)
        block = ((block // per) ^ dp_index) * per + block % per
    made = []
    for side in (core, 1 - core):
        source = (block * 2 + side) * rows + target % rows
        made.append((column[:, None] == source[None, :]).astype(jnp.bfloat16))
    return jnp.stack(made)


def gradient_blocks(lefts, spans, rights, smalls, name_rows):
    widths = [right[0].shape[1] for right in rights]
    total = sum(widths) + (smalls.shape[2] if smalls is not None else 0)
    arrays = [value for pair in zip(lefts, rights) for group in pair for value in group]
    if smalls is not None:
        arrays.append(smalls)
    number = len(lefts)
    rows = (spans[0][1] - spans[0][0]) // 4
    half = rows // 2
    low = jnp.bfloat16

    def body(*refs):
        in_refs, out_refs = refs[: len(arrays)], refs[len(arrays) :]

        def put(made, span):
            own, one, two, three = [made(place) for place in range(4)]
            out_refs[0][:, span] = own
            out_refs[1][:, span] = one[:half].astype(low)
            out_refs[2][:, span] = one[half:]
            out_refs[3][:, span] = two[:half]
            out_refs[4][:, span] = two[half:].astype(low)
            out_refs[5][:, span] = three[:half].astype(low)
            out_refs[6][:, span] = three[half:].astype(low)

        start = 0
        for index in range(number):
            left_a, left_b, right_a, right_b = in_refs[4 * index : 4 * index + 4]
            columns = slice(*spans[index])
            left = jnp.concatenate([left_a[:, columns], left_b[:, columns]], axis=0)
            for begin in range(0, widths[index], 768):
                stop = min(begin + 768, widths[index])
                right = jnp.concatenate([right_a[:, begin:stop], right_b[:, begin:stop]], axis=0)
                result = dot_first(left, right)
                put(
                    lambda place, result=result: result[place * rows : (place + 1) * rows],
                    slice(start + begin, start + stop),
                )
            start += widths[index]
        if smalls is not None:
            put(lambda place: in_refs[-1][place], slice(start, total))

    out = [shape_of((rows, total), jnp.float32)]
    out += [shape_of((half, total), kind) for kind in (low, jnp.float32, jnp.float32, low, low, low)]
    flops = sum(4 * left[0].shape[0] * 4 * rows * right[0].shape[1] for left, right in zip(lefts, rights))
    made = pl.pallas_call(
        body,
        out_shape=out,
        in_specs=[whole_block()] * len(arrays),
        out_specs=[whole_block()] * 7,
        compiler_params=params(),
        cost_estimate=cost(flops, 14 * rows * total),
    )(*arrays)
    return [value.reshape(-1, name_rows, total) for value in made]


def split_three(value):
    low = jnp.bfloat16
    first = value.astype(low)
    rest = value - first.astype(jnp.float32)
    second = rest.astype(low)
    return (first, second, (rest - second.astype(jnp.float32)).astype(low))


def pack_stats(top, total):
    lane = lax.broadcasted_iota(jnp.int32, (top.shape[0], 128), 1)
    tile = jnp.zeros((top.shape[0], 128), jnp.float32)
    for place, part in enumerate(split_three(top) + split_three(total)):
        tile = jnp.where(lane == place, part.astype(jnp.float32), tile)
    return tile.astype(jnp.bfloat16)


def unpack_stats(tile):
    wide = tile.astype(jnp.float32)
    return (
        wide[:, 0:1] + (wide[:, 1:2] + wide[:, 2:3]),
        wide[:, 3:4] + (wide[:, 4:5] + wide[:, 5:6]),
    )


def join(one, two):
    top = jnp.maximum(one[1], two[1])
    scale_one, scale_two = jnp.exp(one[1] - top), jnp.exp(two[1] - top)
    return (
        one[0] * scale_one + two[0] * scale_two,
        top,
        one[2] * scale_one + two[2] * scale_two,
    )


def unpack_rows(packed, width):
    top, total = unpack_stats(packed[:, width:])
    return (packed[:, :width].astype(jnp.float32), top, total)


def head_pass(head_in, table_low, here, rows, pick_count):
    count, width = head_in.shape
    chunks = table_low.shape[0] // CHUNK
    groups = count // (2 * pick_count)
    half = count // 2

    def body(here_ref, head_ref, table_ref, own_ref, stat_ref, sent_ref, acc_ref, tops_ref):
        head = head_ref[...]
        real = jnp.minimum(rows, V_REAL - here_ref[0])
        acc_ref[...] = jnp.zeros_like(acc_ref)

        def step(index, carry, masked):
            top, total = carry
            begin = pl.multiple_of(index * CHUNK, CHUNK)
            part = table_ref[pl.ds(begin, CHUNK), :]
            values = dot_second(head, part)
            if masked:
                local = lax.broadcasted_iota(jnp.int32, (1, CHUNK), 1) + begin
                values = jnp.where(local < real, values, MASKED)
            higher = jnp.maximum(top, jnp.max(values, axis=1, keepdims=True))
            grown = jnp.exp(values - higher)
            scale = jnp.exp(top - higher)
            acc_ref[...] = acc_ref[...] * scale + dot_plain(grown.astype(jnp.bfloat16), part)
            return (higher, total * scale + jnp.sum(grown, axis=1, keepdims=True))

        carry = (jnp.full((count, 1), MASKED, jnp.float32), jnp.zeros((count, 1), jnp.float32))
        unmasked = jnp.maximum(real, 0) // CHUNK
        carry = lax.fori_loop(0, unmasked, functools.partial(step, masked=False), carry)
        top, total = lax.fori_loop(unmasked, chunks, functools.partial(step, masked=True), carry)
        lane = lax.broadcasted_iota(jnp.int32, (count, 128), 1)
        tops_ref[...] = jnp.where(lane == 0, top, jnp.where(lane == 1, total, 0.0))
        for group in range(groups):
            own = pl.multiple_of((2 * group + here_ref[1]) * pick_count, pick_count)
            other = pl.multiple_of((2 * group + 1 - here_ref[1]) * pick_count, pick_count)
            span = slice(group * pick_count, (group + 1) * pick_count)
            own_ref[span, :] = acc_ref[pl.ds(own, pick_count), :]
            stat_ref[span, :] = tops_ref[pl.ds(own, pick_count), :]
            sent_ref[span, :width] = acc_ref[pl.ds(other, pick_count), :].astype(jnp.bfloat16)
            stats = tops_ref[pl.ds(other, pick_count), :]
            sent_ref[span, width:] = pack_stats(stats[:, 0:1], stats[:, 1:2])

    return pl.pallas_call(
        body,
        out_shape=[
            shape_of((half, width), jnp.float32),
            shape_of((half, 128), jnp.float32),
            shape_of((half, width + 128), jnp.bfloat16),
        ],
        in_specs=[pl.BlockSpec(memory_space=pltpu.SMEM)] + [whole_block()] * 2,
        out_specs=[whole_block()] * 3,
        scratch_shapes=[pltpu.VMEM((count, width), jnp.float32), pltpu.VMEM((count, 128), jnp.float32)],
        compiler_params=params(),
        cost_estimate=cost(4 * table_low.size * count, 2 * table_low.size),
    )(here, head_in, table_low)


def join_cores(own, stats, received, outer, pick_count):
    half, width = own.shape
    groups = half // pick_count

    def body(outer_ref, own_ref, stat_ref, received_ref, rows_ref, out_stat_ref, *sent_refs):
        for step in range(groups):
            start = pl.multiple_of((outer_ref[0] ^ step) * pick_count, pick_count)
            span = pl.ds(start, pick_count)
            stat = stat_ref[span, :]
            one = (own_ref[span, :], stat[:, 0:1], stat[:, 1:2])
            value, top, total = join(one, unpack_rows(received_ref[span, :], width))
            if step:
                sent_refs[step - 1][:, :width] = value.astype(jnp.bfloat16)
                sent_refs[step - 1][:, width:] = pack_stats(top, total)
            else:
                lane = lax.broadcasted_iota(jnp.int32, (pick_count, 128), 1)
                rows_ref[...] = value
                out_stat_ref[...] = jnp.where(lane == 0, top, jnp.where(lane == 1, total, 0.0))

    return pl.pallas_call(
        body,
        out_shape=[
            shape_of((pick_count, width), jnp.float32),
            shape_of((pick_count, 128), jnp.float32),
        ]
        + [shape_of((pick_count, width + 128), jnp.bfloat16)] * (groups - 1),
        in_specs=[pl.BlockSpec(memory_space=pltpu.SMEM)] + [whole_block()] * 3,
        out_specs=[whole_block()] * (groups + 1),
        compiler_params=params(),
        cost_estimate=cost(4 * own.size, 8 * own.size),
    )(outer, own, stats, received)


def output_backward(rows, stats, received, picked, target_rows, row_sum, picks, resid_out, vec_rows, token_count):
    count, width = resid_out.shape
    number = picks.shape[0]
    low = jnp.bfloat16
    others = len(received)

    def body(rows_ref, stat_ref, *refs):
        received_refs = refs[:others]
        f_ref, t_ref, sum_ref, pick_ref, x_ref, v_ref, dx_ref, dy_ref, vec_ref, norm_ref = refs[others:]
        stat = stat_ref[...]
        value = (rows_ref[...], stat[:, 0:1], stat[:, 1:2])
        for ref in received_refs:
            value = join(value, unpack_rows(ref[...], width))
        mean, top, total = value
        target = t_ref[...]
        final = f_ref[...].astype(jnp.float32)
        norm = top + jnp.log(total)
        hit = jnp.sum(final * target, axis=1, keepdims=True)
        plain = jnp.sum(final * sum_ref[...], axis=1, keepdims=True)
        loss = (1.0 - SMOOTHING) * (norm - hit) + SMOOTHING * (norm - plain / V_REAL)
        lane = lax.broadcasted_iota(jnp.int32, (number, 128), 1)
        norm_ref[...] = jnp.where(lane == 0, norm, jnp.where(lane == 1, loss, 0.0))
        soft = jnp.exp(hit - norm)
        whole = ((soft - (1.0 - SMOOTHING) - SMOOTHING / V_REAL) / token_count).astype(low)
        factor = whole.astype(jnp.float32) - (soft - SMOOTHING / V_REAL) / token_count
        picked_grad = (
            mean * (1.0 / token_count) / total
            - sum_ref[...] * (SMOOTHING / V_REAL / token_count)
            + target * factor
        )
        hot = pick_ref[...] == lax.broadcasted_iota(jnp.int32, (number, count), 1)
        final_grad = lax.dot_general(
            jnp.where(hot, 1.0, 0.0),
            picked_grad,
            (((0,), (0,)), ((), ())),
            precision=lax.Precision.HIGHEST,
            preferred_element_type=jnp.float32,
        )
        back, gain, shift = norm_backward(final_grad, x_ref[...], v_ref[4:5, :])
        dx_ref[...] = back
        dy = back.astype(low)
        dy_ref[...] = dy
        vec_ref[0:1, :] = gain
        vec_ref[1:2, :] = shift
        vec_ref[2:3, :] = column_sum(dy)
        vec_ref[3:8, :] = jnp.zeros((5, width), jnp.float32)

    return pl.pallas_call(
        body,
        out_shape=[
            shape_of((count, width), jnp.float32),
            shape_of((count, width), low),
            shape_of((8, width), jnp.float32),
            shape_of((number, 128), jnp.float32),
        ],
        in_specs=[whole_block()] * (8 + others),
        out_specs=[whole_block()] * 4,
        compiler_params=params(),
        cost_estimate=cost(20 * count * width, 20 * count * width),
    )(rows, stats, *received, picked, target_rows, row_sum, picks, resid_out, vec_rows)


def hidden_backward(dy, w_down, pre):
    count, width = dy.shape
    hidden = pre.shape[1]
    low = jnp.bfloat16

    def body(dy_ref, w_ref, pre_ref, dpre_ref, vec_ref):
        vec_ref[...] = jnp.zeros_like(vec_ref)
        for place in range(hidden // width):
            span = slice(place * width, (place + 1) * width)
            grad = dot_second(dy_ref[...], w_ref[span, :])
            u = pre_ref[:, span]
            bent = jnp.tanh(0.7978845608028654 * (u + 0.044715 * u * u * u))
            slope = 0.5 * (1.0 + bent) + 0.5 * u * (1.0 - bent * bent) * (
                0.7978845608028654 * (1.0 + 3.0 * 0.044715 * u * u)
            )
            dpre = (grad * slope).astype(low)
            dpre_ref[:, span] = dpre
            vec_ref[place : place + 1, :] = column_sum(dpre)

    return pl.pallas_call(
        body,
        out_shape=[shape_of((count, hidden), low), shape_of((8, width), jnp.float32)],
        in_specs=[whole_block()] * 3,
        out_specs=[whole_block()] * 2,
        compiler_params=params(),
        cost_estimate=cost(2 * count * width * hidden, 2 * width * hidden),
    )(dy, w_down, pre)


def middle_backward(dpre, w_up, dx2, x1, w_proj, vec_rows):
    count, width = x1.shape
    low = jnp.bfloat16

    blocks = len(w_up)

    def body(dpre_ref, dx2_ref, x1_ref, proj_ref, v_ref, *refs):
        up_refs = refs[:blocks]
        dx1_ref, da_ref, mixed_ref, vec_ref = refs[blocks:]
        dh2 = jnp.zeros((count, width), jnp.float32)
        for place in range(blocks):
            span = slice(place * width, (place + 1) * width)
            dh2 = dh2 + dot_second(dpre_ref[:, span], up_refs[place][...])
        back, gain, shift = norm_backward(dh2, x1_ref[...], v_ref[2:3, :])
        dx1 = back + dx2_ref[...]
        dx1_ref[...] = dx1
        da = dx1.astype(low)
        da_ref[...] = da
        vec_ref[0:1, :] = gain
        vec_ref[1:2, :] = shift
        vec_ref[2:3, :] = column_sum(da)
        vec_ref[3:8, :] = jnp.zeros((5, width), jnp.float32)
        mixed_ref[...] = dot_second(da, proj_ref[...]).astype(low)

    return pl.pallas_call(
        body,
        out_shape=[
            shape_of((count, width), jnp.float32),
            shape_of((count, width), low),
            shape_of((count, width), low),
            shape_of((8, width), jnp.float32),
        ],
        in_specs=[whole_block()] * (5 + blocks),
        out_specs=[whole_block()] * 4,
        compiler_params=params(),
        cost_estimate=cost(10 * count * width * width, 10 * width * width),
    )(dpre, dx2, x1, w_proj, vec_rows, *w_up)


def attention_backward(mixed, dx1, packed, x0, w_qkv, vec_rows):
    count, width = x0.shape
    low = jnp.bfloat16

    def body(mixed_ref, dx1_ref, packed_ref, x0_ref, qkv_ref, v_ref, dx0_ref, rows_ref, grad_ref, vec_ref):
        causal = causal_mask(count)
        for head in range(0, width // HD, 2):
            sides = ([], [], [])
            for one in (head, head + 1):
                queries = packed_ref[:, one * HD : (one + 1) * HD]
                keys = packed_ref[:, width + one * HD : width + (one + 1) * HD]
                values = packed_ref[:, 2 * width + one * HD : 2 * width + (one + 1) * HD]
                scores = causal_scores(queries, keys, causal)
                grown = jnp.exp(scores - jnp.max(scores, axis=-1, keepdims=True))
                probs = grown / jnp.sum(grown, axis=-1, keepdims=True)
                out_grad = mixed_ref[:, one * HD : (one + 1) * HD]
                grad_p = dot_second(out_grad, values)
                centre = jnp.sum(probs * grad_p, axis=-1, keepdims=True)
                grad_s = (probs * (grad_p - centre)).astype(low)
                sides[0].append(dot_plain(grad_s, keys) * HD ** (-0.5))
                sides[1].append(dot_first(grad_s, queries) * HD ** (-0.5))
                sides[2].append(dot_first(probs.astype(low), out_grad))
            for place, side in enumerate(sides):
                start = place * width + head * HD
                grad_ref[:, start : start + 2 * HD] = jnp.concatenate(side, axis=1).astype(low)
        dh1 = dot_second(grad_ref[...], qkv_ref[...])
        back, gain, shift = norm_backward(dh1, x0_ref[...], v_ref[0:1, :])
        vec_ref[0:1, :] = gain
        vec_ref[1:2, :] = shift
        vec_ref[2:3, :] = column_sum(grad_ref[:, :width])
        vec_ref[3:4, :] = column_sum(grad_ref[:, 2 * width :])
        vec_ref[4:8, :] = jnp.zeros((4, width), jnp.float32)
        dx0 = back + dx1_ref[...]
        dx0_ref[...] = dx0
        rows_ref[...] = dx0.astype(low)

    return pl.pallas_call(
        body,
        out_shape=[
            shape_of((count, width), jnp.float32),
            shape_of((count, width), low),
            shape_of((count, 3 * width), low),
            shape_of((8, width), jnp.float32),
        ],
        in_specs=[whole_block()] * 6,
        out_specs=[whole_block()] * 4,
        compiler_params=params(),
        cost_estimate=cost(16 * count * width * width, 10 * width * width),
    )(mixed, dx1, packed, x0, w_qkv, vec_rows)


def bit_of(index, level):
    return (index >> level) & 1


def xor_order(parts, index):
    level = 0
    while (1 << level) < len(parts):
        odd = bit_of(index, level) == 1
        step = 1 << level
        placed = list(parts)
        for place in range(len(parts)):
            if not place & step:
                low, high = parts[place], parts[place | step]
                placed[place] = jnp.where(odd, high, low)
                placed[place | step] = jnp.where(odd, low, high)
        parts = placed
        level += 1
    return parts


def tree_sum(parts):
    while len(parts) > 1:
        parts = [parts[place] + parts[place + 1] for place in range(0, len(parts), 2)]
    return parts[0]


def swap_core(value):
    count = lax.axis_size("vocab")
    return lax.ppermute(value, "vocab", [(i, i ^ 1) for i in range(count)])


def swap_outer(value, step):
    count = lax.axis_size("vocab")
    return lax.ppermute(value, "vocab", [(i, i ^ (2 * step)) for i in range(count)])


def swap_dp(value, step):
    count = lax.axis_size("dp")
    return lax.ppermute(value, "dp", [(i, i ^ step) for i in range(count)])


def places():
    vocab_index = lax.axis_index("vocab")
    return (lax.axis_index("dp"), vocab_index // 2, vocab_index % 2)


def gather_vocab(value):
    _, outer, core = places()
    pair = jnp.stack(xor_order([value, swap_core(value)], core))
    count = lax.axis_size("vocab") // 2
    parts = [pair] + [swap_outer(pair, step) for step in range(1, count)]
    return jnp.concatenate(xor_order(parts, outer), axis=0)


def gather_dp(value):
    dp_index, _, _ = places()
    parts = [value] + [swap_dp(value, step) for step in range(1, lax.axis_size("dp"))]
    return jnp.stack(xor_order(parts, dp_index))


def sum_all(value):
    value = value + swap_core(value)
    value = tree_sum([value] + [swap_dp(value, step) for step in range(1, lax.axis_size("dp"))])
    return tree_sum(outer_parts(value))


def outer_parts(value):
    count = lax.axis_size("vocab") // 2
    return [value] + [swap_outer(value, step) for step in range(1, count)]


def behind(value, *others):
    return lax.optimization_barrier((value, others))[0]


class Slots:
    def __init__(self):
        self.last = None

    def open(self, value):
        return value if self.last is None else behind(value, self.last)

    def close(self, *results):
        self.last = results


class OuterGather:
    def __init__(self, value):
        self.held = value[None]

    def advance(self, slots):
        count = lax.axis_size("vocab") // 2
        step = count // (2 * self.held.shape[0])
        if step:
            shape = (-1,) + self.held.shape[1:]
            held = slots.open(self.held)
            self.held = jnp.stack([held, swap_outer(held, step)], axis=1).reshape(shape)

    def finish(self, slots):
        while self.held.shape[0] < lax.axis_size("vocab") // 2:
            self.advance(slots)
        return self.held


def ring_first(held, slots):
    held = slots.open(held)
    return (held, swap_dp(held, 1), swap_dp(held, 2))


def ring_second(parts, slots):
    held, from_one, from_two = parts
    half = held.shape[0] // 2
    low, high = slots.open((from_two[:half], from_one[half:]))
    return jnp.concatenate([held, from_one, from_two, swap_dp(low, 1), swap_dp(high, 2)], axis=0)


def place_blocks(held, other, cuts):
    dp_index, outer, core = places()
    count = held.shape[0]
    outer_count = lax.axis_size("vocab") // 2
    here = jnp.stack([dp_index, outer, core]).astype(jnp.int32)
    if held.ndim == 3:
        spans, shapes = [], []
        for width in cuts:
            spans.append((sum(w for _, w in spans), width))
            shapes.append((held.shape[1], width))

        def take(ref, block, index):
            return ref.at[block, :, pl.ds(*spans[index])]

    else:
        shapes = [
            held.shape[2:] if isinstance(one, int) else (one[1] - one[0],) + held.shape[2:]
            for one in cuts
        ]

        def take(ref, block, index):
            one = cuts[index]
            if isinstance(one, int):
                return ref.at[block, one]
            return ref.at[block, pl.ds(one[0], one[1] - one[0])]


    def body(here_ref, held_ref, other_ref, *refs):
        out_refs, sems = refs[: len(cuts)], refs[len(cuts)]

        def copies(block):
            dp_place = (block // outer_count) ^ here_ref[0]
            outer_place = (block % outer_count) ^ here_ref[1]
            target = (dp_place * outer_count + outer_place) * 2
            made = []
            for side, ref in enumerate((held_ref, other_ref)):
                place = target + (here_ref[2] ^ side)
                for index in range(len(cuts)):
                    made.append(
                        pltpu.make_async_copy(
                            take(ref, block, index),
                            out_refs[index].at[place],
                            sems.at[index, side, block],
                        )
                    )
            return made

        def start(block, carry):
            for copy in copies(block):
                copy.start()
            return carry

        def wait(block, carry):
            for copy in copies(block):
                copy.wait()
            return carry

        lax.fori_loop(0, count, start, 0)
        lax.fori_loop(0, count, wait, 0)

    any_space = pl.BlockSpec(memory_space=pl.ANY)
    return pl.pallas_call(
        body,
        out_shape=[
            jax.ShapeDtypeStruct((2 * count,) + tuple(shape), held.dtype) for shape in shapes
        ],
        in_specs=[pl.BlockSpec(memory_space=pltpu.SMEM), any_space, any_space],
        out_specs=[pl.BlockSpec(memory_space=pltpu.VMEM) for _ in cuts],
        scratch_shapes=[pltpu.SemaphoreType.DMA((len(cuts), 2, count))],
        compiler_params=pltpu.CompilerParams(vmem_limit_bytes=VMEM_BYTES),
        cost_estimate=pl.CostEstimate(
            flops=0, bytes_accessed=4 * held.size * held.dtype.itemsize, transcendentals=0
        ),
    )(here, held, other)


def tile_of(values):
    row = lax.broadcasted_iota(jnp.int32, (8, 128), 0)
    lane = lax.broadcasted_iota(jnp.int32, (8, 128), 1)
    tile = jnp.zeros((8, 128), jnp.float32)
    for place, value in enumerate(values):
        if value is not None:
            tile = jnp.where((row == 0) & (lane == place), value, tile)
    return tile


def total_of(value):
    return jnp.sum(jnp.sum(value, axis=1, keepdims=True), axis=0, keepdims=True)


def fold_rows(value):
    return jnp.sum(value.reshape(-1, 8, value.shape[1]), axis=0)


def prepare_table(table, smalls, dp_count, first):
    rows, width = table.shape
    chunks = -(-rows // CHUNK)
    per = max(n for n in range(1, 9) if chunks % n == 0 and n * CHUNK <= rows)
    tile = per * CHUNK
    steps = chunks // per

    def body(first_ref, table_ref, *refs):
        small_refs, (low_ref, sum_ref, row_ref, acc_ref) = refs[: len(smalls)], refs[len(smalls) :]
        step = pl.program_id(0)
        row = lax.broadcasted_iota(jnp.int32, (tile, 1), 0) + step * tile
        value = jnp.where(row < rows, table_ref[...], 0.0)
        rounded = value.astype(jnp.bfloat16)
        low_ref[...] = rounded
        part = fold_rows(value * value)
        whole = jnp.where(row + first_ref[0] < V_REAL, rounded.astype(jnp.float32), 0.0)
        whole = jnp.sum(fold_rows(whole), axis=0, keepdims=True)

        @pl.when(step == 0)
        def _():
            acc_ref[...] = part
            row_ref[...] = whole

        @pl.when(step > 0)
        def _():
            acc_ref[...] += part
            row_ref[...] += whole

        @pl.when(step == steps - 1)
        def _():
            terms = [None] + [total_of(ref[...] * ref[...]) for ref in small_refs]
            terms.append(total_of(acc_ref[...]) / dp_count)
            sum_ref[...] = tile_of(terms)

    return pl.pallas_call(
        body,
        grid=(steps,),
        out_shape=[
            jax.ShapeDtypeStruct((chunks * CHUNK, width), jnp.bfloat16),
            jax.ShapeDtypeStruct((8, 128), jnp.float32),
            jax.ShapeDtypeStruct((1, width), jnp.float32),
        ],
        in_specs=[pl.BlockSpec(memory_space=pltpu.SMEM), pl.BlockSpec((tile, width), lambda i: (i, 0))]
        + [whole_block() for _ in smalls],
        out_specs=[pl.BlockSpec((tile, width), lambda i: (i, 0)), whole_block(), whole_block()],
        scratch_shapes=[pltpu.VMEM((8, width), jnp.float32)],
        compiler_params=pltpu.CompilerParams(vmem_limit_bytes=VMEM_BYTES),
        cost_estimate=pl.CostEstimate(
            flops=4 * table.size, bytes_accessed=6 * table.size, transcendentals=0
        ),
    )(first, table, *smalls)


def logit_grad(values, columns, norms, targets, scale):
    drop = jnp.where(
        columns == targets,
        scale * (1.0 - SMOOTHING + SMOOTHING / V_REAL),
        scale * (SMOOTHING / V_REAL),
    )
    return jnp.exp(values - norms) - drop


def table_part(earlier, head_all, table_low, targets, norms, first, rows, scale, start, stop):
    count, width = head_all.shape
    block = min(512, count)

    def body(first_ref, head_ref, table_ref, target_ref, norm_ref, *refs):
        out_ref, done_ref = refs[-2:]
        done_ref[...] = jnp.zeros_like(done_ref)
        begin = (pl.program_id(0) + start) * PIECE
        real = jnp.minimum(rows, V_REAL - first_ref[0])
        part = table_ref[...]
        local = lax.broadcasted_iota(jnp.int32, (PIECE, 1), 0) + begin
        columns = local + first_ref[0]

        def total_of_blocks(masked):
            total = jnp.zeros((PIECE, width), jnp.float32)
            for place in range(0, count, block):
                span = slice(place, place + block)
                head = head_ref[span, :]
                grad = logit_grad(
                    dot_second(part, head), columns, norm_ref[:, span], target_ref[:, span], scale
                )
                if masked:
                    grad = jnp.where(local < real, grad, 0.0)
                total = total + dot_plain(grad.astype(jnp.bfloat16), head)
            return total

        @pl.when(begin + PIECE <= real)
        def _():
            out_ref[...] = total_of_blocks(False)

        @pl.when(begin + PIECE > real)
        def _():
            out_ref[...] = total_of_blocks(True)

    args = [first, head_all, table_low, targets, norms]
    specs = [
        pl.BlockSpec(memory_space=pltpu.SMEM),
        whole_block(),
        pl.BlockSpec((PIECE, width), lambda i: (i + start, 0)),
        whole_block(),
        whole_block(),
    ]
    aliases = {}
    if earlier is not None:
        aliases = {len(args): 0}
        args.append(earlier)
        specs.append(pl.BlockSpec(memory_space=pl.ANY))
    size = (stop - start) * PIECE
    return pl.pallas_call(
        body,
        grid=(stop - start,),
        out_shape=[
            jax.ShapeDtypeStruct(table_low.shape, jnp.float32),
            jax.ShapeDtypeStruct((8, 128), jnp.float32),
        ],
        in_specs=specs,
        out_specs=[pl.BlockSpec((PIECE, width), lambda i: (i + start, 0)), whole_block()],
        input_output_aliases=aliases,
        compiler_params=pltpu.CompilerParams(vmem_limit_bytes=VMEM_BYTES),
        cost_estimate=pl.CostEstimate(
            flops=4 * size * width * count,
            bytes_accessed=6 * size * width,
            transcendentals=size * count,
        ),
    )(*args)


def token_lists(ids, first, rows, cap, bands):
    local = ids - first
    mine = (local >= 0) & (local < rows)
    tokens = jnp.arange(ids.shape[1], dtype=jnp.int32)
    band = local // CHUNK
    key = jnp.where(mine, band * ids.shape[1] + tokens[None, :], bands * ids.shape[1])
    slot = jnp.sum((key[:, None, :] < key[:, :, None]).astype(jnp.int32), axis=2)
    slots = jnp.arange(cap, dtype=jnp.int32)
    hot = (slot[:, None, :] == slots[None, :, None]) & mine[:, None, :]
    row = jnp.sum(jnp.where(hot, local[:, None, :], 0), axis=2)
    token = jnp.sum(jnp.where(hot, tokens[None, None, :], 0), axis=2)
    upto = jnp.arange(bands, dtype=jnp.int32)
    ends = (band[:, None, :] <= upto[None, :, None]) & mine[:, None, :]
    return (jnp.sum(ends.astype(jnp.int32), axis=2), row, token)


def add_rows(table_grad, held, other, ends, row_list, token_list, gradients, weight_sums, dp_count):
    padded, width = table_grad.shape
    dp_index, outer, core = places()
    here = jnp.stack([dp_index, outer, core]).astype(jnp.int32)
    outer_count = lax.axis_size("vocab") // 2
    sequences, bands = ends.shape
    tokens = held.shape[1]
    cap = row_list.shape[1]
    fine = 256
    per = CHUNK // fine
    kept = sequences if sequences * tokens * width * 4 <= 2**24 else 1

    def body(here_ref, end_ref, row_ref, token_ref, grad_in_ref, held_ref, other_ref, sums_ref, *refs):
        small_refs = refs[: len(gradients)]
        grad_out_ref, total_ref, grad_ref, rows_ref, in_sems, out_sems = refs[len(gradients) :]

        def in_copy(index):
            span = pl.ds(pl.multiple_of(index * CHUNK, CHUNK), CHUNK)
            return pltpu.make_async_copy(grad_in_ref.at[span], grad_ref.at[span], in_sems.at[index])

        def out_copy(index):
            span = pl.ds(pl.multiple_of(index * CHUNK, CHUNK), CHUNK)
            return pltpu.make_async_copy(grad_ref.at[span], grad_out_ref.at[span], out_sems.at[index])

        for index in range(bands):
            in_copy(index).start()
        clip = jnp.zeros((1, 1), jnp.float32)
        for ref in small_refs:
            clip = clip + total_of(ref[...] * ref[...])

        def widen(index, carry):
            dp_place = (index // 2) // outer_count
            outer_place = (index // 2) % outer_count
            block = (dp_place ^ here_ref[0]) * outer_count + (outer_place ^ here_ref[1])
            span = pl.ds(pl.multiple_of(index % kept * tokens, tokens), tokens)

            @pl.when(index % 2 == here_ref[2])
            def _():
                rows_ref[span, :] = held_ref[block].astype(jnp.float32)

            @pl.when(index % 2 != here_ref[2])
            def _():
                rows_ref[span, :] = other_ref[block].astype(jnp.float32)

            return carry

        if kept > 1:
            lax.fori_loop(0, sequences, widen, 0)
        acc = jnp.zeros((8, width), jnp.float32)
        for band in range(bands):
            in_copy(band).wait()

            def sequence(index, carry, band=band):
                if kept == 1:
                    widen(index, 0)

                def one(slot, carry):
                    row = row_ref[index * cap + slot]
                    token = index % kept * tokens + token_ref[index * cap + slot]
                    grad_ref[pl.ds(row, 1), :] += rows_ref[pl.ds(token, 1), :]
                    return carry

                begin = end_ref[index * bands + band - 1] if band else 0
                lax.fori_loop(begin, end_ref[index * bands + band], one, 0)
                return carry

            lax.fori_loop(0, sequences, sequence, 0)
            out_copy(band).start()

            def square(index, acc, band=band):
                span = pl.ds(pl.multiple_of(band * CHUNK + index * fine, fine), fine)
                value = grad_ref[span, :]
                return acc + fold_rows(value * value)

            acc = lax.fori_loop(0, per, square, acc)
        total_ref[...] = sums_ref[...] + tile_of([clip + total_of(acc) / dp_count])
        for band in range(bands):
            out_copy(band).wait()

    smem = pl.BlockSpec(memory_space=pltpu.SMEM)
    any_space = pl.BlockSpec(memory_space=pl.ANY)
    return pl.pallas_call(
        body,
        out_shape=[
            jax.ShapeDtypeStruct(table_grad.shape, jnp.float32),
            jax.ShapeDtypeStruct((8, 128), jnp.float32),
        ],
        in_specs=[smem, smem, smem, smem, any_space, whole_block(), whole_block(), whole_block()]
        + [whole_block() for _ in gradients],
        out_specs=[any_space, whole_block()],
        scratch_shapes=[
            pltpu.VMEM((padded, width), jnp.float32),
            pltpu.VMEM((kept * tokens, width), jnp.float32),
            pltpu.SemaphoreType.DMA((bands,)),
            pltpu.SemaphoreType.DMA((bands,)),
        ],
        input_output_aliases={4: 0},
        compiler_params=pltpu.CompilerParams(vmem_limit_bytes=VMEM_BYTES),
        cost_estimate=pl.CostEstimate(
            flops=2 * table_grad.size, bytes_accessed=8 * table_grad.size, transcendentals=0
        ),
    )(
        here,
        ends.reshape(-1),
        row_list.reshape(-1),
        token_list.reshape(-1),
        table_grad,
        held,
        other,
        weight_sums,
        *gradients,
    )


def moments_of(gradient, first, second, factor):
    clipped = gradient * factor
    first = BETA_ONE * first + (1.0 - BETA_ONE) * clipped
    second = BETA_TWO * second + (1.0 - BETA_TWO) * clipped * clipped
    return (first, second)


def update_of(weight, first, second):
    scaled = second * (1.0 / (1.0 - BETA_TWO**STEP))
    root = scaled * lax.rsqrt(scaled) + ADAM_EPS
    return first * (1.0 / (1.0 - BETA_ONE**STEP)) / root + DECAY * weight


def clip_factor(sums):
    return jnp.minimum(1.0, CLIP_AT / jnp.sqrt(sums[0:1, 0:1]))


def table_tile(rows, dp_count):
    return -(-rows // (3 * dp_count * 8)) * 8


def update_norms(sums, smalls, table_set, dp_count):
    weight, gradient, first, second = table_set
    rows, width = weight.shape
    tile = -(-rows // (6 * dp_count * 8)) * 8
    last = -(-rows // tile) - 1
    here = lax.axis_index("dp").astype(jnp.int32).reshape(1)
    number = len(smalls)

    def body(here_ref, sums_ref, w_ref, g_ref, m_ref, s_ref, *refs):
        small_refs = refs[: 4 * number]
        out_refs = refs[4 * number : 7 * number]
        norm_ref, acc_ref, term_ref = refs[7 * number :]
        step = pl.program_id(0)
        factor = clip_factor(sums_ref[...])

        @pl.when(step == 0)
        def _():
            acc_ref[...] = jnp.zeros_like(acc_ref)
            terms = [None]
            for place in range(number):
                w, g, m, s = (ref[...] for ref in small_refs[4 * place : 4 * place + 4])
                m, s = moments_of(g, m, s, factor)
                u = update_of(w, m, s)
                out_refs[3 * place][...] = m
                out_refs[3 * place + 1][...] = s
                out_refs[3 * place + 2][...] = u
                terms.append(total_of(u * u))
            term_ref[...] = tile_of(terms)

        row = (here_ref[0] * 6 + step) * tile + lax.broadcasted_iota(jnp.int32, (tile, 1), 0)
        m, s = moments_of(g_ref[...], m_ref[...], s_ref[...], factor)
        u = jnp.where(row < rows, update_of(w_ref[...], m, s), 0.0)
        acc_ref[...] += fold_rows(u * u)

        @pl.when(step == 5)
        def _():
            norm_ref[...] = term_ref[...] + tile_of([None] * (number + 1) + [total_of(acc_ref[...])])

    block = pl.BlockSpec(
        (tile, width), lambda i, here_ref: (jnp.minimum(here_ref[0] * 6 + i, last), 0)
    )
    flat = [value for group in smalls for value in group]
    outs = [jax.ShapeDtypeStruct(group[0].shape, jnp.float32) for group in smalls for _ in range(3)]
    made = pl.pallas_call(
        body,
        grid_spec=pltpu.PrefetchScalarGridSpec(
            num_scalar_prefetch=1,
            grid=(6,),
            in_specs=[whole_block()] + [block] * 4 + [whole_block() for _ in flat],
            out_specs=[whole_block() for _ in outs] + [whole_block()],
            scratch_shapes=[pltpu.VMEM((8, width), jnp.float32), pltpu.VMEM((8, 128), jnp.float32)],
        ),
        out_shape=outs + [jax.ShapeDtypeStruct((8, 128), jnp.float32)],
        compiler_params=pltpu.CompilerParams(vmem_limit_bytes=VMEM_BYTES),
        cost_estimate=pl.CostEstimate(
            flops=20 * tile * 6 * width, bytes_accessed=16 * tile * 6 * width, transcendentals=2 * tile * 6 * width
        ),
    )(here, sums, weight, gradient, first, second, *flat)
    return ([made[3 * place : 3 * place + 3] for place in range(number)], made[-1])


def write_updates(sums, norms, smalls, table_set):
    weight, gradient, first, second = table_set
    rows, width = weight.shape
    tile = 2 * table_tile(rows, lax.axis_size("dp"))
    steps = -(-rows // tile)
    number = len(smalls)

    def body(sums_ref, norms_ref, w_ref, g_ref, m_ref, s_ref, *refs):
        small_refs = refs[: 2 * number]
        out_w, out_m, out_s = refs[2 * number : 2 * number + 3]
        small_outs = refs[2 * number + 3 :]
        sums = sums_ref[...]
        pace = RATE * jnp.sqrt(sums) / jnp.sqrt(norms_ref[...])

        @pl.when(pl.program_id(0) == 0)
        def _():
            for place in range(number):
                w, u = (ref[...] for ref in small_refs[2 * place : 2 * place + 2])
                small_outs[place][...] = w - pace[0:1, place + 1 : place + 2] * u

        m, s = moments_of(g_ref[...], m_ref[...], s_ref[...], clip_factor(sums))
        w = w_ref[...]
        out_m[...] = m
        out_s[...] = s
        out_w[...] = w - pace[0:1, number + 1 : number + 2] * update_of(w, m, s)

    block = pl.BlockSpec((tile, width), lambda i: (i, 0))
    flat = [value for group in smalls for value in group]
    outs = [jax.ShapeDtypeStruct(weight.shape, jnp.float32)] * 3
    outs += [jax.ShapeDtypeStruct(group[0].shape, jnp.float32) for group in smalls]
    return pl.pallas_call(
        body,
        grid=(steps,),
        out_shape=outs,
        in_specs=[whole_block(), whole_block()] + [block] * 4 + [whole_block() for _ in flat],
        out_specs=[block] * 3 + [whole_block() for _ in smalls],
        compiler_params=pltpu.CompilerParams(vmem_limit_bytes=VMEM_BYTES),
        cost_estimate=pl.CostEstimate(
            flops=20 * weight.size, bytes_accessed=28 * weight.size, transcendentals=2 * weight.size
        ),
    )(sums, norms, weight, gradient, first, second, *flat)


def pick_half(value, index, axis):
    return lax.dynamic_index_in_dim(value, index, axis, keepdims=False)


class OuterSum:
    def __init__(self, held):
        self.held = held
        self.step = 1

    def advance(self, slots):
        held = self.held
        if held.shape[0] > 1:
            _, outer, _ = places()
            pairs = held.reshape((-1, 2) + held.shape[1:])
            own = (outer // self.step) % 2
            out = slots.open(pick_half(pairs, 1 - own, 1).astype(jnp.bfloat16))
            self.held = pick_half(pairs, own, 1) + swap_outer(out, self.step).astype(jnp.float32)
            self.step *= 2

    def finish(self, slots):
        while self.held.shape[0] > 1:
            self.advance(slots)
        return self.held.reshape(self.held.shape[1:])


def scatter_first(parts, slots):
    own, one_lower, one_upper, two_lower, two_upper, first, second = parts
    low = jnp.bfloat16
    first, second = slots.open((first, second))
    into_two = swap_dp(first, 1).astype(jnp.float32)
    into_one = swap_dp(second, 2).astype(jnp.float32)
    return (
        own,
        jnp.concatenate([one_lower, (one_upper + into_one).astype(low)], axis=0),
        jnp.concatenate([(two_lower + into_two).astype(low), two_upper], axis=0),
    )


def scatter_second(parts, slots):
    own, one, two = parts
    one, two = slots.open((one, two))
    return own + (swap_dp(one, 1).astype(jnp.float32) + swap_dp(two, 2).astype(jnp.float32))


def shards(
    token_ids,
    pick_rows,
    target_ids,
    attn_in,
    attn_out,
    mlp_in,
    mlp_out,
    positions,
    vectors,
    table,
    *moments,
):
    low = jnp.bfloat16
    dp_index, outer, core = places()
    dp_count = lax.axis_size("dp")
    shard_count = lax.axis_size("vocab")
    device_count = dp_count * shard_count
    outer_count = shard_count // 2
    vocab_rows, width = table.shape
    seq_len = token_ids.shape[1]
    pick_count = pick_rows.shape[1]
    vocab_start = lax.axis_index("vocab") * vocab_rows

    slots = Slots()
    unit_rows = attn_in.shape[0]
    small_count = positions.size + vectors.size
    small_width = -(-small_count // (unit_rows * 128)) * 128
    small = jnp.concatenate([positions.astype(low).reshape(-1), vectors.astype(low).reshape(-1)])
    small = jnp.pad(small, (0, unit_rows * small_width - small_count))
    first = OuterGather(
        jnp.concatenate(
            [attn_in.astype(low), attn_out.astype(low), small.reshape(unit_rows, small_width)], axis=1
        )
    )
    up_parts = mlp_in.shape[1] // width
    both = OuterGather(
        jnp.concatenate(
            [
                jnp.swapaxes(mlp_in.astype(low).reshape(unit_rows, up_parts, width), 0, 1),
                mlp_out.astype(low).reshape(-1, unit_rows, width),
            ],
            axis=0,
        )
    )
    small_masters = (attn_in, attn_out, mlp_in, mlp_out, positions, vectors)

    first.advance(slots)
    packed_ids = jnp.concatenate([token_ids, target_ids], axis=1)
    ids_pair = jnp.stack(xor_order([packed_ids, swap_core(packed_ids)], core))
    slots.close(first.held, ids_pair)

    first.finish(slots)
    ids_parts = outer_parts(slots.open(ids_pair))
    group_packed = jnp.concatenate(xor_order(ids_parts, outer), axis=0).reshape(shard_count, -1)
    group_targets = group_packed[:, seq_len:]
    slots.close(first.held, group_packed)

    first_ring = ring_first(first.held, slots)
    both.advance(slots)
    group_local = slots.open(group_packed) - vocab_start
    mine = (group_local >= 0) & (group_local < vocab_rows)
    served = jnp.take(table, jnp.where(mine, group_local, 0).reshape(-1), axis=0)
    served = jnp.where(mine.reshape(-1)[:, None], served, 0.0).astype(low)
    served = served.reshape(outer_count, 2, -1, width)
    slots.close(first_ring, both.held, served)

    first_held = ring_second(first_ring, slots)
    served = slots.open(served)
    served = pick_half(served, core, 1) + swap_core(pick_half(served, 1 - core, 1))
    slots.close(first_held, served)

    both.finish(slots)
    first_other = swap_core(slots.open(first_held))
    embedded = OuterSum(slots.open(served)[:, :seq_len].astype(jnp.float32))
    embedded.advance(slots)
    first_column = vocab_start.astype(jnp.int32).reshape(1)
    table_low, weight_sums, row_part = prepare_table(
        slots.open(table), small_masters, dp_count, first_column
    )
    slots.close(first_other, both.held, embedded.held, table_low)

    both_ring = ring_first(both.held, slots)
    embedded = embedded.finish(slots)
    w_qkv, w_proj, small_all = place_blocks(
        slots.open(first_held), first_other, (3 * width, width, small_width)
    )
    slots.close(embedded, w_qkv)

    w_qkv = w_qkv.reshape(width, 3 * width)
    w_proj = w_proj.reshape(width, width)
    small_all = slots.open(small_all).reshape(device_count, -1)
    pos_low = small_all[:, : positions.size].reshape(seq_len, width)
    vec_low = small_all[:, positions.size : small_count].reshape((device_count,) + vectors.shape)
    vec_rows = jnp.moveaxis(vec_low, 0, 1).reshape(vectors.shape[0], width).astype(jnp.float32)
    unit_chooser = choosers(width, unit_rows, core, dp_index)
    slots.close(both_ring, embedded, vec_rows, pos_low, unit_chooser)

    both_held = ring_second(both_ring, slots)
    resid_in, packed, resid_mid, normed_two, lefts_own, lefts_sent = attention_forward(
        slots.open(embedded), pos_low, vec_rows, w_qkv, w_proj, unit_chooser
    )
    target_rows = served[:, seq_len:].astype(jnp.float32)
    target_rows = OuterSum(target_rows)
    target_rows.advance(slots)
    slots.close(both_held, normed_two, target_rows.held)

    both_other = swap_core(slots.open(both_held))
    lefts_got = swap_core(slots.open(lefts_sent))
    target_rows = target_rows.finish(slots)
    packed_all = gather_dp(slots.open(group_packed)).reshape(device_count, -1)
    made = place_blocks(
        both_held, both_other, tuple(range(up_parts)) + ((up_parts, both_held.shape[1]),)
    )
    w_up = [value.reshape(width, width) for value in made[:up_parts]]
    w_down = made[up_parts].reshape(-1, width)
    hidden_pre, hidden_act, act_own, act_sent = hidden_forward(
        normed_two,
        vec_rows,
        w_up,
        choosers(width, mlp_out.shape[0], core),
        dp_index.astype(jnp.int32).reshape(1),
    )
    picks = pick_rows.reshape(-1, 1)
    resid_out, picked = output_forward(hidden_act, w_down, resid_mid, vec_rows, picks)
    slots.close(picked, packed_all, lefts_got, target_rows)

    tail_rows = jnp.concatenate(split_three(row_part), axis=0)
    sent = jnp.concatenate([picked, jnp.pad(tail_rows, ((0, 13), (0, 0)))], axis=0)
    same_core = jnp.stack(outer_parts(slots.open(sent)))
    act_got = swap_core(slots.open(act_sent))
    counts, row_list, token_list = token_lists(
        slots.open(packed_all)[:, :seq_len],
        vocab_start,
        vocab_rows,
        4 * seq_len // shard_count,
        table_low.shape[0] // CHUNK,
    )
    slots.close(same_core, act_got, counts, row_list, token_list)

    ordered = jnp.stack(xor_order([same_core[step] for step in range(outer_count)], outer))
    head_in = jnp.stack(xor_order([ordered, swap_core(slots.open(ordered))], core), axis=1)
    row_sum = head_in[:, :, pick_count : pick_count + 3].astype(jnp.float32).reshape(-1, width)
    row_sum = jnp.sum(row_sum, axis=0, keepdims=True)
    head_in = head_in[:, :, :pick_count]
    head_in = head_in.reshape(-1, width)
    slots.close(head_in)
    ring = ring_first(same_core[:, :pick_count], slots)
    here = jnp.stack([vocab_start, core]).astype(jnp.int32)
    head_own, head_stat, head_sent = head_pass(slots.open(head_in), table_low, here, vocab_rows, pick_count)
    slots.close(head_sent, ring)

    head_got = swap_core(slots.open(head_sent))
    joined = join_cores(
        head_own, head_stat, head_got, outer.astype(jnp.int32).reshape(1), pick_count
    )
    slots.close(joined[0])

    received = [
        swap_outer(value, step + 1) for step, value in enumerate(slots.open(tuple(joined[2:])))
    ]
    token_count = device_count * pick_count
    grad_top, grad_branch, vec_down, row_stats = output_backward(
        joined[0],
        joined[1],
        received,
        picked,
        target_rows,
        row_sum,
        picks,
        resid_out,
        vec_rows,
        float(token_count),
    )
    slots.close(grad_branch)

    dy_got = swap_core(slots.open(grad_branch))
    stats_pair = slots.open(row_stats[:, :2].T)
    stats_pair = jnp.stack(xor_order([stats_pair, swap_core(stats_pair)], core))
    ring = ring_second(ring, slots)
    grad_pre, vec_up = hidden_backward(slots.open(grad_branch), w_down, hidden_pre)
    slots.close(dy_got, stats_pair, grad_pre, ring)

    pre_got = swap_core(slots.open(grad_pre))
    stats_parts = outer_parts(slots.open(stats_pair))
    stats_group = jnp.concatenate(xor_order(stats_parts, outer), axis=0)
    down = gradient_blocks(
        [(act_own, act_got)],
        [(0, act_own.shape[1])],
        [(slots.open(grad_branch), dy_got)],
        None,
        mlp_out.shape[0],
    )
    slots.close(pre_got, stats_group, down[5])

    lefts = (lefts_own, lefts_got)
    left_spans = [(place * width // 2, (place + 1) * width // 2) for place in range(3)]
    down = scatter_first(down, slots)
    stats_all = gather_dp(slots.open(stats_group))
    up = gradient_blocks(
        [lefts], left_spans[2:], [(slots.open(grad_pre), pre_got)], None, unit_rows
    )
    grad_mid, grad_attn, grad_mixed, vec_middle = middle_backward(
        behind(grad_pre, up[5]), w_up, grad_top, resid_mid, w_proj, vec_rows
    )
    slots.close(down, up, grad_mid, stats_all)

    down = OuterSum(scatter_second(down, slots))
    attn_got = swap_core(slots.open(grad_attn))
    ring_other = swap_core(slots.open(ring))
    grad_in, grad_rows, grad_packed, vec_first = attention_backward(
        grad_mixed, slots.open(grad_mid), packed, resid_in, w_qkv, vec_rows
    )
    slots.close(down.held, grad_rows, attn_got, ring_other)
    grad_in, vec_first = slots.open((grad_in, vec_first))

    norm_all = (stats_all[:, :, 0].reshape(1, -1) + math.log(token_count)).astype(jnp.float32)
    loss = jnp.sum(stats_all[:, :, 1]) / token_count
    targets_all = packed_all[:, seq_len:].reshape(1, -1)
    vec_grad = jnp.concatenate(
        [
            vec_first[0:2],
            vec_middle[0:2],
            vec_down[0:2],
            vec_first[2:4],
            vec_middle[2:3],
            vec_down[2:3],
            vec_up[0:4],
        ],
        axis=0,
    )
    vec_width = vectors.shape[1]
    vec_blocks = jnp.moveaxis(vec_grad.reshape(-1, device_count, vec_width), 1, 0)
    small_grad = jnp.concatenate(
        [grad_in.reshape(device_count, -1), vec_blocks.reshape(device_count, -1)], axis=1
    )
    small_grad = jnp.pad(small_grad, ((0, 0), (0, unit_rows * small_width - small_count)))
    small_grad = small_grad.reshape(-1, 2, unit_rows, small_width)
    small_sent = pick_half(small_grad, 1 - core, 1).astype(low)

    pieces = table_low.shape[0] // PIECE
    bounds = [0] + [round(pieces * share) for share in (0.3, 0.7, 0.9)] + [pieces]

    def head_part(earlier, part, mark):
        if bounds[part] == bounds[part + 1]:
            return (earlier, mark)
        return table_part(
            earlier,
            head_all,
            table_low,
            targets_all,
            behind(norm_all, mark),
            first_column,
            vocab_rows,
            1.0 / token_count,
            bounds[part],
            bounds[part + 1],
        )

    up = scatter_first(up, slots)
    packed_got = swap_core(slots.open(grad_packed))
    small_got = swap_core(slots.open(small_sent))
    small_sum = pick_half(small_grad, core, 1) + small_got.astype(jnp.float32)
    small_sum = small_sum.reshape(4, outer_count * unit_rows, small_width)
    small_sum = jnp.stack([pick_half(small_sum, dp_index ^ step, 0) for step in range(4)])
    head_all = place_blocks(slots.open(ring), ring_other, (width,))[0].reshape(-1, width)
    rows = OuterGather(slots.open(grad_rows))
    rows.advance(slots)
    slots.close(up[1:], packed_got, small_sum, rows.held, head_all)

    up = OuterSum(scatter_second(up, slots))
    rows_outer = rows.finish(slots)
    down.advance(slots)
    first = gradient_blocks(
        [lefts, lefts],
        left_spans[:2],
        [(grad_packed, slots.open(packed_got)), (grad_attn, attn_got)],
        small_sum,
        unit_rows,
    )
    table_grad, mark = head_part(None, 0, first[5])
    slots.close(up.held, first[5], rows_outer, down.held, mark)

    first = scatter_first(first, slots)
    rows_ring = ring_first(rows_outer, slots)
    up.advance(slots)
    table_grad, mark = head_part(table_grad, 1, slots.last)
    slots.close(first[1:], rows_ring, up.held, mark)

    first = scatter_second(first, slots)
    rows_held = ring_second(rows_ring, slots)
    up_own = up.finish(slots)
    table_grad, mark = head_part(table_grad, 2, slots.last)
    slots.close(first, up_own, rows_held, mark)

    first_terms = [pick_half(first, outer, 0)]
    for step in range(1, outer_count):
        sent = slots.open(pick_half(first, outer ^ step, 0).astype(low))
        first_terms.append(swap_outer(sent, step).astype(jnp.float32))
    first_own = tree_sum(first_terms)
    rows_other = swap_core(slots.open(rows_held))
    down_own = down.finish(slots)
    table_grad, mark = head_part(table_grad, 3, slots.last)
    small_own = first_own[:, 4 * width :].reshape(-1)
    gradients = (
        first_own[:, : 3 * width],
        first_own[:, 3 * width : 4 * width],
        up_own,
        down_own,
        small_own[: positions.size].reshape(positions.shape),
        small_own[positions.size : small_count].reshape(vectors.shape),
    )
    table_grad, sums = add_rows(
        table_grad, rows_held, rows_other, counts, row_list, token_list, gradients, weight_sums, dp_count
    )
    sums = sum_all(sums)
    grad_norm = jnp.sqrt(sums[0, 0])
    firsts, seconds = moments[:7], moments[7:]
    smalls = list(zip(small_masters, gradients, firsts, seconds))
    table_set = (table, table_grad, firsts[6], seconds[6])
    made, norms = update_norms(sums, smalls, table_set, dp_count)
    norms = sum_all(norms)
    ratios = jnp.sqrt(sums[0, 1:8]) / jnp.sqrt(norms[0, 1:8])
    written = write_updates(
        sums, norms, [(weight, group[2]) for weight, group in zip(small_masters, made)], table_set
    )
    new_weights = list(written[3:]) + [written[0]]
    new_firsts = [group[0] for group in made] + [written[1]]
    new_seconds = [group[1] for group in made] + [written[2]]
    return (loss, grad_norm, ratios, *new_weights, *new_firsts, *new_seconds)


def solution(mesh):
    rows = P(("dp", "vocab"), None)
    weights = (rows, rows, rows, rows, rows, P(None, ("dp", "vocab")), P("vocab", None))
    return jax.shard_map(
        shards,
        mesh=mesh,
        in_specs=(rows, rows, rows) + weights * 3,
        out_specs=(P(), P(), P()) + weights * 3,
        check_vma=False,
    )
```

```python
import functools
import math

import jax
import jax.numpy as jnp
from jax import lax
from jax.experimental import pallas as pl
from jax.experimental.pallas import tpu as pltpu
from jax.sharding import PartitionSpec as P

HD = 64
V_REAL = 50257
STEP = 5


LN_EPS = 1e-05
SMOOTHING = 0.1
BETA_ONE = 0.9
BETA_TWO = 0.999
ADAM_EPS = 1e-12
DECAY = 0.01
RATE = 0.3
CLIP_AT = 0.01
MASKED = -1e30
CHUNK = 1280
PIECE = 640
VMEM_BYTES = 58 * 2**20


def layer_norm(inputs, gain, shift):
    centre = jnp.mean(inputs, axis=-1, keepdims=True)
    centred = inputs - centre
    spread = jnp.mean(centred * centred, axis=-1, keepdims=True)
    return centred * lax.rsqrt(spread + LN_EPS) * gain + shift


def gelu_tanh(inputs):
    return (
        0.5
        * inputs
        * (1.0 + jnp.tanh(0.7978845608028654 * (inputs + 0.044715 * inputs * inputs * inputs)))
    )


def dot_plain(left_op, right_op):
    return jnp.dot(left_op, right_op, preferred_element_type=jnp.float32)


def dot_first(left_op, right_op):
    return lax.dot_general(
        left_op, right_op, (((0,), (0,)), ((), ())), preferred_element_type=jnp.float32
    )


def dot_second(left_op, right_op):
    return lax.dot_general(
        left_op, right_op, (((1,), (1,)), ((), ())), preferred_element_type=jnp.float32
    )


def params(limit=26 * 2**20):
    return pltpu.CompilerParams(vmem_limit_bytes=min(limit, VMEM_BYTES))


def cost(flops, bytes_accessed):
    return pl.CostEstimate(
        flops=int(flops), bytes_accessed=int(bytes_accessed), transcendentals=0
    )


def whole_block():
    return pl.BlockSpec(memory_space=pltpu.VMEM)


def shape_of(shape, dtype):
    return jax.ShapeDtypeStruct(tuple(shape), dtype)


def causal_scores(queries, keys, causal):
    return jnp.where(causal, dot_second(queries, keys) * HD ** (-0.5), MASKED)


def causal_mask(count):
    query = lax.broadcasted_iota(jnp.int32, (count, count), 0)
    key = lax.broadcasted_iota(jnp.int32, (count, count), 1)
    return key <= query


def head_span(head):
    return slice(head * HD, (head + 1) * HD)


def attention_forward(embedded, positions, vec_rows, w_qkv, w_proj, chooser):
    count, width = embedded.shape
    low = jnp.bfloat16

    half = width // 2

    def body(
        e_ref, p_ref, v_ref, qkv_ref, proj_ref, c_ref, x0_ref, packed_ref, x1_ref, h2_ref, own_ref, other_ref, o_ref
    ):
        x0 = e_ref[...] + p_ref[...].astype(jnp.float32)
        x0_ref[...] = x0
        h1 = layer_norm(x0, v_ref[0:1, :], v_ref[1:2, :]).astype(low)
        parts = []
        for place, bias in enumerate((6, None, 7)):
            span = slice(place * width, (place + 1) * width)
            part = dot_plain(h1, qkv_ref[:, span])
            if bias is not None:
                part = part + v_ref[bias : bias + 1, :]
            parts.append(part.astype(low))
            packed_ref[:, span] = parts[-1]
        queries, keys, values = parts
        causal = causal_mask(count)
        for head in range(0, width // HD, 2):
            mixed = []
            for one in (head, head + 1):
                span = head_span(one)
                scores = causal_scores(queries[:, span], keys[:, span], causal)
                grown = jnp.exp(scores - jnp.max(scores, axis=-1, keepdims=True))
                probs = (grown / jnp.sum(grown, axis=-1, keepdims=True)).astype(low)
                mixed.append(dot_plain(probs, values[:, span]))
            o_ref[:, head * HD : (head + 2) * HD] = jnp.concatenate(mixed, axis=1).astype(low)
        x1 = x0 + dot_plain(o_ref[...], proj_ref[...]) + v_ref[8:9, :]
        x1_ref[...] = x1
        h2 = layer_norm(x1, v_ref[2:3, :], v_ref[3:4, :]).astype(low)
        h2_ref[...] = h2
        for place, value in enumerate((h1, o_ref[...], h2)):
            span = slice(place * half, (place + 1) * half)
            own_ref[:, span] = dot_plain(value, c_ref[0]).astype(low)
            other_ref[:, span] = dot_plain(value, c_ref[1]).astype(low)

    shape = (count, width)
    return pl.pallas_call(
        body,
        out_shape=[
            shape_of(shape, jnp.float32),
            shape_of((count, 3 * width), low),
            shape_of(shape, jnp.float32),
            shape_of(shape, low),
            shape_of((count, 3 * half), low),
            shape_of((count, 3 * half), low),
        ],
        in_specs=[whole_block()] * 6,
        out_specs=[whole_block()] * 6,
        scratch_shapes=[pltpu.VMEM(shape, low)],
        compiler_params=params(),
        cost_estimate=cost(20 * count * width * width, 8 * width * width),
    )(embedded, positions, vec_rows, w_qkv, w_proj, chooser)


def hidden_forward(normed, vec_rows, w_up, chooser, dp_index):
    count, width = normed.shape
    blocks = len(w_up)
    hidden = blocks * width
    half = width // 2
    low = jnp.bfloat16

    def body(dp_ref, h_ref, v_ref, c_ref, *refs):
        w_refs = refs[:blocks]
        pre_ref, act_ref, own_ref, other_ref = refs[blocks:]
        for place in range(blocks):
            span = slice(place * width, (place + 1) * width)
            pre = dot_plain(h_ref[...], w_refs[place][...]) + v_ref[10 + place : 11 + place, :]
            pre_ref[:, span] = pre
            act_ref[:, span] = gelu_tanh(pre).astype(low)
        for place in range(blocks):
            source = pl.multiple_of((dp_ref[0] ^ place) * width, width)
            part = act_ref[:, pl.ds(source, width)]
            span = slice(place * half, (place + 1) * half)
            own_ref[:, span] = dot_plain(part, c_ref[0]).astype(low)
            other_ref[:, span] = dot_plain(part, c_ref[1]).astype(low)

    return pl.pallas_call(
        body,
        out_shape=[
            shape_of((count, hidden), jnp.float32),
            shape_of((count, hidden), low),
            shape_of((count, hidden // 2), low),
            shape_of((count, hidden // 2), low),
        ],
        in_specs=[pl.BlockSpec(memory_space=pltpu.SMEM)] + [whole_block()] * (3 + blocks),
        out_specs=[whole_block()] * 4,
        compiler_params=params(),
        cost_estimate=cost(3 * count * width * hidden, 2 * width * hidden),
    )(dp_index, normed, vec_rows, chooser, *w_up)


def output_forward(act, w_down, resid_mid, vec_rows, picks):
    count, width = resid_mid.shape
    number = picks.shape[0]

    def body(act_ref, w_ref, x1_ref, v_ref, pick_ref, x2_ref, out_ref):
        x2 = x1_ref[...] + dot_plain(act_ref[...], w_ref[...]) + v_ref[9:10, :]
        x2_ref[...] = x2
        final = layer_norm(x2, v_ref[4:5, :], v_ref[5:6, :]).astype(jnp.bfloat16)
        hot = pick_ref[...] == lax.broadcasted_iota(jnp.int32, (number, count), 1)
        hot = jnp.where(hot, 1.0, 0.0).astype(jnp.bfloat16)
        out_ref[...] = dot_plain(hot, final).astype(jnp.bfloat16)

    return pl.pallas_call(
        body,
        out_shape=[
            shape_of((count, width), jnp.float32),
            shape_of((number, width), jnp.bfloat16),
        ],
        in_specs=[whole_block()] * 5,
        out_specs=[whole_block()] * 2,
        compiler_params=params(),
        cost_estimate=cost(2 * act.size * width, 2 * w_down.size),
    )(act, w_down, resid_mid, vec_rows, picks)


def norm_backward(grad, inputs, gain):
    centred = inputs - jnp.mean(inputs, axis=-1, keepdims=True)
    scale = lax.rsqrt(jnp.mean(centred * centred, axis=-1, keepdims=True) + LN_EPS)
    normed = centred * scale
    scaled = grad * gain
    back = scale * (
        scaled
        - jnp.mean(scaled, axis=-1, keepdims=True)
        - normed * jnp.mean(scaled * normed, axis=-1, keepdims=True)
    )
    return (
        back,
        jnp.sum(grad * normed, axis=0, keepdims=True),
        jnp.sum(grad, axis=0, keepdims=True),
    )


def column_sum(value):
    return jnp.sum(value.astype(jnp.float32), axis=0, keepdims=True)


def choosers(width, rows, core, dp_index=None):
    column = jnp.arange(width, dtype=jnp.int32)
    target = jnp.arange(width // 2, dtype=jnp.int32)
    block = target // rows
    if dp_index is not None:
        per = width // (8 * rows)
        block = ((block // per) ^ dp_index) * per + block % per
    made = []
    for side in (core, 1 - core):
        source = (block * 2 + side) * rows + target % rows
        made.append((column[:, None] == source[None, :]).astype(jnp.bfloat16))
    return jnp.stack(made)


def gradient_blocks(lefts, spans, rights, smalls, name_rows):
    widths = [right[0].shape[1] for right in rights]
    total = sum(widths) + (smalls.shape[2] if smalls is not None else 0)
    arrays = [value for pair in zip(lefts, rights) for group in pair for value in group]
    if smalls is not None:
        arrays.append(smalls)
    number = len(lefts)
    rows = (spans[0][1] - spans[0][0]) // 4
    half = rows // 2
    low = jnp.bfloat16

    def body(*refs):
        in_refs, out_refs = refs[: len(arrays)], refs[len(arrays) :]

        def put(made, span):
            own, one, two, three = [made(place) for place in range(4)]
            out_refs[0][:, span] = own
            out_refs[1][:, span] = one[:half].astype(low)
            out_refs[2][:, span] = one[half:]
            out_refs[3][:, span] = two[:half]
            out_refs[4][:, span] = two[half:].astype(low)
            out_refs[5][:, span] = three[:half].astype(low)
            out_refs[6][:, span] = three[half:].astype(low)

        start = 0
        for index in range(number):
            left_a, left_b, right_a, right_b = in_refs[4 * index : 4 * index + 4]
            columns = slice(*spans[index])
            left = jnp.concatenate([left_a[:, columns], left_b[:, columns]], axis=0)
            for begin in range(0, widths[index], 768):
                stop = min(begin + 768, widths[index])
                right = jnp.concatenate([right_a[:, begin:stop], right_b[:, begin:stop]], axis=0)
                result = dot_first(left, right)
                put(
                    lambda place, result=result: result[place * rows : (place + 1) * rows],
                    slice(start + begin, start + stop),
                )
            start += widths[index]
        if smalls is not None:
            put(lambda place: in_refs[-1][place], slice(start, total))

    out = [shape_of((rows, total), jnp.float32)]
    out += [shape_of((half, total), kind) for kind in (low, jnp.float32, jnp.float32, low, low, low)]
    flops = sum(4 * left[0].shape[0] * 4 * rows * right[0].shape[1] for left, right in zip(lefts, rights))
    made = pl.pallas_call(
        body,
        out_shape=out,
        in_specs=[whole_block()] * len(arrays),
        out_specs=[whole_block()] * 7,
        compiler_params=params(),
        cost_estimate=cost(flops, 14 * rows * total),
    )(*arrays)
    return [value.reshape(-1, name_rows, total) for value in made]


def split_three(value):
    low = jnp.bfloat16
    first = value.astype(low)
    rest = value - first.astype(jnp.float32)
    second = rest.astype(low)
    return (first, second, (rest - second.astype(jnp.float32)).astype(low))


def pack_stats(top, total):
    lane = lax.broadcasted_iota(jnp.int32, (top.shape[0], 128), 1)
    tile = jnp.zeros((top.shape[0], 128), jnp.float32)
    for place, part in enumerate(split_three(top) + split_three(total)):
        tile = jnp.where(lane == place, part.astype(jnp.float32), tile)
    return tile.astype(jnp.bfloat16)


def unpack_stats(tile):
    wide = tile.astype(jnp.float32)
    return (
        wide[:, 0:1] + (wide[:, 1:2] + wide[:, 2:3]),
        wide[:, 3:4] + (wide[:, 4:5] + wide[:, 5:6]),
    )


def join(one, two):
    top = jnp.maximum(one[1], two[1])
    scale_one, scale_two = jnp.exp(one[1] - top), jnp.exp(two[1] - top)
    return (
        one[0] * scale_one + two[0] * scale_two,
        top,
        one[2] * scale_one + two[2] * scale_two,
    )


def unpack_rows(packed, width):
    top, total = unpack_stats(packed[:, width:])
    return (packed[:, :width].astype(jnp.float32), top, total)


def head_pass(head_in, table_low, here, rows, pick_count):
    count, width = head_in.shape
    chunks = table_low.shape[0] // CHUNK
    groups = count // (2 * pick_count)
    half = count // 2

    def body(here_ref, head_ref, table_ref, own_ref, stat_ref, sent_ref, acc_ref, tops_ref):
        head = head_ref[...]
        real = jnp.minimum(rows, V_REAL - here_ref[0])
        acc_ref[...] = jnp.zeros_like(acc_ref)

        def step(index, carry, masked):
            top, total = carry
            begin = pl.multiple_of(index * CHUNK, CHUNK)
            part = table_ref[pl.ds(begin, CHUNK), :]
            values = dot_second(head, part)
            if masked:
                local = lax.broadcasted_iota(jnp.int32, (1, CHUNK), 1) + begin
                values = jnp.where(local < real, values, MASKED)
            higher = jnp.maximum(top, jnp.max(values, axis=1, keepdims=True))
            grown = jnp.exp(values - higher)
            scale = jnp.exp(top - higher)
            acc_ref[...] = acc_ref[...] * scale + dot_plain(grown.astype(jnp.bfloat16), part)
            return (higher, total * scale + jnp.sum(grown, axis=1, keepdims=True))

        carry = (jnp.full((count, 1), MASKED, jnp.float32), jnp.zeros((count, 1), jnp.float32))
        unmasked = jnp.maximum(real, 0) // CHUNK
        carry = lax.fori_loop(0, unmasked, functools.partial(step, masked=False), carry)
        top, total = lax.fori_loop(unmasked, chunks, functools.partial(step, masked=True), carry)
        lane = lax.broadcasted_iota(jnp.int32, (count, 128), 1)
        tops_ref[...] = jnp.where(lane == 0, top, jnp.where(lane == 1, total, 0.0))
        for group in range(groups):
            own = pl.multiple_of((2 * group + here_ref[1]) * pick_count, pick_count)
            other = pl.multiple_of((2 * group + 1 - here_ref[1]) * pick_count, pick_count)
            span = slice(group * pick_count, (group + 1) * pick_count)
            own_ref[span, :] = acc_ref[pl.ds(own, pick_count), :]
            stat_ref[span, :] = tops_ref[pl.ds(own, pick_count), :]
            sent_ref[span, :width] = acc_ref[pl.ds(other, pick_count), :].astype(jnp.bfloat16)
            stats = tops_ref[pl.ds(other, pick_count), :]
            sent_ref[span, width:] = pack_stats(stats[:, 0:1], stats[:, 1:2])

    return pl.pallas_call(
        body,
        out_shape=[
            shape_of((half, width), jnp.float32),
            shape_of((half, 128), jnp.float32),
            shape_of((half, width + 128), jnp.bfloat16),
        ],
        in_specs=[pl.BlockSpec(memory_space=pltpu.SMEM)] + [whole_block()] * 2,
        out_specs=[whole_block()] * 3,
        scratch_shapes=[pltpu.VMEM((count, width), jnp.float32), pltpu.VMEM((count, 128), jnp.float32)],
        compiler_params=params(VMEM_BYTES),
        cost_estimate=cost(4 * table_low.size * count, 2 * table_low.size),
    )(here, head_in, table_low)


def join_cores(own, stats, received, outer, pick_count):
    half, width = own.shape
    groups = half // pick_count

    def body(outer_ref, own_ref, stat_ref, received_ref, rows_ref, out_stat_ref, *sent_refs):
        for step in range(groups):
            start = pl.multiple_of((outer_ref[0] ^ step) * pick_count, pick_count)
            span = pl.ds(start, pick_count)
            stat = stat_ref[span, :]
            one = (own_ref[span, :], stat[:, 0:1], stat[:, 1:2])
            value, top, total = join(one, unpack_rows(received_ref[span, :], width))
            if step:
                sent_refs[step - 1][:, :width] = value.astype(jnp.bfloat16)
                sent_refs[step - 1][:, width:] = pack_stats(top, total)
            else:
                lane = lax.broadcasted_iota(jnp.int32, (pick_count, 128), 1)
                rows_ref[...] = value
                out_stat_ref[...] = jnp.where(lane == 0, top, jnp.where(lane == 1, total, 0.0))

    return pl.pallas_call(
        body,
        out_shape=[
            shape_of((pick_count, width), jnp.float32),
            shape_of((pick_count, 128), jnp.float32),
        ]
        + [shape_of((pick_count, width + 128), jnp.bfloat16)] * (groups - 1),
        in_specs=[pl.BlockSpec(memory_space=pltpu.SMEM)] + [whole_block()] * 3,
        out_specs=[whole_block()] * (groups + 1),
        compiler_params=params(),
        cost_estimate=cost(4 * own.size, 8 * own.size),
    )(outer, own, stats, received)


def output_backward(rows, stats, received, picked, target_rows, row_sum, picks, resid_out, vec_rows, token_count):
    count, width = resid_out.shape
    number = picks.shape[0]
    low = jnp.bfloat16
    others = len(received)

    def body(rows_ref, stat_ref, *refs):
        received_refs = refs[:others]
        f_ref, t_ref, sum_ref, pick_ref, x_ref, v_ref, dx_ref, dy_ref, vec_ref, norm_ref = refs[others:]
        stat = stat_ref[...]
        value = (rows_ref[...], stat[:, 0:1], stat[:, 1:2])
        for ref in received_refs:
            value = join(value, unpack_rows(ref[...], width))
        mean, top, total = value
        target = t_ref[...]
        final = f_ref[...].astype(jnp.float32)
        norm = top + jnp.log(total)
        hit = jnp.sum(final * target, axis=1, keepdims=True)
        plain = jnp.sum(final * sum_ref[...], axis=1, keepdims=True)
        loss = (1.0 - SMOOTHING) * (norm - hit) + SMOOTHING * (norm - plain / V_REAL)
        lane = lax.broadcasted_iota(jnp.int32, (number, 128), 1)
        norm_ref[...] = jnp.where(lane == 0, norm, jnp.where(lane == 1, loss, 0.0))
        soft = jnp.exp(hit - norm)
        whole = ((soft - (1.0 - SMOOTHING) - SMOOTHING / V_REAL) / token_count).astype(low)
        factor = whole.astype(jnp.float32) - (soft - SMOOTHING / V_REAL) / token_count
        picked_grad = (
            mean * (1.0 / token_count) / total
            - sum_ref[...] * (SMOOTHING / V_REAL / token_count)
            + target * factor
        )
        hot = pick_ref[...] == lax.broadcasted_iota(jnp.int32, (number, count), 1)
        final_grad = lax.dot_general(
            jnp.where(hot, 1.0, 0.0),
            picked_grad,
            (((0,), (0,)), ((), ())),
            precision=lax.Precision.HIGHEST,
            preferred_element_type=jnp.float32,
        )
        back, gain, shift = norm_backward(final_grad, x_ref[...], v_ref[4:5, :])
        dx_ref[...] = back
        dy = back.astype(low)
        dy_ref[...] = dy
        vec_ref[0:1, :] = gain
        vec_ref[1:2, :] = shift
        vec_ref[2:3, :] = column_sum(dy)
        vec_ref[3:8, :] = jnp.zeros((5, width), jnp.float32)

    return pl.pallas_call(
        body,
        out_shape=[
            shape_of((count, width), jnp.float32),
            shape_of((count, width), low),
            shape_of((8, width), jnp.float32),
            shape_of((number, 128), jnp.float32),
        ],
        in_specs=[whole_block()] * (8 + others),
        out_specs=[whole_block()] * 4,
        compiler_params=params(),
        cost_estimate=cost(20 * count * width, 20 * count * width),
    )(rows, stats, *received, picked, target_rows, row_sum, picks, resid_out, vec_rows)


def hidden_backward(dy, w_down, pre):
    count, width = dy.shape
    hidden = pre.shape[1]
    low = jnp.bfloat16

    def body(dy_ref, w_ref, pre_ref, dpre_ref, vec_ref):
        vec_ref[...] = jnp.zeros_like(vec_ref)
        for place in range(hidden // width):
            span = slice(place * width, (place + 1) * width)
            grad = dot_second(dy_ref[...], w_ref[span, :])
            u = pre_ref[:, span]
            bent = jnp.tanh(0.7978845608028654 * (u + 0.044715 * u * u * u))
            slope = 0.5 * (1.0 + bent) + 0.5 * u * (1.0 - bent * bent) * (
                0.7978845608028654 * (1.0 + 3.0 * 0.044715 * u * u)
            )
            dpre = (grad * slope).astype(low)
            dpre_ref[:, span] = dpre
            vec_ref[place : place + 1, :] = column_sum(dpre)

    return pl.pallas_call(
        body,
        out_shape=[shape_of((count, hidden), low), shape_of((8, width), jnp.float32)],
        in_specs=[whole_block()] * 3,
        out_specs=[whole_block()] * 2,
        compiler_params=params(),
        cost_estimate=cost(2 * count * width * hidden, 2 * width * hidden),
    )(dy, w_down, pre)


def middle_backward(dpre, w_up, dx2, x1, w_proj, vec_rows):
    count, width = x1.shape
    low = jnp.bfloat16

    blocks = len(w_up)

    def body(dpre_ref, dx2_ref, x1_ref, proj_ref, v_ref, *refs):
        up_refs = refs[:blocks]
        dx1_ref, da_ref, mixed_ref, vec_ref = refs[blocks:]
        dh2 = jnp.zeros((count, width), jnp.float32)
        for place in range(blocks):
            span = slice(place * width, (place + 1) * width)
            dh2 = dh2 + dot_second(dpre_ref[:, span], up_refs[place][...])
        back, gain, shift = norm_backward(dh2, x1_ref[...], v_ref[2:3, :])
        dx1 = back + dx2_ref[...]
        dx1_ref[...] = dx1
        da = dx1.astype(low)
        da_ref[...] = da
        vec_ref[0:1, :] = gain
        vec_ref[1:2, :] = shift
        vec_ref[2:3, :] = column_sum(da)
        vec_ref[3:8, :] = jnp.zeros((5, width), jnp.float32)
        mixed_ref[...] = dot_second(da, proj_ref[...]).astype(low)

    return pl.pallas_call(
        body,
        out_shape=[
            shape_of((count, width), jnp.float32),
            shape_of((count, width), low),
            shape_of((count, width), low),
            shape_of((8, width), jnp.float32),
        ],
        in_specs=[whole_block()] * (5 + blocks),
        out_specs=[whole_block()] * 4,
        compiler_params=params(),
        cost_estimate=cost(10 * count * width * width, 10 * width * width),
    )(dpre, dx2, x1, w_proj, vec_rows, *w_up)


def attention_backward(mixed, dx1, packed, x0, w_qkv, vec_rows):
    count, width = x0.shape
    low = jnp.bfloat16

    def body(mixed_ref, dx1_ref, packed_ref, x0_ref, qkv_ref, v_ref, dx0_ref, rows_ref, grad_ref, vec_ref):
        causal = causal_mask(count)
        for head in range(0, width // HD, 2):
            sides = ([], [], [])
            for one in (head, head + 1):
                queries = packed_ref[:, one * HD : (one + 1) * HD]
                keys = packed_ref[:, width + one * HD : width + (one + 1) * HD]
                values = packed_ref[:, 2 * width + one * HD : 2 * width + (one + 1) * HD]
                scores = causal_scores(queries, keys, causal)
                grown = jnp.exp(scores - jnp.max(scores, axis=-1, keepdims=True))
                probs = grown / jnp.sum(grown, axis=-1, keepdims=True)
                out_grad = mixed_ref[:, one * HD : (one + 1) * HD]
                grad_p = dot_second(out_grad, values)
                centre = jnp.sum(probs * grad_p, axis=-1, keepdims=True)
                grad_s = (probs * (grad_p - centre)).astype(low)
                sides[0].append(dot_plain(grad_s, keys) * HD ** (-0.5))
                sides[1].append(dot_first(grad_s, queries) * HD ** (-0.5))
                sides[2].append(dot_first(probs.astype(low), out_grad))
            for place, side in enumerate(sides):
                start = place * width + head * HD
                grad_ref[:, start : start + 2 * HD] = jnp.concatenate(side, axis=1).astype(low)
        dh1 = dot_second(grad_ref[...], qkv_ref[...])
        back, gain, shift = norm_backward(dh1, x0_ref[...], v_ref[0:1, :])
        vec_ref[0:1, :] = gain
        vec_ref[1:2, :] = shift
        vec_ref[2:3, :] = column_sum(grad_ref[:, :width])
        vec_ref[3:4, :] = column_sum(grad_ref[:, 2 * width :])
        vec_ref[4:8, :] = jnp.zeros((4, width), jnp.float32)
        dx0 = back + dx1_ref[...]
        dx0_ref[...] = dx0
        rows_ref[...] = dx0.astype(low)

    return pl.pallas_call(
        body,
        out_shape=[
            shape_of((count, width), jnp.float32),
            shape_of((count, width), low),
            shape_of((count, 3 * width), low),
            shape_of((8, width), jnp.float32),
        ],
        in_specs=[whole_block()] * 6,
        out_specs=[whole_block()] * 4,
        compiler_params=params(),
        cost_estimate=cost(16 * count * width * width, 10 * width * width),
    )(mixed, dx1, packed, x0, w_qkv, vec_rows)


def bit_of(index, level):
    return (index >> level) & 1


def xor_order(parts, index):
    level = 0
    while (1 << level) < len(parts):
        odd = bit_of(index, level) == 1
        step = 1 << level
        placed = list(parts)
        for place in range(len(parts)):
            if not place & step:
                low, high = parts[place], parts[place | step]
                placed[place] = jnp.where(odd, high, low)
                placed[place | step] = jnp.where(odd, low, high)
        parts = placed
        level += 1
    return parts


def tree_sum(parts):
    while len(parts) > 1:
        parts = [parts[place] + parts[place + 1] for place in range(0, len(parts), 2)]
    return parts[0]


def swap_core(value):
    count = lax.axis_size("vocab")
    return lax.ppermute(value, "vocab", [(i, i ^ 1) for i in range(count)])


def swap_outer(value, step):
    count = lax.axis_size("vocab")
    return lax.ppermute(value, "vocab", [(i, i ^ (2 * step)) for i in range(count)])


def swap_dp(value, step):
    count = lax.axis_size("dp")
    return lax.ppermute(value, "dp", [(i, i ^ step) for i in range(count)])


def places():
    vocab_index = lax.axis_index("vocab")
    return (lax.axis_index("dp"), vocab_index // 2, vocab_index % 2)


def gather_vocab(value):
    _, outer, core = places()
    pair = jnp.stack(xor_order([value, swap_core(value)], core))
    count = lax.axis_size("vocab") // 2
    parts = [pair] + [swap_outer(pair, step) for step in range(1, count)]
    return jnp.concatenate(xor_order(parts, outer), axis=0)


def gather_dp(value):
    dp_index, _, _ = places()
    parts = [value] + [swap_dp(value, step) for step in range(1, lax.axis_size("dp"))]
    return jnp.stack(xor_order(parts, dp_index))


def sum_all(value):
    value = value + swap_core(value)
    value = tree_sum([value] + [swap_dp(value, step) for step in range(1, lax.axis_size("dp"))])
    return tree_sum(outer_parts(value))


def outer_parts(value):
    count = lax.axis_size("vocab") // 2
    return [value] + [swap_outer(value, step) for step in range(1, count)]


def behind(value, *others):
    return lax.optimization_barrier((value, others))[0]


class Slots:
    def __init__(self):
        self.last = None

    def open(self, value):
        return value if self.last is None else behind(value, self.last)

    def close(self, *results):
        self.last = results


class OuterGather:
    def __init__(self, value):
        self.held = value[None]

    def advance(self, slots):
        count = lax.axis_size("vocab") // 2
        step = count // (2 * self.held.shape[0])
        if step:
            shape = (-1,) + self.held.shape[1:]
            held = slots.open(self.held)
            self.held = jnp.stack([held, swap_outer(held, step)], axis=1).reshape(shape)

    def finish(self, slots):
        while self.held.shape[0] < lax.axis_size("vocab") // 2:
            self.advance(slots)
        return self.held


def ring_first(held, slots):
    held = slots.open(held)
    return (held, swap_dp(held, 1), swap_dp(held, 2))


def ring_second(parts, slots):
    held, from_one, from_two = parts
    half = held.shape[0] // 2
    low, high = slots.open((from_two[:half], from_one[half:]))
    return jnp.concatenate([held, from_one, from_two, swap_dp(low, 1), swap_dp(high, 2)], axis=0)


def place_blocks(held, other, cuts):
    dp_index, outer, core = places()
    count = held.shape[0]
    outer_count = lax.axis_size("vocab") // 2
    here = jnp.stack([dp_index, outer, core]).astype(jnp.int32)
    if held.ndim == 3:
        spans, shapes = [], []
        for width in cuts:
            spans.append((sum(w for _, w in spans), width))
            shapes.append((held.shape[1], width))

        def take(ref, block, index):
            return ref.at[block, :, pl.ds(*spans[index])]

    else:
        shapes = [
            held.shape[2:] if isinstance(one, int) else (one[1] - one[0],) + held.shape[2:]
            for one in cuts
        ]

        def take(ref, block, index):
            one = cuts[index]
            if isinstance(one, int):
                return ref.at[block, one]
            return ref.at[block, pl.ds(one[0], one[1] - one[0])]


    def body(here_ref, held_ref, other_ref, *refs):
        out_refs, sems = refs[: len(cuts)], refs[len(cuts)]

        def copies(block):
            dp_place = (block // outer_count) ^ here_ref[0]
            outer_place = (block % outer_count) ^ here_ref[1]
            target = (dp_place * outer_count + outer_place) * 2
            made = []
            for side, ref in enumerate((held_ref, other_ref)):
                place = target + (here_ref[2] ^ side)
                for index in range(len(cuts)):
                    made.append(
                        pltpu.make_async_copy(
                            take(ref, block, index),
                            out_refs[index].at[place],
                            sems.at[index, side, block],
                        )
                    )
            return made

        def start(block, carry):
            for copy in copies(block):
                copy.start()
            return carry

        def wait(block, carry):
            for copy in copies(block):
                copy.wait()
            return carry

        lax.fori_loop(0, count, start, 0)
        lax.fori_loop(0, count, wait, 0)

    any_space = pl.BlockSpec(memory_space=pl.ANY)
    return pl.pallas_call(
        body,
        out_shape=[
            jax.ShapeDtypeStruct((2 * count,) + tuple(shape), held.dtype) for shape in shapes
        ],
        in_specs=[pl.BlockSpec(memory_space=pltpu.SMEM), any_space, any_space],
        out_specs=[pl.BlockSpec(memory_space=pltpu.VMEM) for _ in cuts],
        scratch_shapes=[pltpu.SemaphoreType.DMA((len(cuts), 2, count))],
        compiler_params=params(),
        cost_estimate=pl.CostEstimate(
            flops=0, bytes_accessed=4 * held.size * held.dtype.itemsize, transcendentals=0
        ),
    )(here, held, other)


def tile_of(values):
    row = lax.broadcasted_iota(jnp.int32, (8, 128), 0)
    lane = lax.broadcasted_iota(jnp.int32, (8, 128), 1)
    tile = jnp.zeros((8, 128), jnp.float32)
    for place, value in enumerate(values):
        if value is not None:
            tile = jnp.where((row == 0) & (lane == place), value, tile)
    return tile


def total_of(value):
    return jnp.sum(jnp.sum(value, axis=1, keepdims=True), axis=0, keepdims=True)


def fold_rows(value):
    return jnp.sum(value.reshape(-1, 8, value.shape[1]), axis=0)


def prepare_table(table, smalls, dp_count, first):
    rows, width = table.shape
    chunks = -(-rows // CHUNK)
    per = max(n for n in range(1, 9) if chunks % n == 0 and n * CHUNK <= rows)
    tile = per * CHUNK
    steps = chunks // per

    def body(first_ref, table_ref, *refs):
        small_refs, (low_ref, sum_ref, row_ref, acc_ref) = refs[: len(smalls)], refs[len(smalls) :]
        step = pl.program_id(0)
        row = lax.broadcasted_iota(jnp.int32, (tile, 1), 0) + step * tile
        value = jnp.where(row < rows, table_ref[...], 0.0)
        rounded = value.astype(jnp.bfloat16)
        low_ref[...] = rounded
        part = fold_rows(value * value)
        whole = jnp.where(row + first_ref[0] < V_REAL, rounded.astype(jnp.float32), 0.0)
        whole = jnp.sum(fold_rows(whole), axis=0, keepdims=True)

        @pl.when(step == 0)
        def _():
            acc_ref[...] = part
            row_ref[...] = whole

        @pl.when(step > 0)
        def _():
            acc_ref[...] += part
            row_ref[...] += whole

        @pl.when(step == steps - 1)
        def _():
            terms = [None] + [total_of(ref[...] * ref[...]) for ref in small_refs]
            terms.append(total_of(acc_ref[...]) / dp_count)
            sum_ref[...] = tile_of(terms)

    return pl.pallas_call(
        body,
        grid=(steps,),
        out_shape=[
            jax.ShapeDtypeStruct((chunks * CHUNK, width), jnp.bfloat16),
            jax.ShapeDtypeStruct((8, 128), jnp.float32),
            jax.ShapeDtypeStruct((1, width), jnp.float32),
        ],
        in_specs=[pl.BlockSpec(memory_space=pltpu.SMEM), pl.BlockSpec((tile, width), lambda i: (i, 0))]
        + [whole_block() for _ in smalls],
        out_specs=[pl.BlockSpec((tile, width), lambda i: (i, 0)), whole_block(), whole_block()],
        scratch_shapes=[pltpu.VMEM((8, width), jnp.float32)],
        compiler_params=pltpu.CompilerParams(vmem_limit_bytes=VMEM_BYTES),
        cost_estimate=pl.CostEstimate(
            flops=4 * table.size, bytes_accessed=6 * table.size, transcendentals=0
        ),
    )(first, table, *smalls)


def logit_grad(values, columns, norms, targets, scale):
    drop = jnp.where(
        columns == targets,
        scale * (1.0 - SMOOTHING + SMOOTHING / V_REAL),
        scale * (SMOOTHING / V_REAL),
    )
    return jnp.exp(values - norms) - drop


def table_part(earlier, head_all, table_low, targets, norms, first, rows, scale, start, stop):
    count, width = head_all.shape
    block = min(512, count)

    def body(first_ref, head_ref, table_ref, target_ref, norm_ref, *refs):
        out_ref, done_ref = refs[-2:]
        done_ref[...] = jnp.zeros_like(done_ref)
        begin = (pl.program_id(0) + start) * PIECE
        real = jnp.minimum(rows, V_REAL - first_ref[0])
        part = table_ref[...]
        local = lax.broadcasted_iota(jnp.int32, (PIECE, 1), 0) + begin
        columns = local + first_ref[0]

        def total_of_blocks(masked):
            total = jnp.zeros((PIECE, width), jnp.float32)
            for place in range(0, count, block):
                span = slice(place, place + block)
                head = head_ref[span, :]
                grad = logit_grad(
                    dot_second(part, head), columns, norm_ref[:, span], target_ref[:, span], scale
                )
                if masked:
                    grad = jnp.where(local < real, grad, 0.0)
                total = total + dot_plain(grad.astype(jnp.bfloat16), head)
            return total

        @pl.when(begin + PIECE <= real)
        def _():
            out_ref[...] = total_of_blocks(False)

        @pl.when(begin + PIECE > real)
        def _():
            out_ref[...] = total_of_blocks(True)

    args = [first, head_all, table_low, targets, norms]
    specs = [
        pl.BlockSpec(memory_space=pltpu.SMEM),
        whole_block(),
        pl.BlockSpec((PIECE, width), lambda i: (i + start, 0)),
        whole_block(),
        whole_block(),
    ]
    aliases = {}
    if earlier is not None:
        aliases = {len(args): 0}
        args.append(earlier)
        specs.append(pl.BlockSpec(memory_space=pl.ANY))
    size = (stop - start) * PIECE
    return pl.pallas_call(
        body,
        grid=(stop - start,),
        out_shape=[
            jax.ShapeDtypeStruct(table_low.shape, jnp.float32),
            jax.ShapeDtypeStruct((8, 128), jnp.float32),
        ],
        in_specs=specs,
        out_specs=[pl.BlockSpec((PIECE, width), lambda i: (i + start, 0)), whole_block()],
        input_output_aliases=aliases,
        compiler_params=params(20 * 2**20 + 4 * head_all.size),
        cost_estimate=pl.CostEstimate(
            flops=4 * size * width * count,
            bytes_accessed=6 * size * width,
            transcendentals=size * count,
        ),
    )(*args)


def token_lists(ids, first, rows, cap, bands):
    local = ids - first
    mine = (local >= 0) & (local < rows)
    tokens = jnp.arange(ids.shape[1], dtype=jnp.int32)
    band = local // CHUNK
    key = jnp.where(mine, band * ids.shape[1] + tokens[None, :], bands * ids.shape[1])
    slot = jnp.sum((key[:, None, :] < key[:, :, None]).astype(jnp.int32), axis=2)
    slots = jnp.arange(cap, dtype=jnp.int32)
    hot = (slot[:, None, :] == slots[None, :, None]) & mine[:, None, :]
    row = jnp.sum(jnp.where(hot, local[:, None, :], 0), axis=2)
    token = jnp.sum(jnp.where(hot, tokens[None, None, :], 0), axis=2)
    upto = jnp.arange(bands, dtype=jnp.int32)
    ends = (band[:, None, :] <= upto[None, :, None]) & mine[:, None, :]
    return (jnp.sum(ends.astype(jnp.int32), axis=2), row, token)


def add_rows(table_grad, held, other, ends, row_list, token_list, gradients, weight_sums, dp_count):
    padded, width = table_grad.shape
    dp_index, outer, core = places()
    here = jnp.stack([dp_index, outer, core]).astype(jnp.int32)
    outer_count = lax.axis_size("vocab") // 2
    sequences, bands = ends.shape
    tokens = held.shape[1]
    cap = row_list.shape[1]
    fine = 256
    per = CHUNK // fine
    kept = sequences if sequences * tokens * width * 4 <= 2**24 else 1

    def body(here_ref, end_ref, row_ref, token_ref, grad_in_ref, held_ref, other_ref, sums_ref, *refs):
        small_refs = refs[: len(gradients)]
        grad_out_ref, total_ref, grad_ref, rows_ref, in_sems, out_sems = refs[len(gradients) :]

        def in_copy(index):
            span = pl.ds(pl.multiple_of(index * CHUNK, CHUNK), CHUNK)
            return pltpu.make_async_copy(grad_in_ref.at[span], grad_ref.at[span], in_sems.at[index])

        def out_copy(index):
            span = pl.ds(pl.multiple_of(index * CHUNK, CHUNK), CHUNK)
            return pltpu.make_async_copy(grad_ref.at[span], grad_out_ref.at[span], out_sems.at[index])

        for index in range(bands):
            in_copy(index).start()
        clip = jnp.zeros((1, 1), jnp.float32)
        for ref in small_refs:
            clip = clip + total_of(ref[...] * ref[...])

        def widen(index, carry):
            dp_place = (index // 2) // outer_count
            outer_place = (index // 2) % outer_count
            block = (dp_place ^ here_ref[0]) * outer_count + (outer_place ^ here_ref[1])
            span = pl.ds(pl.multiple_of(index % kept * tokens, tokens), tokens)

            @pl.when(index % 2 == here_ref[2])
            def _():
                rows_ref[span, :] = held_ref[block].astype(jnp.float32)

            @pl.when(index % 2 != here_ref[2])
            def _():
                rows_ref[span, :] = other_ref[block].astype(jnp.float32)

            return carry

        if kept > 1:
            lax.fori_loop(0, sequences, widen, 0)
        acc = jnp.zeros((8, width), jnp.float32)
        for band in range(bands):
            in_copy(band).wait()

            def sequence(index, carry, band=band):
                if kept == 1:
                    widen(index, 0)

                def one(slot, carry):
                    row = row_ref[index * cap + slot]
                    token = index % kept * tokens + token_ref[index * cap + slot]
                    grad_ref[pl.ds(row, 1), :] += rows_ref[pl.ds(token, 1), :]
                    return carry

                begin = end_ref[index * bands + band - 1] if band else 0
                lax.fori_loop(begin, end_ref[index * bands + band], one, 0)
                return carry

            lax.fori_loop(0, sequences, sequence, 0)
            out_copy(band).start()

            def square(index, acc, band=band):
                span = pl.ds(pl.multiple_of(band * CHUNK + index * fine, fine), fine)
                value = grad_ref[span, :]
                return acc + fold_rows(value * value)

            acc = lax.fori_loop(0, per, square, acc)
        total_ref[...] = sums_ref[...] + tile_of([clip + total_of(acc) / dp_count])
        for band in range(bands):
            out_copy(band).wait()

    smem = pl.BlockSpec(memory_space=pltpu.SMEM)
    any_space = pl.BlockSpec(memory_space=pl.ANY)
    return pl.pallas_call(
        body,
        out_shape=[
            jax.ShapeDtypeStruct(table_grad.shape, jnp.float32),
            jax.ShapeDtypeStruct((8, 128), jnp.float32),
        ],
        in_specs=[smem, smem, smem, smem, any_space, whole_block(), whole_block(), whole_block()]
        + [whole_block() for _ in gradients],
        out_specs=[any_space, whole_block()],
        scratch_shapes=[
            pltpu.VMEM((padded, width), jnp.float32),
            pltpu.VMEM((kept * tokens, width), jnp.float32),
            pltpu.SemaphoreType.DMA((bands,)),
            pltpu.SemaphoreType.DMA((bands,)),
        ],
        input_output_aliases={4: 0},
        compiler_params=pltpu.CompilerParams(vmem_limit_bytes=VMEM_BYTES),
        cost_estimate=pl.CostEstimate(
            flops=2 * table_grad.size, bytes_accessed=8 * table_grad.size, transcendentals=0
        ),
    )(
        here,
        ends.reshape(-1),
        row_list.reshape(-1),
        token_list.reshape(-1),
        table_grad,
        held,
        other,
        weight_sums,
        *gradients,
    )


def moments_of(gradient, first, second, factor):
    clipped = gradient * factor
    first = BETA_ONE * first + (1.0 - BETA_ONE) * clipped
    second = BETA_TWO * second + (1.0 - BETA_TWO) * clipped * clipped
    return (first, second)


def update_of(weight, first, second):
    scaled = second * (1.0 / (1.0 - BETA_TWO**STEP))
    root = scaled * lax.rsqrt(scaled) + ADAM_EPS
    return first * (1.0 / (1.0 - BETA_ONE**STEP)) / root + DECAY * weight


def clip_factor(sums):
    return jnp.minimum(1.0, CLIP_AT / jnp.sqrt(sums[0:1, 0:1]))


def table_tile(rows, dp_count):
    return -(-rows // (3 * dp_count * 8)) * 8


def update_norms(sums, smalls, table_set, dp_count):
    weight, gradient, first, second = table_set
    rows, width = weight.shape
    tile = -(-rows // (6 * dp_count * 8)) * 8
    last = -(-rows // tile) - 1
    here = lax.axis_index("dp").astype(jnp.int32).reshape(1)
    number = len(smalls)

    def body(here_ref, sums_ref, w_ref, g_ref, m_ref, s_ref, *refs):
        small_refs = refs[: 4 * number]
        out_refs = refs[4 * number : 7 * number]
        norm_ref, acc_ref, term_ref = refs[7 * number :]
        step = pl.program_id(0)
        factor = clip_factor(sums_ref[...])

        @pl.when(step == 0)
        def _():
            acc_ref[...] = jnp.zeros_like(acc_ref)
            terms = [None]
            for place in range(number):
                w, g, m, s = (ref[...] for ref in small_refs[4 * place : 4 * place + 4])
                m, s = moments_of(g, m, s, factor)
                u = update_of(w, m, s)
                out_refs[3 * place][...] = m
                out_refs[3 * place + 1][...] = s
                out_refs[3 * place + 2][...] = u
                terms.append(total_of(u * u))
            term_ref[...] = tile_of(terms)

        row = (here_ref[0] * 6 + step) * tile + lax.broadcasted_iota(jnp.int32, (tile, 1), 0)
        m, s = moments_of(g_ref[...], m_ref[...], s_ref[...], factor)
        u = jnp.where(row < rows, update_of(w_ref[...], m, s), 0.0)
        acc_ref[...] += fold_rows(u * u)

        @pl.when(step == 5)
        def _():
            norm_ref[...] = term_ref[...] + tile_of([None] * (number + 1) + [total_of(acc_ref[...])])

    block = pl.BlockSpec(
        (tile, width), lambda i, here_ref: (jnp.minimum(here_ref[0] * 6 + i, last), 0)
    )
    flat = [value for group in smalls for value in group]
    outs = [jax.ShapeDtypeStruct(group[0].shape, jnp.float32) for group in smalls for _ in range(3)]
    made = pl.pallas_call(
        body,
        grid_spec=pltpu.PrefetchScalarGridSpec(
            num_scalar_prefetch=1,
            grid=(6,),
            in_specs=[whole_block()] + [block] * 4 + [whole_block() for _ in flat],
            out_specs=[whole_block() for _ in outs] + [whole_block()],
            scratch_shapes=[pltpu.VMEM((8, width), jnp.float32), pltpu.VMEM((8, 128), jnp.float32)],
        ),
        out_shape=outs + [jax.ShapeDtypeStruct((8, 128), jnp.float32)],
        compiler_params=pltpu.CompilerParams(vmem_limit_bytes=VMEM_BYTES),
        cost_estimate=pl.CostEstimate(
            flops=20 * tile * 6 * width, bytes_accessed=16 * tile * 6 * width, transcendentals=2 * tile * 6 * width
        ),
    )(here, sums, weight, gradient, first, second, *flat)
    return ([made[3 * place : 3 * place + 3] for place in range(number)], made[-1])


def write_updates(sums, norms, smalls, table_set):
    weight, gradient, first, second = table_set
    rows, width = weight.shape
    tile = 2 * table_tile(rows, lax.axis_size("dp"))
    steps = -(-rows // tile)
    number = len(smalls)

    def body(sums_ref, norms_ref, w_ref, g_ref, m_ref, s_ref, *refs):
        small_refs = refs[: 2 * number]
        out_w, out_m, out_s = refs[2 * number : 2 * number + 3]
        small_outs = refs[2 * number + 3 :]
        sums = sums_ref[...]
        pace = RATE * jnp.sqrt(sums) / jnp.sqrt(norms_ref[...])

        @pl.when(pl.program_id(0) == 0)
        def _():
            for place in range(number):
                w, u = (ref[...] for ref in small_refs[2 * place : 2 * place + 2])
                small_outs[place][...] = w - pace[0:1, place + 1 : place + 2] * u

        m, s = moments_of(g_ref[...], m_ref[...], s_ref[...], clip_factor(sums))
        w = w_ref[...]
        out_m[...] = m
        out_s[...] = s
        out_w[...] = w - pace[0:1, number + 1 : number + 2] * update_of(w, m, s)

    block = pl.BlockSpec((tile, width), lambda i: (i, 0))
    flat = [value for group in smalls for value in group]
    outs = [jax.ShapeDtypeStruct(weight.shape, jnp.float32)] * 3
    outs += [jax.ShapeDtypeStruct(group[0].shape, jnp.float32) for group in smalls]
    return pl.pallas_call(
        body,
        grid=(steps,),
        out_shape=outs,
        in_specs=[whole_block(), whole_block()] + [block] * 4 + [whole_block() for _ in flat],
        out_specs=[block] * 3 + [whole_block() for _ in smalls],
        compiler_params=pltpu.CompilerParams(vmem_limit_bytes=VMEM_BYTES),
        cost_estimate=pl.CostEstimate(
            flops=20 * weight.size, bytes_accessed=28 * weight.size, transcendentals=2 * weight.size
        ),
    )(sums, norms, weight, gradient, first, second, *flat)


def pick_half(value, index, axis):
    return lax.dynamic_index_in_dim(value, index, axis, keepdims=False)


class OuterSum:
    def __init__(self, held):
        self.held = held
        self.step = 1

    def advance(self, slots):
        held = self.held
        if held.shape[0] > 1:
            _, outer, _ = places()
            pairs = held.reshape((-1, 2) + held.shape[1:])
            own = (outer // self.step) % 2
            out = slots.open(pick_half(pairs, 1 - own, 1).astype(jnp.bfloat16))
            self.held = pick_half(pairs, own, 1) + swap_outer(out, self.step).astype(jnp.float32)
            self.step *= 2

    def finish(self, slots):
        while self.held.shape[0] > 1:
            self.advance(slots)
        return self.held.reshape(self.held.shape[1:])


def scatter_first(parts, slots):
    own, one_lower, one_upper, two_lower, two_upper, first, second = parts
    low = jnp.bfloat16
    first, second = slots.open((first, second))
    into_two = swap_dp(first, 1).astype(jnp.float32)
    into_one = swap_dp(second, 2).astype(jnp.float32)
    return (
        own,
        jnp.concatenate([one_lower, (one_upper + into_one).astype(low)], axis=0),
        jnp.concatenate([(two_lower + into_two).astype(low), two_upper], axis=0),
    )


def scatter_second(parts, slots):
    own, one, two = parts
    one, two = slots.open((one, two))
    return own + (swap_dp(one, 1).astype(jnp.float32) + swap_dp(two, 2).astype(jnp.float32))


def shards(
    token_ids,
    pick_rows,
    target_ids,
    attn_in,
    attn_out,
    mlp_in,
    mlp_out,
    positions,
    vectors,
    table,
    *moments,
):
    low = jnp.bfloat16
    dp_index, outer, core = places()
    dp_count = lax.axis_size("dp")
    shard_count = lax.axis_size("vocab")
    device_count = dp_count * shard_count
    outer_count = shard_count // 2
    vocab_rows, width = table.shape
    seq_len = token_ids.shape[1]
    pick_count = pick_rows.shape[1]
    vocab_start = lax.axis_index("vocab") * vocab_rows

    slots = Slots()
    unit_rows = attn_in.shape[0]
    small_count = positions.size + vectors.size
    small_width = -(-small_count // (unit_rows * 128)) * 128
    small = jnp.concatenate([positions.astype(low).reshape(-1), vectors.astype(low).reshape(-1)])
    small = jnp.pad(small, (0, unit_rows * small_width - small_count))
    first = OuterGather(
        jnp.concatenate(
            [attn_in.astype(low), attn_out.astype(low), small.reshape(unit_rows, small_width)], axis=1
        )
    )
    up_parts = mlp_in.shape[1] // width
    both = OuterGather(
        jnp.concatenate(
            [
                jnp.swapaxes(mlp_in.astype(low).reshape(unit_rows, up_parts, width), 0, 1),
                mlp_out.astype(low).reshape(-1, unit_rows, width),
            ],
            axis=0,
        )
    )
    small_masters = (attn_in, attn_out, mlp_in, mlp_out, positions, vectors)

    first.advance(slots)
    packed_ids = jnp.concatenate([token_ids, target_ids], axis=1)
    ids_pair = jnp.stack(xor_order([packed_ids, swap_core(packed_ids)], core))
    slots.close(first.held, ids_pair)

    first.finish(slots)
    ids_parts = outer_parts(slots.open(ids_pair))
    group_packed = jnp.concatenate(xor_order(ids_parts, outer), axis=0).reshape(shard_count, -1)
    group_targets = group_packed[:, seq_len:]
    slots.close(first.held, group_packed)

    first_ring = ring_first(first.held, slots)
    both.advance(slots)
    group_local = slots.open(group_packed) - vocab_start
    mine = (group_local >= 0) & (group_local < vocab_rows)
    served = jnp.take(table, jnp.where(mine, group_local, 0).reshape(-1), axis=0)
    served = jnp.where(mine.reshape(-1)[:, None], served, 0.0).astype(low)
    served = served.reshape(outer_count, 2, -1, width)
    slots.close(first_ring, both.held, served)

    first_held = ring_second(first_ring, slots)
    served = slots.open(served)
    served = pick_half(served, core, 1) + swap_core(pick_half(served, 1 - core, 1))
    slots.close(first_held, served)

    both.finish(slots)
    first_other = swap_core(slots.open(first_held))
    embedded = OuterSum(slots.open(served)[:, :seq_len].astype(jnp.float32))
    embedded.advance(slots)
    first_column = vocab_start.astype(jnp.int32).reshape(1)
    table_low, weight_sums, row_part = prepare_table(
        slots.open(table), small_masters, dp_count, first_column
    )
    slots.close(first_other, both.held, embedded.held, table_low)

    both_ring = ring_first(both.held, slots)
    embedded = embedded.finish(slots)
    w_qkv, w_proj, small_all = place_blocks(
        slots.open(first_held), first_other, (3 * width, width, small_width)
    )
    slots.close(embedded, w_qkv)

    w_qkv = w_qkv.reshape(width, 3 * width)
    w_proj = w_proj.reshape(width, width)
    small_all = slots.open(small_all).reshape(device_count, -1)
    pos_low = small_all[:, : positions.size].reshape(seq_len, width)
    vec_low = small_all[:, positions.size : small_count].reshape((device_count,) + vectors.shape)
    vec_rows = jnp.moveaxis(vec_low, 0, 1).reshape(vectors.shape[0], width).astype(jnp.float32)
    unit_chooser = choosers(width, unit_rows, core, dp_index)
    slots.close(both_ring, embedded, vec_rows, pos_low, unit_chooser)

    both_held = ring_second(both_ring, slots)
    resid_in, packed, resid_mid, normed_two, lefts_own, lefts_sent = attention_forward(
        slots.open(embedded), pos_low, vec_rows, w_qkv, w_proj, unit_chooser
    )
    target_rows = served[:, seq_len:].astype(jnp.float32)
    target_rows = OuterSum(target_rows)
    target_rows.advance(slots)
    slots.close(both_held, normed_two, target_rows.held)

    both_other = swap_core(slots.open(both_held))
    lefts_got = swap_core(slots.open(lefts_sent))
    target_rows = target_rows.finish(slots)
    packed_all = gather_dp(slots.open(group_packed)).reshape(device_count, -1)
    made = place_blocks(
        both_held, both_other, tuple(range(up_parts)) + ((up_parts, both_held.shape[1]),)
    )
    w_up = [value.reshape(width, width) for value in made[:up_parts]]
    w_down = made[up_parts].reshape(-1, width)
    hidden_pre, hidden_act, act_own, act_sent = hidden_forward(
        normed_two,
        vec_rows,
        w_up,
        choosers(width, mlp_out.shape[0], core),
        dp_index.astype(jnp.int32).reshape(1),
    )
    picks = pick_rows.reshape(-1, 1)
    resid_out, picked = output_forward(hidden_act, w_down, resid_mid, vec_rows, picks)
    slots.close(picked, packed_all, lefts_got, target_rows)

    tail_rows = jnp.concatenate(split_three(row_part), axis=0)
    sent = jnp.concatenate([picked, jnp.pad(tail_rows, ((0, 13), (0, 0)))], axis=0)
    same_core = jnp.stack(outer_parts(slots.open(sent)))
    act_got = swap_core(slots.open(act_sent))
    counts, row_list, token_list = token_lists(
        slots.open(packed_all)[:, :seq_len],
        vocab_start,
        vocab_rows,
        4 * seq_len // shard_count,
        table_low.shape[0] // CHUNK,
    )
    slots.close(same_core, act_got, counts, row_list, token_list)

    ordered = jnp.stack(xor_order([same_core[step] for step in range(outer_count)], outer))
    head_in = jnp.stack(xor_order([ordered, swap_core(slots.open(ordered))], core), axis=1)
    row_sum = head_in[:, :, pick_count : pick_count + 3].astype(jnp.float32).reshape(-1, width)
    row_sum = jnp.sum(row_sum, axis=0, keepdims=True)
    head_in = head_in[:, :, :pick_count]
    head_in = head_in.reshape(-1, width)
    slots.close(head_in)
    ring = ring_first(same_core[:, :pick_count], slots)
    here = jnp.stack([vocab_start, core]).astype(jnp.int32)
    head_own, head_stat, head_sent = head_pass(slots.open(head_in), table_low, here, vocab_rows, pick_count)
    slots.close(head_sent, ring)

    head_got = swap_core(slots.open(head_sent))
    joined = join_cores(
        head_own, head_stat, head_got, outer.astype(jnp.int32).reshape(1), pick_count
    )
    slots.close(joined[0])

    received = [
        swap_outer(value, step + 1) for step, value in enumerate(slots.open(tuple(joined[2:])))
    ]
    token_count = device_count * pick_count
    grad_top, grad_branch, vec_down, row_stats = output_backward(
        joined[0],
        joined[1],
        received,
        picked,
        target_rows,
        row_sum,
        picks,
        resid_out,
        vec_rows,
        float(token_count),
    )
    slots.close(grad_branch)

    dy_got = swap_core(slots.open(grad_branch))
    stats_pair = slots.open(row_stats[:, :2].T)
    stats_pair = jnp.stack(xor_order([stats_pair, swap_core(stats_pair)], core))
    ring = ring_second(ring, slots)
    grad_pre, vec_up = hidden_backward(slots.open(grad_branch), w_down, hidden_pre)
    slots.close(dy_got, stats_pair, grad_pre, ring)

    pre_got = swap_core(slots.open(grad_pre))
    stats_parts = outer_parts(slots.open(stats_pair))
    stats_group = jnp.concatenate(xor_order(stats_parts, outer), axis=0)
    down = gradient_blocks(
        [(act_own, act_got)],
        [(0, act_own.shape[1])],
        [(slots.open(grad_branch), dy_got)],
        None,
        mlp_out.shape[0],
    )
    slots.close(pre_got, stats_group, down[5])

    lefts = (lefts_own, lefts_got)
    left_spans = [(place * width // 2, (place + 1) * width // 2) for place in range(3)]
    down = scatter_first(down, slots)
    stats_all = gather_dp(slots.open(stats_group))
    up = gradient_blocks(
        [lefts], left_spans[2:], [(slots.open(grad_pre), pre_got)], None, unit_rows
    )
    grad_mid, grad_attn, grad_mixed, vec_middle = middle_backward(
        behind(grad_pre, up[5]), w_up, grad_top, resid_mid, w_proj, vec_rows
    )
    slots.close(down, up, grad_mid, stats_all)

    down = OuterSum(scatter_second(down, slots))
    attn_got = swap_core(slots.open(grad_attn))
    ring_other = swap_core(slots.open(ring))
    grad_in, grad_rows, grad_packed, vec_first = attention_backward(
        grad_mixed, slots.open(grad_mid), packed, resid_in, w_qkv, vec_rows
    )
    slots.close(down.held, grad_rows, attn_got, ring_other)
    grad_in, vec_first = slots.open((grad_in, vec_first))

    norm_all = (stats_all[:, :, 0].reshape(1, -1) + math.log(token_count)).astype(jnp.float32)
    loss = jnp.sum(stats_all[:, :, 1]) / token_count
    targets_all = packed_all[:, seq_len:].reshape(1, -1)
    vec_grad = jnp.concatenate(
        [
            vec_first[0:2],
            vec_middle[0:2],
            vec_down[0:2],
            vec_first[2:4],
            vec_middle[2:3],
            vec_down[2:3],
            vec_up[0:4],
        ],
        axis=0,
    )
    vec_width = vectors.shape[1]
    vec_blocks = jnp.moveaxis(vec_grad.reshape(-1, device_count, vec_width), 1, 0)
    small_grad = jnp.concatenate(
        [grad_in.reshape(device_count, -1), vec_blocks.reshape(device_count, -1)], axis=1
    )
    small_grad = jnp.pad(small_grad, ((0, 0), (0, unit_rows * small_width - small_count)))
    small_grad = small_grad.reshape(-1, 2, unit_rows, small_width)
    small_sent = pick_half(small_grad, 1 - core, 1).astype(low)

    pieces = table_low.shape[0] // PIECE
    bounds = [0] + [round(pieces * share) for share in (0.3, 0.7, 0.9)] + [pieces]

    def head_part(earlier, part, mark):
        if bounds[part] == bounds[part + 1]:
            return (earlier, mark)
        return table_part(
            earlier,
            head_all,
            table_low,
            targets_all,
            behind(norm_all, mark),
            first_column,
            vocab_rows,
            1.0 / token_count,
            bounds[part],
            bounds[part + 1],
        )

    up = scatter_first(up, slots)
    packed_got = swap_core(slots.open(grad_packed))
    small_got = swap_core(slots.open(small_sent))
    small_sum = pick_half(small_grad, core, 1) + small_got.astype(jnp.float32)
    small_sum = small_sum.reshape(4, outer_count * unit_rows, small_width)
    small_sum = jnp.stack([pick_half(small_sum, dp_index ^ step, 0) for step in range(4)])
    head_all = place_blocks(slots.open(ring), ring_other, (width,))[0].reshape(-1, width)
    rows = OuterGather(slots.open(grad_rows))
    rows.advance(slots)
    slots.close(up[1:], packed_got, small_sum, rows.held, head_all)

    up = OuterSum(scatter_second(up, slots))
    rows_outer = rows.finish(slots)
    down.advance(slots)
    first = gradient_blocks(
        [lefts, lefts],
        left_spans[:2],
        [(grad_packed, slots.open(packed_got)), (grad_attn, attn_got)],
        small_sum,
        unit_rows,
    )
    table_grad, mark = head_part(None, 0, first[5])
    slots.close(up.held, first[5], rows_outer, down.held, mark)

    first = scatter_first(first, slots)
    rows_ring = ring_first(rows_outer, slots)
    up.advance(slots)
    table_grad, mark = head_part(table_grad, 1, slots.last)
    slots.close(first[1:], rows_ring, up.held, mark)

    first = scatter_second(first, slots)
    rows_held = ring_second(rows_ring, slots)
    up_own = up.finish(slots)
    table_grad, mark = head_part(table_grad, 2, slots.last)
    slots.close(first, up_own, rows_held, mark)

    first_terms = [pick_half(first, outer, 0)]
    for step in range(1, outer_count):
        sent = slots.open(pick_half(first, outer ^ step, 0).astype(low))
        first_terms.append(swap_outer(sent, step).astype(jnp.float32))
    first_own = tree_sum(first_terms)
    rows_other = swap_core(slots.open(rows_held))
    down_own = down.finish(slots)
    table_grad, mark = head_part(table_grad, 3, slots.last)
    small_own = first_own[:, 4 * width :].reshape(-1)
    gradients = (
        first_own[:, : 3 * width],
        first_own[:, 3 * width : 4 * width],
        up_own,
        down_own,
        small_own[: positions.size].reshape(positions.shape),
        small_own[positions.size : small_count].reshape(vectors.shape),
    )
    table_grad, sums = add_rows(
        table_grad, rows_held, rows_other, counts, row_list, token_list, gradients, weight_sums, dp_count
    )
    sums = sum_all(sums)
    grad_norm = jnp.sqrt(sums[0, 0])
    firsts, seconds = moments[:7], moments[7:]
    smalls = list(zip(small_masters, gradients, firsts, seconds))
    table_set = (table, table_grad, firsts[6], seconds[6])
    made, norms = update_norms(sums, smalls, table_set, dp_count)
    norms = sum_all(norms)
    ratios = jnp.sqrt(sums[0, 1:8]) / jnp.sqrt(norms[0, 1:8])
    written = write_updates(
        sums, norms, [(weight, group[2]) for weight, group in zip(small_masters, made)], table_set
    )
    new_weights = list(written[3:]) + [written[0]]
    new_firsts = [group[0] for group in made] + [written[1]]
    new_seconds = [group[1] for group in made] + [written[2]]
    return (loss, grad_norm, ratios, *new_weights, *new_firsts, *new_seconds)


def solution(mesh):
    rows = P(("dp", "vocab"), None)
    weights = (rows, rows, rows, rows, rows, P(None, ("dp", "vocab")), P("vocab", None))
    return jax.shard_map(
        shards,
        mesh=mesh,
        in_specs=(rows, rows, rows) + weights * 3,
        out_specs=(P(), P(), P()) + weights * 3,
        check_vma=False,
    )
```

```python
import functools
import math

import jax
import jax.numpy as jnp
from jax import lax
from jax.experimental import pallas as pl
from jax.experimental.pallas import tpu as pltpu
from jax.sharding import PartitionSpec as P

HD = 64
V_REAL = 50257
STEP = 5


LN_EPS = 1e-05
SMOOTHING = 0.1
BETA_ONE = 0.9
BETA_TWO = 0.999
ADAM_EPS = 1e-12
DECAY = 0.01
RATE = 0.3
CLIP_AT = 0.01
MASKED = -1e30
CHUNK = 1280
PIECE = 640
VMEM_BYTES = 58 * 2**20


def layer_norm(inputs, gain, shift):
    centre = jnp.mean(inputs, axis=-1, keepdims=True)
    centred = inputs - centre
    spread = jnp.mean(centred * centred, axis=-1, keepdims=True)
    return centred * lax.rsqrt(spread + LN_EPS) * gain + shift


def gelu_tanh(inputs):
    return (
        0.5
        * inputs
        * (1.0 + jnp.tanh(0.7978845608028654 * (inputs + 0.044715 * inputs * inputs * inputs)))
    )


def dot_plain(left_op, right_op):
    return jnp.dot(left_op, right_op, preferred_element_type=jnp.float32)


def dot_first(left_op, right_op):
    return lax.dot_general(
        left_op, right_op, (((0,), (0,)), ((), ())), preferred_element_type=jnp.float32
    )


def dot_second(left_op, right_op):
    return lax.dot_general(
        left_op, right_op, (((1,), (1,)), ((), ())), preferred_element_type=jnp.float32
    )


def params(limit=26 * 2**20):
    return pltpu.CompilerParams(vmem_limit_bytes=min(limit, VMEM_BYTES))


def cost(flops, bytes_accessed):
    return pl.CostEstimate(
        flops=int(flops), bytes_accessed=int(bytes_accessed), transcendentals=0
    )


def whole_block():
    return pl.BlockSpec(memory_space=pltpu.VMEM)


def shape_of(shape, dtype):
    return jax.ShapeDtypeStruct(tuple(shape), dtype)


def causal_scores(queries, keys, causal):
    return jnp.where(causal, dot_second(queries, keys) * HD ** (-0.5), MASKED)


def causal_mask(count):
    query = lax.broadcasted_iota(jnp.int32, (count, count), 0)
    key = lax.broadcasted_iota(jnp.int32, (count, count), 1)
    return key <= query


def head_span(head):
    return slice(head * HD, (head + 1) * HD)


def attention_forward(embedded, positions, vec_rows, w_qkv, w_proj, chooser):
    count, width = embedded.shape
    low = jnp.bfloat16

    half = width // 2

    def body(
        e_ref, p_ref, v_ref, qkv_ref, proj_ref, c_ref, x0_ref, packed_ref, x1_ref, h2_ref, own_ref, other_ref, o_ref
    ):
        x0 = e_ref[...] + p_ref[...].astype(jnp.float32)
        x0_ref[...] = x0
        h1 = layer_norm(x0, v_ref[0:1, :], v_ref[1:2, :]).astype(low)
        parts = []
        for place, bias in enumerate((6, None, 7)):
            span = slice(place * width, (place + 1) * width)
            part = dot_plain(h1, qkv_ref[:, span])
            if bias is not None:
                part = part + v_ref[bias : bias + 1, :]
            parts.append(part.astype(low))
            packed_ref[:, span] = parts[-1]
        queries, keys, values = parts
        causal = causal_mask(count)
        for head in range(0, width // HD, 2):
            mixed = []
            for one in (head, head + 1):
                span = head_span(one)
                scores = causal_scores(queries[:, span], keys[:, span], causal)
                grown = jnp.exp(scores - jnp.max(scores, axis=-1, keepdims=True))
                probs = (grown / jnp.sum(grown, axis=-1, keepdims=True)).astype(low)
                mixed.append(dot_plain(probs, values[:, span]))
            o_ref[:, head * HD : (head + 2) * HD] = jnp.concatenate(mixed, axis=1).astype(low)
        x1 = x0 + dot_plain(o_ref[...], proj_ref[...]) + v_ref[8:9, :]
        x1_ref[...] = x1
        h2 = layer_norm(x1, v_ref[2:3, :], v_ref[3:4, :]).astype(low)
        h2_ref[...] = h2
        for place, value in enumerate((h1, o_ref[...], h2)):
            span = slice(place * half, (place + 1) * half)
            own_ref[:, span] = dot_plain(value, c_ref[0]).astype(low)
            other_ref[:, span] = dot_plain(value, c_ref[1]).astype(low)

    shape = (count, width)
    return pl.pallas_call(
        body,
        out_shape=[
            shape_of(shape, jnp.float32),
            shape_of((count, 3 * width), low),
            shape_of(shape, jnp.float32),
            shape_of(shape, low),
            shape_of((count, 3 * half), low),
            shape_of((count, 3 * half), low),
        ],
        in_specs=[whole_block()] * 6,
        out_specs=[whole_block()] * 6,
        scratch_shapes=[pltpu.VMEM(shape, low)],
        compiler_params=params(),
        cost_estimate=cost(20 * count * width * width, 8 * width * width),
    )(embedded, positions, vec_rows, w_qkv, w_proj, chooser)


def hidden_forward(normed, vec_rows, w_up, chooser, dp_index):
    count, width = normed.shape
    blocks = len(w_up)
    hidden = blocks * width
    half = width // 2
    low = jnp.bfloat16

    def body(dp_ref, h_ref, v_ref, c_ref, *refs):
        w_refs = refs[:blocks]
        pre_ref, act_ref, own_ref, other_ref = refs[blocks:]
        for place in range(blocks):
            span = slice(place * width, (place + 1) * width)
            pre = dot_plain(h_ref[...], w_refs[place][...]) + v_ref[10 + place : 11 + place, :]
            pre_ref[:, span] = pre
            act_ref[:, span] = gelu_tanh(pre).astype(low)
        for place in range(blocks):
            source = pl.multiple_of((dp_ref[0] ^ place) * width, width)
            part = act_ref[:, pl.ds(source, width)]
            span = slice(place * half, (place + 1) * half)
            own_ref[:, span] = dot_plain(part, c_ref[0]).astype(low)
            other_ref[:, span] = dot_plain(part, c_ref[1]).astype(low)

    return pl.pallas_call(
        body,
        out_shape=[
            shape_of((count, hidden), jnp.float32),
            shape_of((count, hidden), low),
            shape_of((count, hidden // 2), low),
            shape_of((count, hidden // 2), low),
        ],
        in_specs=[pl.BlockSpec(memory_space=pltpu.SMEM)] + [whole_block()] * (3 + blocks),
        out_specs=[whole_block()] * 4,
        compiler_params=params(),
        cost_estimate=cost(3 * count * width * hidden, 2 * width * hidden),
    )(dp_index, normed, vec_rows, chooser, *w_up)


def output_forward(act, w_down, resid_mid, vec_rows, picks):
    count, width = resid_mid.shape
    number = picks.shape[0]

    def body(act_ref, w_ref, x1_ref, v_ref, pick_ref, x2_ref, out_ref):
        x2 = x1_ref[...] + dot_plain(act_ref[...], w_ref[...]) + v_ref[9:10, :]
        x2_ref[...] = x2
        final = layer_norm(x2, v_ref[4:5, :], v_ref[5:6, :]).astype(jnp.bfloat16)
        hot = pick_ref[...] == lax.broadcasted_iota(jnp.int32, (number, count), 1)
        hot = jnp.where(hot, 1.0, 0.0).astype(jnp.bfloat16)
        out_ref[...] = dot_plain(hot, final).astype(jnp.bfloat16)

    return pl.pallas_call(
        body,
        out_shape=[
            shape_of((count, width), jnp.float32),
            shape_of((number, width), jnp.bfloat16),
        ],
        in_specs=[whole_block()] * 5,
        out_specs=[whole_block()] * 2,
        compiler_params=params(),
        cost_estimate=cost(2 * act.size * width, 2 * w_down.size),
    )(act, w_down, resid_mid, vec_rows, picks)


def norm_backward(grad, inputs, gain):
    centred = inputs - jnp.mean(inputs, axis=-1, keepdims=True)
    scale = lax.rsqrt(jnp.mean(centred * centred, axis=-1, keepdims=True) + LN_EPS)
    normed = centred * scale
    scaled = grad * gain
    back = scale * (
        scaled
        - jnp.mean(scaled, axis=-1, keepdims=True)
        - normed * jnp.mean(scaled * normed, axis=-1, keepdims=True)
    )
    return (
        back,
        jnp.sum(grad * normed, axis=0, keepdims=True),
        jnp.sum(grad, axis=0, keepdims=True),
    )


def column_sum(value):
    return jnp.sum(value.astype(jnp.float32), axis=0, keepdims=True)


def choosers(width, rows, core, dp_index=None):
    column = jnp.arange(width, dtype=jnp.int32)
    target = jnp.arange(width // 2, dtype=jnp.int32)
    block = target // rows
    if dp_index is not None:
        per = width // (8 * rows)
        block = ((block // per) ^ dp_index) * per + block % per
    made = []
    for side in (core, 1 - core):
        source = (block * 2 + side) * rows + target % rows
        made.append((column[:, None] == source[None, :]).astype(jnp.bfloat16))
    return jnp.stack(made)


def gradient_blocks(lefts, spans, rights, smalls, name_rows):
    widths = [right[0].shape[1] for right in rights]
    total = sum(widths) + (smalls.shape[2] if smalls is not None else 0)
    arrays = [value for pair in zip(lefts, rights) for group in pair for value in group]
    if smalls is not None:
        arrays.append(smalls)
    number = len(lefts)
    rows = (spans[0][1] - spans[0][0]) // 4
    half = rows // 2
    low = jnp.bfloat16

    def body(*refs):
        in_refs, out_refs = refs[: len(arrays)], refs[len(arrays) :]

        def put(made, span):
            own, one, two, three = [made(place) for place in range(4)]
            out_refs[0][:, span] = own
            out_refs[1][:, span] = one[:half].astype(low)
            out_refs[2][:, span] = one[half:]
            out_refs[3][:, span] = two[:half]
            out_refs[4][:, span] = two[half:].astype(low)
            out_refs[5][:, span] = three[:half].astype(low)
            out_refs[6][:, span] = three[half:].astype(low)

        start = 0
        for index in range(number):
            left_a, left_b, right_a, right_b = in_refs[4 * index : 4 * index + 4]
            columns = slice(*spans[index])
            left = jnp.concatenate([left_a[:, columns], left_b[:, columns]], axis=0)
            for begin in range(0, widths[index], 768):
                stop = min(begin + 768, widths[index])
                right = jnp.concatenate([right_a[:, begin:stop], right_b[:, begin:stop]], axis=0)
                result = dot_first(left, right)
                put(
                    lambda place, result=result: result[place * rows : (place + 1) * rows],
                    slice(start + begin, start + stop),
                )
            start += widths[index]
        if smalls is not None:
            put(lambda place: in_refs[-1][place], slice(start, total))

    out = [shape_of((rows, total), jnp.float32)]
    out += [shape_of((half, total), kind) for kind in (low, jnp.float32, jnp.float32, low, low, low)]
    flops = sum(4 * left[0].shape[0] * 4 * rows * right[0].shape[1] for left, right in zip(lefts, rights))
    made = pl.pallas_call(
        body,
        out_shape=out,
        in_specs=[whole_block()] * len(arrays),
        out_specs=[whole_block()] * 7,
        compiler_params=params(),
        cost_estimate=cost(flops, 14 * rows * total),
    )(*arrays)
    return [value.reshape(-1, name_rows, total) for value in made]


def split_three(value):
    low = jnp.bfloat16
    first = value.astype(low)
    rest = value - first.astype(jnp.float32)
    second = rest.astype(low)
    return (first, second, (rest - second.astype(jnp.float32)).astype(low))


def pack_stats(top, total):
    lane = lax.broadcasted_iota(jnp.int32, (top.shape[0], 128), 1)
    tile = jnp.zeros((top.shape[0], 128), jnp.float32)
    for place, part in enumerate(split_three(top) + split_three(total)):
        tile = jnp.where(lane == place, part.astype(jnp.float32), tile)
    return tile.astype(jnp.bfloat16)


def unpack_stats(tile):
    wide = tile.astype(jnp.float32)
    return (
        wide[:, 0:1] + (wide[:, 1:2] + wide[:, 2:3]),
        wide[:, 3:4] + (wide[:, 4:5] + wide[:, 5:6]),
    )


def join(one, two):
    top = jnp.maximum(one[1], two[1])
    scale_one, scale_two = jnp.exp(one[1] - top), jnp.exp(two[1] - top)
    return (
        one[0] * scale_one + two[0] * scale_two,
        top,
        one[2] * scale_one + two[2] * scale_two,
    )


def unpack_rows(packed, width):
    top, total = unpack_stats(packed[:, width:])
    return (packed[:, :width].astype(jnp.float32), top, total)


def head_pass(head_in, table_low, here, rows, pick_count):
    count, width = head_in.shape
    chunks = table_low.shape[0] // CHUNK
    groups = count // (2 * pick_count)
    half = count // 2

    def body(here_ref, head_ref, table_ref, own_ref, stat_ref, sent_ref, acc_ref, tops_ref):
        head = head_ref[...]
        real = jnp.minimum(rows, V_REAL - here_ref[0])
        acc_ref[...] = jnp.zeros_like(acc_ref)

        def step(index, carry, masked):
            top, total = carry
            begin = pl.multiple_of(index * CHUNK, CHUNK)
            part = table_ref[pl.ds(begin, CHUNK), :]
            values = dot_second(head, part)
            if masked:
                local = lax.broadcasted_iota(jnp.int32, (1, CHUNK), 1) + begin
                values = jnp.where(local < real, values, MASKED)
            higher = jnp.maximum(top, jnp.max(values, axis=1, keepdims=True))
            grown = jnp.exp(values - higher)
            scale = jnp.exp(top - higher)
            acc_ref[...] = acc_ref[...] * scale + dot_plain(grown.astype(jnp.bfloat16), part)
            return (higher, total * scale + jnp.sum(grown, axis=1, keepdims=True))

        carry = (jnp.full((count, 1), MASKED, jnp.float32), jnp.zeros((count, 1), jnp.float32))
        unmasked = jnp.maximum(real, 0) // CHUNK
        carry = lax.fori_loop(0, unmasked, functools.partial(step, masked=False), carry)
        top, total = lax.fori_loop(unmasked, chunks, functools.partial(step, masked=True), carry)
        lane = lax.broadcasted_iota(jnp.int32, (count, 128), 1)
        tops_ref[...] = jnp.where(lane == 0, top, jnp.where(lane == 1, total, 0.0))
        for group in range(groups):
            own = pl.multiple_of((2 * group + here_ref[1]) * pick_count, pick_count)
            other = pl.multiple_of((2 * group + 1 - here_ref[1]) * pick_count, pick_count)
            span = slice(group * pick_count, (group + 1) * pick_count)
            own_ref[span, :] = acc_ref[pl.ds(own, pick_count), :]
            stat_ref[span, :] = tops_ref[pl.ds(own, pick_count), :]
            sent_ref[span, :width] = acc_ref[pl.ds(other, pick_count), :].astype(jnp.bfloat16)
            stats = tops_ref[pl.ds(other, pick_count), :]
            sent_ref[span, width:] = pack_stats(stats[:, 0:1], stats[:, 1:2])

    return pl.pallas_call(
        body,
        out_shape=[
            shape_of((half, width), jnp.float32),
            shape_of((half, 128), jnp.float32),
            shape_of((half, width + 128), jnp.bfloat16),
        ],
        in_specs=[pl.BlockSpec(memory_space=pltpu.SMEM)] + [whole_block()] * 2,
        out_specs=[whole_block()] * 3,
        scratch_shapes=[pltpu.VMEM((count, width), jnp.float32), pltpu.VMEM((count, 128), jnp.float32)],
        compiler_params=params(10 * 2**20 + 2 * table_low.size + 16 * count * CHUNK),
        cost_estimate=cost(4 * table_low.size * count, 2 * table_low.size),
    )(here, head_in, table_low)


def join_cores(own, stats, received, outer, pick_count):
    half, width = own.shape
    groups = half // pick_count

    def body(outer_ref, own_ref, stat_ref, received_ref, rows_ref, out_stat_ref, *sent_refs):
        for step in range(groups):
            start = pl.multiple_of((outer_ref[0] ^ step) * pick_count, pick_count)
            span = pl.ds(start, pick_count)
            stat = stat_ref[span, :]
            one = (own_ref[span, :], stat[:, 0:1], stat[:, 1:2])
            value, top, total = join(one, unpack_rows(received_ref[span, :], width))
            if step:
                sent_refs[step - 1][:, :width] = value.astype(jnp.bfloat16)
                sent_refs[step - 1][:, width:] = pack_stats(top, total)
            else:
                lane = lax.broadcasted_iota(jnp.int32, (pick_count, 128), 1)
                rows_ref[...] = value
                out_stat_ref[...] = jnp.where(lane == 0, top, jnp.where(lane == 1, total, 0.0))

    return pl.pallas_call(
        body,
        out_shape=[
            shape_of((pick_count, width), jnp.float32),
            shape_of((pick_count, 128), jnp.float32),
        ]
        + [shape_of((pick_count, width + 128), jnp.bfloat16)] * (groups - 1),
        in_specs=[pl.BlockSpec(memory_space=pltpu.SMEM)] + [whole_block()] * 3,
        out_specs=[whole_block()] * (groups + 1),
        compiler_params=params(),
        cost_estimate=cost(4 * own.size, 8 * own.size),
    )(outer, own, stats, received)


def output_backward(rows, stats, received, picked, target_rows, row_sum, picks, resid_out, vec_rows, token_count):
    count, width = resid_out.shape
    number = picks.shape[0]
    low = jnp.bfloat16
    others = len(received)

    def body(rows_ref, stat_ref, *refs):
        received_refs = refs[:others]
        f_ref, t_ref, sum_ref, pick_ref, x_ref, v_ref, dx_ref, dy_ref, vec_ref, norm_ref = refs[others:]
        stat = stat_ref[...]
        value = (rows_ref[...], stat[:, 0:1], stat[:, 1:2])
        for ref in received_refs:
            value = join(value, unpack_rows(ref[...], width))
        mean, top, total = value
        target = t_ref[...]
        final = f_ref[...].astype(jnp.float32)
        norm = top + jnp.log(total)
        hit = jnp.sum(final * target, axis=1, keepdims=True)
        plain = jnp.sum(final * sum_ref[...], axis=1, keepdims=True)
        loss = (1.0 - SMOOTHING) * (norm - hit) + SMOOTHING * (norm - plain / V_REAL)
        lane = lax.broadcasted_iota(jnp.int32, (number, 128), 1)
        norm_ref[...] = jnp.where(lane == 0, norm, jnp.where(lane == 1, loss, 0.0))
        soft = jnp.exp(hit - norm)
        whole = ((soft - (1.0 - SMOOTHING) - SMOOTHING / V_REAL) / token_count).astype(low)
        factor = whole.astype(jnp.float32) - (soft - SMOOTHING / V_REAL) / token_count
        picked_grad = (
            mean * (1.0 / token_count) / total
            - sum_ref[...] * (SMOOTHING / V_REAL / token_count)
            + target * factor
        )
        hot = pick_ref[...] == lax.broadcasted_iota(jnp.int32, (number, count), 1)
        final_grad = lax.dot_general(
            jnp.where(hot, 1.0, 0.0),
            picked_grad,
            (((0,), (0,)), ((), ())),
            precision=lax.Precision.HIGHEST,
            preferred_element_type=jnp.float32,
        )
        back, gain, shift = norm_backward(final_grad, x_ref[...], v_ref[4:5, :])
        dx_ref[...] = back
        dy = back.astype(low)
        dy_ref[...] = dy
        vec_ref[0:1, :] = gain
        vec_ref[1:2, :] = shift
        vec_ref[2:3, :] = column_sum(dy)
        vec_ref[3:8, :] = jnp.zeros((5, width), jnp.float32)

    return pl.pallas_call(
        body,
        out_shape=[
            shape_of((count, width), jnp.float32),
            shape_of((count, width), low),
            shape_of((8, width), jnp.float32),
            shape_of((number, 128), jnp.float32),
        ],
        in_specs=[whole_block()] * (8 + others),
        out_specs=[whole_block()] * 4,
        compiler_params=params(),
        cost_estimate=cost(20 * count * width, 20 * count * width),
    )(rows, stats, *received, picked, target_rows, row_sum, picks, resid_out, vec_rows)


def hidden_backward(dy, w_down, pre):
    count, width = dy.shape
    hidden = pre.shape[1]
    low = jnp.bfloat16

    def body(dy_ref, w_ref, pre_ref, dpre_ref, vec_ref):
        vec_ref[...] = jnp.zeros_like(vec_ref)
        for place in range(hidden // width):
            span = slice(place * width, (place + 1) * width)
            grad = dot_second(dy_ref[...], w_ref[span, :])
            u = pre_ref[:, span]
            bent = jnp.tanh(0.7978845608028654 * (u + 0.044715 * u * u * u))
            slope = 0.5 * (1.0 + bent) + 0.5 * u * (1.0 - bent * bent) * (
                0.7978845608028654 * (1.0 + 3.0 * 0.044715 * u * u)
            )
            dpre = (grad * slope).astype(low)
            dpre_ref[:, span] = dpre
            vec_ref[place : place + 1, :] = column_sum(dpre)

    return pl.pallas_call(
        body,
        out_shape=[shape_of((count, hidden), low), shape_of((8, width), jnp.float32)],
        in_specs=[whole_block()] * 3,
        out_specs=[whole_block()] * 2,
        compiler_params=params(),
        cost_estimate=cost(2 * count * width * hidden, 2 * width * hidden),
    )(dy, w_down, pre)


def middle_backward(dpre, w_up, dx2, x1, w_proj, vec_rows):
    count, width = x1.shape
    low = jnp.bfloat16

    blocks = len(w_up)

    def body(dpre_ref, dx2_ref, x1_ref, proj_ref, v_ref, *refs):
        up_refs = refs[:blocks]
        dx1_ref, da_ref, mixed_ref, vec_ref = refs[blocks:]
        dh2 = jnp.zeros((count, width), jnp.float32)
        for place in range(blocks):
            span = slice(place * width, (place + 1) * width)
            dh2 = dh2 + dot_second(dpre_ref[:, span], up_refs[place][...])
        back, gain, shift = norm_backward(dh2, x1_ref[...], v_ref[2:3, :])
        dx1 = back + dx2_ref[...]
        dx1_ref[...] = dx1
        da = dx1.astype(low)
        da_ref[...] = da
        vec_ref[0:1, :] = gain
        vec_ref[1:2, :] = shift
        vec_ref[2:3, :] = column_sum(da)
        vec_ref[3:8, :] = jnp.zeros((5, width), jnp.float32)
        mixed_ref[...] = dot_second(da, proj_ref[...]).astype(low)

    return pl.pallas_call(
        body,
        out_shape=[
            shape_of((count, width), jnp.float32),
            shape_of((count, width), low),
            shape_of((count, width), low),
            shape_of((8, width), jnp.float32),
        ],
        in_specs=[whole_block()] * (5 + blocks),
        out_specs=[whole_block()] * 4,
        compiler_params=params(),
        cost_estimate=cost(10 * count * width * width, 10 * width * width),
    )(dpre, dx2, x1, w_proj, vec_rows, *w_up)


def attention_backward(mixed, dx1, packed, x0, w_qkv, vec_rows):
    count, width = x0.shape
    low = jnp.bfloat16

    def body(mixed_ref, dx1_ref, packed_ref, x0_ref, qkv_ref, v_ref, dx0_ref, rows_ref, grad_ref, vec_ref):
        causal = causal_mask(count)
        for head in range(0, width // HD, 2):
            sides = ([], [], [])
            for one in (head, head + 1):
                queries = packed_ref[:, one * HD : (one + 1) * HD]
                keys = packed_ref[:, width + one * HD : width + (one + 1) * HD]
                values = packed_ref[:, 2 * width + one * HD : 2 * width + (one + 1) * HD]
                scores = causal_scores(queries, keys, causal)
                grown = jnp.exp(scores - jnp.max(scores, axis=-1, keepdims=True))
                probs = grown / jnp.sum(grown, axis=-1, keepdims=True)
                out_grad = mixed_ref[:, one * HD : (one + 1) * HD]
                grad_p = dot_second(out_grad, values)
                centre = jnp.sum(probs * grad_p, axis=-1, keepdims=True)
                grad_s = (probs * (grad_p - centre)).astype(low)
                sides[0].append(dot_plain(grad_s, keys) * HD ** (-0.5))
                sides[1].append(dot_first(grad_s, queries) * HD ** (-0.5))
                sides[2].append(dot_first(probs.astype(low), out_grad))
            for place, side in enumerate(sides):
                start = place * width + head * HD
                grad_ref[:, start : start + 2 * HD] = jnp.concatenate(side, axis=1).astype(low)
        dh1 = dot_second(grad_ref[...], qkv_ref[...])
        back, gain, shift = norm_backward(dh1, x0_ref[...], v_ref[0:1, :])
        vec_ref[0:1, :] = gain
        vec_ref[1:2, :] = shift
        vec_ref[2:3, :] = column_sum(grad_ref[:, :width])
        vec_ref[3:4, :] = column_sum(grad_ref[:, 2 * width :])
        vec_ref[4:8, :] = jnp.zeros((4, width), jnp.float32)
        dx0 = back + dx1_ref[...]
        dx0_ref[...] = dx0
        rows_ref[...] = dx0.astype(low)

    return pl.pallas_call(
        body,
        out_shape=[
            shape_of((count, width), jnp.float32),
            shape_of((count, width), low),
            shape_of((count, 3 * width), low),
            shape_of((8, width), jnp.float32),
        ],
        in_specs=[whole_block()] * 6,
        out_specs=[whole_block()] * 4,
        compiler_params=params(),
        cost_estimate=cost(16 * count * width * width, 10 * width * width),
    )(mixed, dx1, packed, x0, w_qkv, vec_rows)


def bit_of(index, level):
    return (index >> level) & 1


def xor_order(parts, index):
    level = 0
    while (1 << level) < len(parts):
        odd = bit_of(index, level) == 1
        step = 1 << level
        placed = list(parts)
        for place in range(len(parts)):
            if not place & step:
                low, high = parts[place], parts[place | step]
                placed[place] = jnp.where(odd, high, low)
                placed[place | step] = jnp.where(odd, low, high)
        parts = placed
        level += 1
    return parts


def tree_sum(parts):
    while len(parts) > 1:
        parts = [parts[place] + parts[place + 1] for place in range(0, len(parts), 2)]
    return parts[0]


def swap_core(value):
    count = lax.axis_size("vocab")
    return lax.ppermute(value, "vocab", [(i, i ^ 1) for i in range(count)])


def swap_outer(value, step):
    count = lax.axis_size("vocab")
    return lax.ppermute(value, "vocab", [(i, i ^ (2 * step)) for i in range(count)])


def swap_dp(value, step):
    count = lax.axis_size("dp")
    return lax.ppermute(value, "dp", [(i, i ^ step) for i in range(count)])


def places():
    vocab_index = lax.axis_index("vocab")
    return (lax.axis_index("dp"), vocab_index // 2, vocab_index % 2)


def gather_vocab(value):
    _, outer, core = places()
    pair = jnp.stack(xor_order([value, swap_core(value)], core))
    count = lax.axis_size("vocab") // 2
    parts = [pair] + [swap_outer(pair, step) for step in range(1, count)]
    return jnp.concatenate(xor_order(parts, outer), axis=0)


def gather_dp(value):
    dp_index, _, _ = places()
    parts = [value] + [swap_dp(value, step) for step in range(1, lax.axis_size("dp"))]
    return jnp.stack(xor_order(parts, dp_index))


def sum_all(value):
    value = value + swap_core(value)
    value = tree_sum([value] + [swap_dp(value, step) for step in range(1, lax.axis_size("dp"))])
    return tree_sum(outer_parts(value))


def outer_parts(value):
    count = lax.axis_size("vocab") // 2
    return [value] + [swap_outer(value, step) for step in range(1, count)]


def behind(value, *others):
    return lax.optimization_barrier((value, others))[0]


class Slots:
    def __init__(self):
        self.last = None

    def open(self, value):
        return value if self.last is None else behind(value, self.last)

    def close(self, *results):
        self.last = results


class OuterGather:
    def __init__(self, value):
        self.held = value[None]

    def advance(self, slots):
        count = lax.axis_size("vocab") // 2
        step = count // (2 * self.held.shape[0])
        if step:
            shape = (-1,) + self.held.shape[1:]
            held = slots.open(self.held)
            self.held = jnp.stack([held, swap_outer(held, step)], axis=1).reshape(shape)

    def finish(self, slots):
        while self.held.shape[0] < lax.axis_size("vocab") // 2:
            self.advance(slots)
        return self.held


def ring_first(held, slots):
    held = slots.open(held)
    return (held, swap_dp(held, 1), swap_dp(held, 2))


def ring_second(parts, slots):
    held, from_one, from_two = parts
    half = held.shape[0] // 2
    low, high = slots.open((from_two[:half], from_one[half:]))
    return jnp.concatenate([held, from_one, from_two, swap_dp(low, 1), swap_dp(high, 2)], axis=0)


def place_blocks(held, other, cuts):
    dp_index, outer, core = places()
    count = held.shape[0]
    outer_count = lax.axis_size("vocab") // 2
    here = jnp.stack([dp_index, outer, core]).astype(jnp.int32)
    if held.ndim == 3:
        spans, shapes = [], []
        for width in cuts:
            spans.append((sum(w for _, w in spans), width))
            shapes.append((held.shape[1], width))

        def take(ref, block, index):
            return ref.at[block, :, pl.ds(*spans[index])]

    else:
        shapes = [
            held.shape[2:] if isinstance(one, int) else (one[1] - one[0],) + held.shape[2:]
            for one in cuts
        ]

        def take(ref, block, index):
            one = cuts[index]
            if isinstance(one, int):
                return ref.at[block, one]
            return ref.at[block, pl.ds(one[0], one[1] - one[0])]


    def body(here_ref, held_ref, other_ref, *refs):
        out_refs, sems = refs[: len(cuts)], refs[len(cuts)]

        def copies(block):
            dp_place = (block // outer_count) ^ here_ref[0]
            outer_place = (block % outer_count) ^ here_ref[1]
            target = (dp_place * outer_count + outer_place) * 2
            made = []
            for side, ref in enumerate((held_ref, other_ref)):
                place = target + (here_ref[2] ^ side)
                for index in range(len(cuts)):
                    made.append(
                        pltpu.make_async_copy(
                            take(ref, block, index),
                            out_refs[index].at[place],
                            sems.at[index, side, block],
                        )
                    )
            return made

        def start(block, carry):
            for copy in copies(block):
                copy.start()
            return carry

        def wait(block, carry):
            for copy in copies(block):
                copy.wait()
            return carry

        lax.fori_loop(0, count, start, 0)
        lax.fori_loop(0, count, wait, 0)

    any_space = pl.BlockSpec(memory_space=pl.ANY)
    return pl.pallas_call(
        body,
        out_shape=[
            jax.ShapeDtypeStruct((2 * count,) + tuple(shape), held.dtype) for shape in shapes
        ],
        in_specs=[pl.BlockSpec(memory_space=pltpu.SMEM), any_space, any_space],
        out_specs=[pl.BlockSpec(memory_space=pltpu.VMEM) for _ in cuts],
        scratch_shapes=[pltpu.SemaphoreType.DMA((len(cuts), 2, count))],
        compiler_params=params(),
        cost_estimate=pl.CostEstimate(
            flops=0, bytes_accessed=4 * held.size * held.dtype.itemsize, transcendentals=0
        ),
    )(here, held, other)


def tile_of(values):
    row = lax.broadcasted_iota(jnp.int32, (8, 128), 0)
    lane = lax.broadcasted_iota(jnp.int32, (8, 128), 1)
    tile = jnp.zeros((8, 128), jnp.float32)
    for place, value in enumerate(values):
        if value is not None:
            tile = jnp.where((row == 0) & (lane == place), value, tile)
    return tile


def total_of(value):
    return jnp.sum(jnp.sum(value, axis=1, keepdims=True), axis=0, keepdims=True)


def fold_rows(value):
    return jnp.sum(value.reshape(-1, 8, value.shape[1]), axis=0)


def prepare_table(table, smalls, dp_count, first):
    rows, width = table.shape
    chunks = -(-rows // CHUNK)
    per = max(n for n in range(1, 9) if chunks % n == 0 and n * CHUNK <= rows)
    tile = per * CHUNK
    steps = chunks // per

    def body(first_ref, table_ref, *refs):
        small_refs, (low_ref, sum_ref, row_ref, acc_ref) = refs[: len(smalls)], refs[len(smalls) :]
        step = pl.program_id(0)
        row = lax.broadcasted_iota(jnp.int32, (tile, 1), 0) + step * tile
        value = jnp.where(row < rows, table_ref[...], 0.0)
        rounded = value.astype(jnp.bfloat16)
        low_ref[...] = rounded
        part = fold_rows(value * value)
        whole = jnp.where(row + first_ref[0] < V_REAL, rounded.astype(jnp.float32), 0.0)
        whole = jnp.sum(fold_rows(whole), axis=0, keepdims=True)

        @pl.when(step == 0)
        def _():
            acc_ref[...] = part
            row_ref[...] = whole

        @pl.when(step > 0)
        def _():
            acc_ref[...] += part
            row_ref[...] += whole

        @pl.when(step == steps - 1)
        def _():
            terms = [None] + [total_of(ref[...] * ref[...]) for ref in small_refs]
            terms.append(total_of(acc_ref[...]) / dp_count)
            sum_ref[...] = tile_of(terms)

    return pl.pallas_call(
        body,
        grid=(steps,),
        out_shape=[
            jax.ShapeDtypeStruct((chunks * CHUNK, width), jnp.bfloat16),
            jax.ShapeDtypeStruct((8, 128), jnp.float32),
            jax.ShapeDtypeStruct((1, width), jnp.float32),
        ],
        in_specs=[pl.BlockSpec(memory_space=pltpu.SMEM), pl.BlockSpec((tile, width), lambda i: (i, 0))]
        + [whole_block() for _ in smalls],
        out_specs=[pl.BlockSpec((tile, width), lambda i: (i, 0)), whole_block(), whole_block()],
        scratch_shapes=[pltpu.VMEM((8, width), jnp.float32)],
        compiler_params=params(34 * 2**20),
        cost_estimate=pl.CostEstimate(
            flops=4 * table.size, bytes_accessed=6 * table.size, transcendentals=0
        ),
    )(first, table, *smalls)


def logit_grad(values, columns, norms, targets, scale):
    drop = jnp.where(
        columns == targets,
        scale * (1.0 - SMOOTHING + SMOOTHING / V_REAL),
        scale * (SMOOTHING / V_REAL),
    )
    return jnp.exp(values - norms) - drop


def table_part(earlier, head_all, table_low, targets, norms, first, rows, scale, start, stop):
    count, width = head_all.shape
    block = min(512, count)

    def body(first_ref, head_ref, table_ref, target_ref, norm_ref, *refs):
        out_ref, done_ref = refs[-2:]
        done_ref[...] = jnp.zeros_like(done_ref)
        begin = (pl.program_id(0) + start) * PIECE
        real = jnp.minimum(rows, V_REAL - first_ref[0])
        part = table_ref[...]
        local = lax.broadcasted_iota(jnp.int32, (PIECE, 1), 0) + begin
        columns = local + first_ref[0]

        def total_of_blocks(masked):
            total = jnp.zeros((PIECE, width), jnp.float32)
            for place in range(0, count, block):
                span = slice(place, place + block)
                head = head_ref[span, :]
                grad = logit_grad(
                    dot_second(part, head), columns, norm_ref[:, span], target_ref[:, span], scale
                )
                if masked:
                    grad = jnp.where(local < real, grad, 0.0)
                total = total + dot_plain(grad.astype(jnp.bfloat16), head)
            return total

        @pl.when(begin + PIECE <= real)
        def _():
            out_ref[...] = total_of_blocks(False)

        @pl.when(begin + PIECE > real)
        def _():
            out_ref[...] = total_of_blocks(True)

    args = [first, head_all, table_low, targets, norms]
    specs = [
        pl.BlockSpec(memory_space=pltpu.SMEM),
        whole_block(),
        pl.BlockSpec((PIECE, width), lambda i: (i + start, 0)),
        whole_block(),
        whole_block(),
    ]
    aliases = {}
    if earlier is not None:
        aliases = {len(args): 0}
        args.append(earlier)
        specs.append(pl.BlockSpec(memory_space=pl.ANY))
    size = (stop - start) * PIECE
    return pl.pallas_call(
        body,
        grid=(stop - start,),
        out_shape=[
            jax.ShapeDtypeStruct(table_low.shape, jnp.float32),
            jax.ShapeDtypeStruct((8, 128), jnp.float32),
        ],
        in_specs=specs,
        out_specs=[pl.BlockSpec((PIECE, width), lambda i: (i + start, 0)), whole_block()],
        input_output_aliases=aliases,
        compiler_params=params(20 * 2**20 + 4 * head_all.size),
        cost_estimate=pl.CostEstimate(
            flops=4 * size * width * count,
            bytes_accessed=6 * size * width,
            transcendentals=size * count,
        ),
    )(*args)


def token_lists(ids, first, rows, cap, bands):
    local = ids - first
    mine = (local >= 0) & (local < rows)
    tokens = jnp.arange(ids.shape[1], dtype=jnp.int32)
    band = local // CHUNK
    key = jnp.where(mine, band * ids.shape[1] + tokens[None, :], bands * ids.shape[1])
    slot = jnp.sum((key[:, None, :] < key[:, :, None]).astype(jnp.int32), axis=2)
    slots = jnp.arange(cap, dtype=jnp.int32)
    hot = (slot[:, None, :] == slots[None, :, None]) & mine[:, None, :]
    row = jnp.sum(jnp.where(hot, local[:, None, :], 0), axis=2)
    token = jnp.sum(jnp.where(hot, tokens[None, None, :], 0), axis=2)
    upto = jnp.arange(bands, dtype=jnp.int32)
    ends = (band[:, None, :] <= upto[None, :, None]) & mine[:, None, :]
    return (jnp.sum(ends.astype(jnp.int32), axis=2), row, token)


def add_rows(table_grad, held, other, ends, row_list, token_list, gradients, weight_sums, dp_count):
    padded, width = table_grad.shape
    dp_index, outer, core = places()
    here = jnp.stack([dp_index, outer, core]).astype(jnp.int32)
    outer_count = lax.axis_size("vocab") // 2
    sequences, bands = ends.shape
    tokens = held.shape[1]
    cap = row_list.shape[1]
    fine = 256
    per = CHUNK // fine
    kept = sequences if sequences * tokens * width * 4 <= 2**24 else 1

    def body(here_ref, end_ref, row_ref, token_ref, grad_in_ref, held_ref, other_ref, sums_ref, *refs):
        small_refs = refs[: len(gradients)]
        grad_out_ref, total_ref, grad_ref, rows_ref, in_sems, out_sems = refs[len(gradients) :]

        def in_copy(index):
            span = pl.ds(pl.multiple_of(index * CHUNK, CHUNK), CHUNK)
            return pltpu.make_async_copy(grad_in_ref.at[span], grad_ref.at[span], in_sems.at[index])

        def out_copy(index):
            span = pl.ds(pl.multiple_of(index * CHUNK, CHUNK), CHUNK)
            return pltpu.make_async_copy(grad_ref.at[span], grad_out_ref.at[span], out_sems.at[index])

        for index in range(bands):
            in_copy(index).start()
        clip = jnp.zeros((1, 1), jnp.float32)
        for ref in small_refs:
            clip = clip + total_of(ref[...] * ref[...])

        def widen(index, carry):
            dp_place = (index // 2) // outer_count
            outer_place = (index // 2) % outer_count
            block = (dp_place ^ here_ref[0]) * outer_count + (outer_place ^ here_ref[1])
            span = pl.ds(pl.multiple_of(index % kept * tokens, tokens), tokens)

            @pl.when(index % 2 == here_ref[2])
            def _():
                rows_ref[span, :] = held_ref[block].astype(jnp.float32)

            @pl.when(index % 2 != here_ref[2])
            def _():
                rows_ref[span, :] = other_ref[block].astype(jnp.float32)

            return carry

        if kept > 1:
            lax.fori_loop(0, sequences, widen, 0)
        acc = jnp.zeros((8, width), jnp.float32)
        for band in range(bands):
            in_copy(band).wait()

            def sequence(index, carry, band=band):
                if kept == 1:
                    widen(index, 0)

                def one(slot, carry):
                    row = row_ref[index * cap + slot]
                    token = index % kept * tokens + token_ref[index * cap + slot]
                    grad_ref[pl.ds(row, 1), :] += rows_ref[pl.ds(token, 1), :]
                    return carry

                begin = end_ref[index * bands + band - 1] if band else 0
                lax.fori_loop(begin, end_ref[index * bands + band], one, 0)
                return carry

            lax.fori_loop(0, sequences, sequence, 0)
            out_copy(band).start()

            def square(index, acc, band=band):
                span = pl.ds(pl.multiple_of(band * CHUNK + index * fine, fine), fine)
                value = grad_ref[span, :]
                return acc + fold_rows(value * value)

            acc = lax.fori_loop(0, per, square, acc)
        total_ref[...] = sums_ref[...] + tile_of([clip + total_of(acc) / dp_count])
        for band in range(bands):
            out_copy(band).wait()

    smem = pl.BlockSpec(memory_space=pltpu.SMEM)
    any_space = pl.BlockSpec(memory_space=pl.ANY)
    return pl.pallas_call(
        body,
        out_shape=[
            jax.ShapeDtypeStruct(table_grad.shape, jnp.float32),
            jax.ShapeDtypeStruct((8, 128), jnp.float32),
        ],
        in_specs=[smem, smem, smem, smem, any_space, whole_block(), whole_block(), whole_block()]
        + [whole_block() for _ in gradients],
        out_specs=[any_space, whole_block()],
        scratch_shapes=[
            pltpu.VMEM((padded, width), jnp.float32),
            pltpu.VMEM((kept * tokens, width), jnp.float32),
            pltpu.SemaphoreType.DMA((bands,)),
            pltpu.SemaphoreType.DMA((bands,)),
        ],
        input_output_aliases={4: 0},
        compiler_params=params(47 * 2**20),
        cost_estimate=pl.CostEstimate(
            flops=2 * table_grad.size, bytes_accessed=8 * table_grad.size, transcendentals=0
        ),
    )(
        here,
        ends.reshape(-1),
        row_list.reshape(-1),
        token_list.reshape(-1),
        table_grad,
        held,
        other,
        weight_sums,
        *gradients,
    )


def moments_of(gradient, first, second, factor):
    clipped = gradient * factor
    first = BETA_ONE * first + (1.0 - BETA_ONE) * clipped
    second = BETA_TWO * second + (1.0 - BETA_TWO) * clipped * clipped
    return (first, second)


def update_of(weight, first, second):
    scaled = second * (1.0 / (1.0 - BETA_TWO**STEP))
    root = scaled * lax.rsqrt(scaled) + ADAM_EPS
    return first * (1.0 / (1.0 - BETA_ONE**STEP)) / root + DECAY * weight


def clip_factor(sums):
    return jnp.minimum(1.0, CLIP_AT / jnp.sqrt(sums[0:1, 0:1]))


def table_tile(rows, dp_count):
    return -(-rows // (3 * dp_count * 8)) * 8


def update_norms(sums, smalls, table_set, dp_count):
    weight, gradient, first, second = table_set
    rows, width = weight.shape
    tile = -(-rows // (6 * dp_count * 8)) * 8
    last = -(-rows // tile) - 1
    here = lax.axis_index("dp").astype(jnp.int32).reshape(1)
    number = len(smalls)

    def body(here_ref, sums_ref, w_ref, g_ref, m_ref, s_ref, *refs):
        small_refs = refs[: 4 * number]
        out_refs = refs[4 * number : 7 * number]
        norm_ref, acc_ref, term_ref = refs[7 * number :]
        step = pl.program_id(0)
        factor = clip_factor(sums_ref[...])

        @pl.when(step == 0)
        def _():
            acc_ref[...] = jnp.zeros_like(acc_ref)
            terms = [None]
            for place in range(number):
                w, g, m, s = (ref[...] for ref in small_refs[4 * place : 4 * place + 4])
                m, s = moments_of(g, m, s, factor)
                u = update_of(w, m, s)
                out_refs[3 * place][...] = m
                out_refs[3 * place + 1][...] = s
                out_refs[3 * place + 2][...] = u
                terms.append(total_of(u * u))
            term_ref[...] = tile_of(terms)

        row = (here_ref[0] * 6 + step) * tile + lax.broadcasted_iota(jnp.int32, (tile, 1), 0)
        m, s = moments_of(g_ref[...], m_ref[...], s_ref[...], factor)
        u = jnp.where(row < rows, update_of(w_ref[...], m, s), 0.0)
        acc_ref[...] += fold_rows(u * u)

        @pl.when(step == 5)
        def _():
            norm_ref[...] = term_ref[...] + tile_of([None] * (number + 1) + [total_of(acc_ref[...])])

    block = pl.BlockSpec(
        (tile, width), lambda i, here_ref: (jnp.minimum(here_ref[0] * 6 + i, last), 0)
    )
    flat = [value for group in smalls for value in group]
    outs = [jax.ShapeDtypeStruct(group[0].shape, jnp.float32) for group in smalls for _ in range(3)]
    made = pl.pallas_call(
        body,
        grid_spec=pltpu.PrefetchScalarGridSpec(
            num_scalar_prefetch=1,
            grid=(6,),
            in_specs=[whole_block()] + [block] * 4 + [whole_block() for _ in flat],
            out_specs=[whole_block() for _ in outs] + [whole_block()],
            scratch_shapes=[pltpu.VMEM((8, width), jnp.float32), pltpu.VMEM((8, 128), jnp.float32)],
        ),
        out_shape=outs + [jax.ShapeDtypeStruct((8, 128), jnp.float32)],
        compiler_params=params(),
        cost_estimate=pl.CostEstimate(
            flops=20 * tile * 6 * width, bytes_accessed=16 * tile * 6 * width, transcendentals=2 * tile * 6 * width
        ),
    )(here, sums, weight, gradient, first, second, *flat)
    return ([made[3 * place : 3 * place + 3] for place in range(number)], made[-1])


def write_updates(sums, norms, smalls, table_set):
    weight, gradient, first, second = table_set
    rows, width = weight.shape
    tile = 2 * table_tile(rows, lax.axis_size("dp"))
    steps = -(-rows // tile)
    number = len(smalls)

    def body(sums_ref, norms_ref, w_ref, g_ref, m_ref, s_ref, *refs):
        small_refs = refs[: 2 * number]
        out_w, out_m, out_s = refs[2 * number : 2 * number + 3]
        small_outs = refs[2 * number + 3 :]
        sums = sums_ref[...]
        pace = RATE * jnp.sqrt(sums) / jnp.sqrt(norms_ref[...])

        @pl.when(pl.program_id(0) == 0)
        def _():
            for place in range(number):
                w, u = (ref[...] for ref in small_refs[2 * place : 2 * place + 2])
                small_outs[place][...] = w - pace[0:1, place + 1 : place + 2] * u

        m, s = moments_of(g_ref[...], m_ref[...], s_ref[...], clip_factor(sums))
        w = w_ref[...]
        out_m[...] = m
        out_s[...] = s
        out_w[...] = w - pace[0:1, number + 1 : number + 2] * update_of(w, m, s)

    block = pl.BlockSpec((tile, width), lambda i: (i, 0))
    flat = [value for group in smalls for value in group]
    outs = [jax.ShapeDtypeStruct(weight.shape, jnp.float32)] * 3
    outs += [jax.ShapeDtypeStruct(group[0].shape, jnp.float32) for group in smalls]
    return pl.pallas_call(
        body,
        grid=(steps,),
        out_shape=outs,
        in_specs=[whole_block(), whole_block()] + [block] * 4 + [whole_block() for _ in flat],
        out_specs=[block] * 3 + [whole_block() for _ in smalls],
        compiler_params=pltpu.CompilerParams(vmem_limit_bytes=VMEM_BYTES),
        cost_estimate=pl.CostEstimate(
            flops=20 * weight.size, bytes_accessed=28 * weight.size, transcendentals=2 * weight.size
        ),
    )(sums, norms, weight, gradient, first, second, *flat)


def pick_half(value, index, axis):
    return lax.dynamic_index_in_dim(value, index, axis, keepdims=False)


class OuterSum:
    def __init__(self, held):
        self.held = held
        self.step = 1

    def advance(self, slots):
        held = self.held
        if held.shape[0] > 1:
            _, outer, _ = places()
            pairs = held.reshape((-1, 2) + held.shape[1:])
            own = (outer // self.step) % 2
            out = slots.open(pick_half(pairs, 1 - own, 1).astype(jnp.bfloat16))
            self.held = pick_half(pairs, own, 1) + swap_outer(out, self.step).astype(jnp.float32)
            self.step *= 2

    def finish(self, slots):
        while self.held.shape[0] > 1:
            self.advance(slots)
        return self.held.reshape(self.held.shape[1:])


def scatter_first(parts, slots):
    own, one_lower, one_upper, two_lower, two_upper, first, second = parts
    low = jnp.bfloat16
    first, second = slots.open((first, second))
    into_two = swap_dp(first, 1).astype(jnp.float32)
    into_one = swap_dp(second, 2).astype(jnp.float32)
    return (
        own,
        jnp.concatenate([one_lower, (one_upper + into_one).astype(low)], axis=0),
        jnp.concatenate([(two_lower + into_two).astype(low), two_upper], axis=0),
    )


def scatter_second(parts, slots):
    own, one, two = parts
    one, two = slots.open((one, two))
    return own + (swap_dp(one, 1).astype(jnp.float32) + swap_dp(two, 2).astype(jnp.float32))


def shards(
    token_ids,
    pick_rows,
    target_ids,
    attn_in,
    attn_out,
    mlp_in,
    mlp_out,
    positions,
    vectors,
    table,
    *moments,
):
    low = jnp.bfloat16
    dp_index, outer, core = places()
    dp_count = lax.axis_size("dp")
    shard_count = lax.axis_size("vocab")
    device_count = dp_count * shard_count
    outer_count = shard_count // 2
    vocab_rows, width = table.shape
    seq_len = token_ids.shape[1]
    pick_count = pick_rows.shape[1]
    vocab_start = lax.axis_index("vocab") * vocab_rows

    slots = Slots()
    unit_rows = attn_in.shape[0]
    small_count = positions.size + vectors.size
    small_width = -(-small_count // (unit_rows * 128)) * 128
    small = jnp.concatenate([positions.astype(low).reshape(-1), vectors.astype(low).reshape(-1)])
    small = jnp.pad(small, (0, unit_rows * small_width - small_count))
    first = OuterGather(
        jnp.concatenate(
            [attn_in.astype(low), attn_out.astype(low), small.reshape(unit_rows, small_width)], axis=1
        )
    )
    up_parts = mlp_in.shape[1] // width
    both = OuterGather(
        jnp.concatenate(
            [
                jnp.swapaxes(mlp_in.astype(low).reshape(unit_rows, up_parts, width), 0, 1),
                mlp_out.astype(low).reshape(-1, unit_rows, width),
            ],
            axis=0,
        )
    )
    small_masters = (attn_in, attn_out, mlp_in, mlp_out, positions, vectors)

    first.advance(slots)
    packed_ids = jnp.concatenate([token_ids, target_ids], axis=1)
    ids_pair = jnp.stack(xor_order([packed_ids, swap_core(packed_ids)], core))
    slots.close(first.held, ids_pair)

    first.finish(slots)
    ids_parts = outer_parts(slots.open(ids_pair))
    group_packed = jnp.concatenate(xor_order(ids_parts, outer), axis=0).reshape(shard_count, -1)
    group_targets = group_packed[:, seq_len:]
    slots.close(first.held, group_packed)

    first_ring = ring_first(first.held, slots)
    both.advance(slots)
    group_local = slots.open(group_packed) - vocab_start
    mine = (group_local >= 0) & (group_local < vocab_rows)
    served = jnp.take(table, jnp.where(mine, group_local, 0).reshape(-1), axis=0)
    served = jnp.where(mine.reshape(-1)[:, None], served, 0.0).astype(low)
    served = served.reshape(outer_count, 2, -1, width)
    slots.close(first_ring, both.held, served)

    first_held = ring_second(first_ring, slots)
    served = slots.open(served)
    served = pick_half(served, core, 1) + swap_core(pick_half(served, 1 - core, 1))
    slots.close(first_held, served)

    both.finish(slots)
    first_other = swap_core(slots.open(first_held))
    embedded = OuterSum(slots.open(served)[:, :seq_len].astype(jnp.float32))
    embedded.advance(slots)
    first_column = vocab_start.astype(jnp.int32).reshape(1)
    table_low, weight_sums, row_part = prepare_table(
        slots.open(table), small_masters, dp_count, first_column
    )
    slots.close(first_other, both.held, embedded.held, table_low)

    both_ring = ring_first(both.held, slots)
    embedded = embedded.finish(slots)
    w_qkv, w_proj, small_all = place_blocks(
        slots.open(first_held), first_other, (3 * width, width, small_width)
    )
    slots.close(embedded, w_qkv)

    w_qkv = w_qkv.reshape(width, 3 * width)
    w_proj = w_proj.reshape(width, width)
    small_all = slots.open(small_all).reshape(device_count, -1)
    pos_low = small_all[:, : positions.size].reshape(seq_len, width)
    vec_low = small_all[:, positions.size : small_count].reshape((device_count,) + vectors.shape)
    vec_rows = jnp.moveaxis(vec_low, 0, 1).reshape(vectors.shape[0], width).astype(jnp.float32)
    unit_chooser = choosers(width, unit_rows, core, dp_index)
    slots.close(both_ring, embedded, vec_rows, pos_low, unit_chooser)

    both_held = ring_second(both_ring, slots)
    resid_in, packed, resid_mid, normed_two, lefts_own, lefts_sent = attention_forward(
        slots.open(embedded), pos_low, vec_rows, w_qkv, w_proj, unit_chooser
    )
    target_rows = served[:, seq_len:].astype(jnp.float32)
    target_rows = OuterSum(target_rows)
    target_rows.advance(slots)
    slots.close(both_held, normed_two, target_rows.held)

    both_other = swap_core(slots.open(both_held))
    lefts_got = swap_core(slots.open(lefts_sent))
    target_rows = target_rows.finish(slots)
    packed_all = gather_dp(slots.open(group_packed)).reshape(device_count, -1)
    made = place_blocks(
        both_held, both_other, tuple(range(up_parts)) + ((up_parts, both_held.shape[1]),)
    )
    w_up = [value.reshape(width, width) for value in made[:up_parts]]
    w_down = made[up_parts].reshape(-1, width)
    hidden_pre, hidden_act, act_own, act_sent = hidden_forward(
        normed_two,
        vec_rows,
        w_up,
        choosers(width, mlp_out.shape[0], core),
        dp_index.astype(jnp.int32).reshape(1),
    )
    picks = pick_rows.reshape(-1, 1)
    resid_out, picked = output_forward(hidden_act, w_down, resid_mid, vec_rows, picks)
    slots.close(picked, packed_all, lefts_got, target_rows)

    tail_rows = jnp.concatenate(split_three(row_part), axis=0)
    sent = jnp.concatenate([picked, jnp.pad(tail_rows, ((0, 13), (0, 0)))], axis=0)
    same_core = jnp.stack(outer_parts(slots.open(sent)))
    act_got = swap_core(slots.open(act_sent))
    counts, row_list, token_list = token_lists(
        slots.open(packed_all)[:, :seq_len],
        vocab_start,
        vocab_rows,
        4 * seq_len // shard_count,
        table_low.shape[0] // CHUNK,
    )
    slots.close(same_core, act_got, counts, row_list, token_list)

    ordered = jnp.stack(xor_order([same_core[step] for step in range(outer_count)], outer))
    head_in = jnp.stack(xor_order([ordered, swap_core(slots.open(ordered))], core), axis=1)
    row_sum = head_in[:, :, pick_count : pick_count + 3].astype(jnp.float32).reshape(-1, width)
    row_sum = jnp.sum(row_sum, axis=0, keepdims=True)
    head_in = head_in[:, :, :pick_count]
    head_in = head_in.reshape(-1, width)
    slots.close(head_in)
    ring = ring_first(same_core[:, :pick_count], slots)
    here = jnp.stack([vocab_start, core]).astype(jnp.int32)
    head_own, head_stat, head_sent = head_pass(slots.open(head_in), table_low, here, vocab_rows, pick_count)
    slots.close(head_sent, ring)

    head_got = swap_core(slots.open(head_sent))
    joined = join_cores(
        head_own, head_stat, head_got, outer.astype(jnp.int32).reshape(1), pick_count
    )
    slots.close(joined[0])

    received = [
        swap_outer(value, step + 1) for step, value in enumerate(slots.open(tuple(joined[2:])))
    ]
    token_count = device_count * pick_count
    grad_top, grad_branch, vec_down, row_stats = output_backward(
        joined[0],
        joined[1],
        received,
        picked,
        target_rows,
        row_sum,
        picks,
        resid_out,
        vec_rows,
        float(token_count),
    )
    slots.close(grad_branch)

    dy_got = swap_core(slots.open(grad_branch))
    stats_pair = slots.open(row_stats[:, :2].T)
    stats_pair = jnp.stack(xor_order([stats_pair, swap_core(stats_pair)], core))
    ring = ring_second(ring, slots)
    grad_pre, vec_up = hidden_backward(slots.open(grad_branch), w_down, hidden_pre)
    slots.close(dy_got, stats_pair, grad_pre, ring)

    pre_got = swap_core(slots.open(grad_pre))
    stats_parts = outer_parts(slots.open(stats_pair))
    stats_group = jnp.concatenate(xor_order(stats_parts, outer), axis=0)
    down = gradient_blocks(
        [(act_own, act_got)],
        [(0, act_own.shape[1])],
        [(slots.open(grad_branch), dy_got)],
        None,
        mlp_out.shape[0],
    )
    slots.close(pre_got, stats_group, down[5])

    lefts = (lefts_own, lefts_got)
    left_spans = [(place * width // 2, (place + 1) * width // 2) for place in range(3)]
    down = scatter_first(down, slots)
    stats_all = gather_dp(slots.open(stats_group))
    up = gradient_blocks(
        [lefts], left_spans[2:], [(slots.open(grad_pre), pre_got)], None, unit_rows
    )
    grad_mid, grad_attn, grad_mixed, vec_middle = middle_backward(
        behind(grad_pre, up[5]), w_up, grad_top, resid_mid, w_proj, vec_rows
    )
    slots.close(down, up, grad_mid, stats_all)

    down = OuterSum(scatter_second(down, slots))
    attn_got = swap_core(slots.open(grad_attn))
    ring_other = swap_core(slots.open(ring))
    grad_in, grad_rows, grad_packed, vec_first = attention_backward(
        grad_mixed, slots.open(grad_mid), packed, resid_in, w_qkv, vec_rows
    )
    slots.close(down.held, grad_rows, attn_got, ring_other)
    grad_in, vec_first = slots.open((grad_in, vec_first))

    norm_all = (stats_all[:, :, 0].reshape(1, -1) + math.log(token_count)).astype(jnp.float32)
    loss = jnp.sum(stats_all[:, :, 1]) / token_count
    targets_all = packed_all[:, seq_len:].reshape(1, -1)
    vec_grad = jnp.concatenate(
        [
            vec_first[0:2],
            vec_middle[0:2],
            vec_down[0:2],
            vec_first[2:4],
            vec_middle[2:3],
            vec_down[2:3],
            vec_up[0:4],
        ],
        axis=0,
    )
    vec_width = vectors.shape[1]
    vec_blocks = jnp.moveaxis(vec_grad.reshape(-1, device_count, vec_width), 1, 0)
    small_grad = jnp.concatenate(
        [grad_in.reshape(device_count, -1), vec_blocks.reshape(device_count, -1)], axis=1
    )
    small_grad = jnp.pad(small_grad, ((0, 0), (0, unit_rows * small_width - small_count)))
    small_grad = small_grad.reshape(-1, 2, unit_rows, small_width)
    small_sent = pick_half(small_grad, 1 - core, 1).astype(low)

    pieces = table_low.shape[0] // PIECE
    bounds = [0] + [round(pieces * share) for share in (0.3, 0.7, 0.9)] + [pieces]

    def head_part(earlier, part, mark):
        if bounds[part] == bounds[part + 1]:
            return (earlier, mark)
        return table_part(
            earlier,
            head_all,
            table_low,
            targets_all,
            behind(norm_all, mark),
            first_column,
            vocab_rows,
            1.0 / token_count,
            bounds[part],
            bounds[part + 1],
        )

    up = scatter_first(up, slots)
    packed_got = swap_core(slots.open(grad_packed))
    small_got = swap_core(slots.open(small_sent))
    small_sum = pick_half(small_grad, core, 1) + small_got.astype(jnp.float32)
    small_sum = small_sum.reshape(4, outer_count * unit_rows, small_width)
    small_sum = jnp.stack([pick_half(small_sum, dp_index ^ step, 0) for step in range(4)])
    head_all = place_blocks(slots.open(ring), ring_other, (width,))[0].reshape(-1, width)
    rows = OuterGather(slots.open(grad_rows))
    rows.advance(slots)
    slots.close(up[1:], packed_got, small_sum, rows.held, head_all)

    up = OuterSum(scatter_second(up, slots))
    rows_outer = rows.finish(slots)
    down.advance(slots)
    first = gradient_blocks(
        [lefts, lefts],
        left_spans[:2],
        [(grad_packed, slots.open(packed_got)), (grad_attn, attn_got)],
        small_sum,
        unit_rows,
    )
    table_grad, mark = head_part(None, 0, first[5])
    slots.close(up.held, first[5], rows_outer, down.held, mark)

    first = scatter_first(first, slots)
    rows_ring = ring_first(rows_outer, slots)
    up.advance(slots)
    table_grad, mark = head_part(table_grad, 1, slots.last)
    slots.close(first[1:], rows_ring, up.held, mark)

    first = scatter_second(first, slots)
    rows_held = ring_second(rows_ring, slots)
    up_own = up.finish(slots)
    table_grad, mark = head_part(table_grad, 2, slots.last)
    slots.close(first, up_own, rows_held, mark)

    first_terms = [pick_half(first, outer, 0)]
    for step in range(1, outer_count):
        sent = slots.open(pick_half(first, outer ^ step, 0).astype(low))
        first_terms.append(swap_outer(sent, step).astype(jnp.float32))
    first_own = tree_sum(first_terms)
    rows_other = swap_core(slots.open(rows_held))
    down_own = down.finish(slots)
    table_grad, mark = head_part(table_grad, 3, slots.last)
    small_own = first_own[:, 4 * width :].reshape(-1)
    gradients = (
        first_own[:, : 3 * width],
        first_own[:, 3 * width : 4 * width],
        up_own,
        down_own,
        small_own[: positions.size].reshape(positions.shape),
        small_own[positions.size : small_count].reshape(vectors.shape),
    )
    table_grad, sums = add_rows(
        table_grad, rows_held, rows_other, counts, row_list, token_list, gradients, weight_sums, dp_count
    )
    sums = sum_all(sums)
    grad_norm = jnp.sqrt(sums[0, 0])
    firsts, seconds = moments[:7], moments[7:]
    smalls = list(zip(small_masters, gradients, firsts, seconds))
    table_set = (table, table_grad, firsts[6], seconds[6])
    made, norms = update_norms(sums, smalls, table_set, dp_count)
    norms = sum_all(norms)
    ratios = jnp.sqrt(sums[0, 1:8]) / jnp.sqrt(norms[0, 1:8])
    written = write_updates(
        sums, norms, [(weight, group[2]) for weight, group in zip(small_masters, made)], table_set
    )
    new_weights = list(written[3:]) + [written[0]]
    new_firsts = [group[0] for group in made] + [written[1]]
    new_seconds = [group[1] for group in made] + [written[2]]
    return (loss, grad_norm, ratios, *new_weights, *new_firsts, *new_seconds)


def solution(mesh):
    rows = P(("dp", "vocab"), None)
    weights = (rows, rows, rows, rows, rows, P(None, ("dp", "vocab")), P("vocab", None))
    return jax.shard_map(
        shards,
        mesh=mesh,
        in_specs=(rows, rows, rows) + weights * 3,
        out_specs=(P(), P(), P()) + weights * 3,
        check_vma=False,
    )
```
